128 devices in a mesh: gy: 16 (over x, y), gz: 8 (over z, core).
Axes of the slice: x: 4, y: 4, z: 4, core: 2. Of those that a mesh axis runs over, the one named last changes fastest.
Arguments:
- adjoint: float32 [19, 128, 256, 128], P(None, 'gy', 'gz'), may hold values from -6 to 6
- collision: float32 [19, 19], replicated, may hold values from -0.25 to 0.85
- link_cell: int32 [128, 128, 8], P(('gy', 'gz')), may hold values from 0 to 255
- link_dir: int32 [128, 128, 8], P(('gy', 'gz')), may hold values from 1 to 18
- link_panel: int32 [128, 128, 8], P(('gy', 'gz')), may hold values from -1 to 63, as said below
Outputs:
- adjoint_out: float32 [19, 128, 256, 128], P(None, 'gy', 'gz')
- panel_sens: float32 [8192, 128], P(('gy', 'gz'))
The draws below stay inside these ranges and needn't reach their ends.
Inputs may be any that keep to these rules, and one draw needn't show every extreme that they name: `link_panel`: -1 marks an empty slot.
All inputs are finite; a program needn't handle non-finite values.
Results may differ from the reference program's by a relative error of at most 0.0001.
Values sent between devices are 32-bit elements; how exact they have to be, the bound alone decides.
No kernel may reach another device: no remote copies, remote signals or barrier semaphores. Data moves between devices by JAX's collectives and lax.ppermute only.
A program may use at most 64 MiB of HBM per device.

```python
import jax
import jax.numpy as jnp
from jax import lax

Q = 19
X = 128
CY = 8
CZ = 32
STEPS = 2
P_DEV = 64
CAP = 8
NY = 128
NZ = 256
PANELS = 8192
N_GZ = 8
DEVICES = 128


def draw_collision(key, part):
    first, second = jax.random.split(jax.random.fold_in(key, 11))
    diagonal = jax.random.uniform(first, (Q,), jnp.float32, 0.45, 0.85)
    offdiag = jnp.clip(jax.random.normal(second, (Q, Q), jnp.float32) * 0.07, -0.25, 0.25)
    unit = jnp.eye(Q, dtype=jnp.float32)
    return unit * diagonal[:, None] + (1.0 - unit) * offdiag


def draw_link_panel(key, part):
    base = jax.random.fold_in(key, 23)
    first, second, third, fourth = jax.random.split(base, 4)
    level = jax.random.randint(first, (DEVICES, 1, 1), 1, 9)
    deck = jax.random.randint(second, (DEVICES, 1, 1), 0, 4) == 0
    level = jnp.where(deck, 8, level)
    level = jnp.where(jnp.arange(DEVICES)[:, None, None] == 0, 8, level)
    level = jnp.where(jnp.arange(DEVICES)[:, None, None] == 1, 4, level)
    valid = jax.random.randint(third, (DEVICES, DEVICES, CAP), 0, 8) < level
    panel = jax.random.randint(fourth, (DEVICES, DEVICES, CAP), 0, P_DEV)
    return jnp.where(valid, panel, -1).astype(jnp.int32)


def set_ends(drawn, key, least, high):
    shape = drawn.shape
    spot = [jax.random.randint(jax.random.fold_in(key, axis), (), 0, shape[axis]) for axis in range(len(shape))]
    drawn = drawn.at[tuple(spot)].set(least)
    longest = shape.index(max(shape))
    spot[longest] = (spot[longest] + 1) % shape[longest]
    return drawn.at[tuple(spot)].set(high)


def block_levels(key, dims, shards, smallest, largest):
    def one(dim, shards_of):
        draws = jax.random.uniform(jax.random.fold_in(jax.random.fold_in(key, 6), dim), (shards_of,), jnp.float32, smallest / len(shards), largest / len(shards))
        return jnp.repeat(jnp.exp(draws), dims[dim] // shards_of).reshape((-1,) + (1,) * (len(dims) - dim - 1))

    level = one(*shards[0])
    for cut in shards[1:]:
        level = level * one(*cut)
    return level


def gaussian(own_key, shape, deviation, most, cuts=(), kind=jnp.bfloat16):
    drawn = deviation * jax.random.normal(own_key, shape, jnp.float32)
    if cuts:
        drawn = drawn * block_levels(own_key, shape, cuts, -0.22, 0.18)
    return jnp.clip(drawn, -most, most).astype(kind)


def setup_inputs(seed: int = 0) -> dict:
    key_list = jax.random.split(jax.random.key(seed), 6)
    return {
        "adjoint": gaussian(key_list[0], (Q, NY, NZ, X), 1.0, 6.0, ((1, 16), (2, 8)), jnp.float32),
        "collision": draw_collision(jax.random.fold_in(key_list[5], 71), 0),
        "link_cell": set_ends(jax.random.randint(key_list[2], (DEVICES, DEVICES, CAP), 0, CY * CZ), jax.random.fold_in(key_list[2], 1), 0, (CY * CZ) - 1).astype(jnp.int32),
        "link_dir": set_ends(jax.random.randint(key_list[3], (DEVICES, DEVICES, CAP), 1, 19), jax.random.fold_in(key_list[3], 1), 1, 18).astype(jnp.int32),
        "link_panel": draw_link_panel(jax.random.fold_in(key_list[5], 71), 0),
    }


DIRS = [(0, 0, 0), (1, 0, 0), (-1, 0, 0), (0, 1, 0), (0, -1, 0), (0, 0, 1), (0, 0, -1),
        (1, 1, 0), (-1, -1, 0), (1, -1, 0), (-1, 1, 0), (1, 0, 1), (-1, 0, -1), (1, 0, -1),
        (-1, 0, 1), (0, 1, 1), (0, -1, -1), (0, 1, -1), (0, -1, 1)]
LINK_WEIGHTS = [2.0] + [1.0 / 3.0] * 6 + [1.0 / 6.0] * 12


def stream(field):
    padded = jnp.pad(field, ((0, 0), (1, 1), (1, 1), (0, 0)))
    ny = field.shape[1]
    nz = field.shape[2]
    pieces = []
    for q, (cx, cy, cz) in enumerate(DIRS):
        piece = padded[q, 1 + cy:1 + cy + ny, 1 + cz:1 + cz + nz, :]
        pieces.append(jnp.roll(piece, -cx, axis=2))
    return jnp.stack(pieces)


def collide(collision, field):
    flat = field.reshape(field.shape[0], -1)
    mixed = jnp.dot(collision.T, flat, precision=lax.Precision.HIGHEST)
    return mixed.reshape(field.shape)


def reference(adjoint, collision, link_cell, link_dir, link_panel):
    field = adjoint
    for step in range(STEPS):
        field = collide(collision, stream(field))
    source = jnp.arange(DEVICES, dtype=jnp.int32)
    src_y = (source // N_GZ)[:, None, None]
    src_z = (source % N_GZ)[:, None, None]
    ypos = src_y * CY + link_cell // CZ
    zpos = src_z * CZ + link_cell % CZ
    values = field[link_dir, ypos, zpos, :]
    table = jnp.array(LINK_WEIGHTS, dtype=field.dtype)
    weight = table[link_dir]
    valid = (link_panel >= 0).astype(field.dtype)
    rows = values * weight[..., None] * valid[..., None]
    owner = jnp.arange(DEVICES, dtype=jnp.int32)[None, :, None]
    segment = jnp.where(link_panel >= 0, owner * P_DEV + link_panel, PANELS)
    summed = jax.ops.segment_sum(rows.reshape(-1, X), segment.reshape(-1), num_segments=PANELS + 1)
    return field, summed[:PANELS]
```

```python
import functools

import jax
import jax.numpy as jnp
from jax import lax
from jax.experimental import pallas as pl
from jax.experimental.pallas import tpu as pltpu
from jax.sharding import PartitionSpec as P

Q = 19
QP = 20
P_DEV = 64
CAP = 8
CY = 8
CZ = 32
X = 128
ROWS = 48
Z0 = 8

DIRS = [
    (0, 0, 0),
    (1, 0, 0),
    (-1, 0, 0),
    (0, 1, 0),
    (0, -1, 0),
    (0, 0, 1),
    (0, 0, -1),
    (1, 1, 0),
    (-1, -1, 0),
    (1, -1, 0),
    (-1, 1, 0),
    (1, 0, 1),
    (-1, 0, -1),
    (1, 0, -1),
    (-1, 0, 1),
    (0, 1, 1),
    (0, -1, -1),
    (0, 1, -1),
    (0, -1, 1),
]
LINK_WEIGHTS = [2.0] + [1.0 / 3.0] * 6 + [1.0 / 6.0] * 12

Y_UP = [q for q in range(Q) if DIRS[q][1] == 1]
Y_DOWN = [q for q in range(Q) if DIRS[q][1] == -1]
Z_UP = [q for q in range(Q) if DIRS[q][2] == 1]
Z_DOWN = [q for q in range(Q) if DIRS[q][2] == -1]
Z_FLAT = [q for q in range(Q) if DIRS[q][2] == 0]
SEND_LOW = [(q, 0) for q in Z_FLAT] + [(q, 0) for q in Z_UP] + [(q, 1) for q in Z_UP]
SEND_HIGH = [(q, 0) for q in Z_FLAT] + [(q, 0) for q in Z_DOWN] + [(q, 1) for q in Z_DOWN]

RAW = 0
ENDS = 5 * CZ
MIXED = ENDS + 16
Y_ROWS = MIXED + 5 * CZ

f32 = jnp.float32
bf16 = jnp.bfloat16


def along_x(value, q):
    cx = DIRS[q][0]
    if cx == 0:
        return value
    return pltpu.roll(value, (-cx) % X, value.ndim - 1)


def split(value):
    high = value.astype(bf16)
    return high, (value - high.astype(f32)).astype(bf16)


def mix(weights, reads):
    wh, wl = weights
    rh, rl = split(reads)
    dot = functools.partial(jnp.dot, preferred_element_type=f32)
    return dot(wh, rh) + (dot(wl, rh) + dot(wh, rl))


def stacked(tiles):
    count = max(len(t) for t in tiles if t is not None)
    zero = jnp.zeros((8, X), f32)
    full = [t if t is not None else [zero] * count for t in tiles]
    return jnp.concatenate(
        [jnp.concatenate([t[c] for t in full], axis=0) for c in range(count)], axis=1
    )


def line_tiles(line):
    return [line[8 * t : 8 * t + 8, :] for t in range(CZ // 8)]


def read_line(ref, p, y, shift=0):
    cx, cy, cz = DIRS[p]
    return ref[p, y + 1 + cy, pl.ds(Z0 + cz + shift, CZ), :]


def read_row(ref, y):
    return stacked([line_tiles(read_line(ref, p, y)) for p in range(Q)] + [None])


def group(w_ref, channels):
    rows = [w_ref[8 * q : 8 * q + 8, :] for q in channels]
    rows += [jnp.zeros_like(rows[0])] * ((-len(rows)) % 2)
    return split(jnp.concatenate(rows, axis=0))


def load_column(ref, q, y, z):
    flat = ref.reshape(Q, (CY + 2) * ROWS, X)
    return flat[q, pl.ds((1 + y) * ROWS + Z0 + z, CY, stride=ROWS), :]


def store_column(ref, q, y, z, value):
    flat = ref.reshape(Q, (CY + 2) * ROWS, X)
    flat[q, pl.ds((1 + y) * ROWS + Z0 + z, CY, stride=ROWS), :] = value


def pack_z_kernel(field, to_pair, to_next):
    even = lax.rem(lax.axis_index("gz"), 2) == 0
    for i in range(Q):
        q, d = SEND_LOW[i]
        low = field[q, pl.ds(d, CY, stride=CZ), :]
        q, d = SEND_HIGH[i]
        high = field[q, pl.ds(CZ - 1 - d, CY, stride=CZ), :]
        to_pair[8 * i : 8 * i + 8, :] = jnp.where(even, high, low)
        to_next[8 * i : 8 * i + 8, :] = jnp.where(even, low, high)


def prepare_kernel(field, collision, cell, direction, s0, w, pick):
    for q in range(Q):
        for y in range(CY):
            s0[q, 1 + y, Z0 : Z0 + CZ, :] = along_x(field[q, CZ * y : CZ * y + CZ, :], q)
    zero = jnp.zeros((ROWS, X), f32)
    for q in Y_DOWN:
        s0[q, 0, :, :] = zero
    for q in Y_UP:
        s0[q, CY + 1, :, :] = zero
    n = QP * 8
    spread = (
        lax.broadcasted_iota(jnp.int32, (n, Q), 0) // 8 == lax.broadcasted_iota(jnp.int32, (n, Q), 1)
    ).astype(f32)
    turned = lax.dot_general(
        spread, collision[...], (((1,), (1,)), ((), ())),
        precision=lax.Precision.HIGHEST, preferred_element_type=f32,
    )
    wide = lax.dot_general(
        turned, spread, (((1,), (1,)), ((), ())),
        precision=lax.Precision.HIGHEST, preferred_element_type=f32,
    )
    same = (
        lax.broadcasted_iota(jnp.int32, (n, n), 0) % 8
        == lax.broadcasted_iota(jnp.int32, (n, n), 1) % 8
    )
    w[...] = jnp.where(same, wide, 0.0)
    pick[...] = direction[...] * (CY * CZ) + cell[...]


def edge_rows_kernel(s0_in, w, from_pair, from_next, s0, s1, to_low, to_high):
    del s0_in
    iz = lax.axis_index("gz")
    even = lax.rem(iz, 2) == 0
    above = iz < lax.axis_size("gz") - 1
    below = iz > 0
    for i in range(Q):
        pair = from_pair[8 * i : 8 * i + 8, :]
        following = from_next[8 * i : 8 * i + 8, :]
        q, d = SEND_LOW[i]
        value = jnp.where(above, jnp.where(even, pair, following), 0.0)
        store_column(s0, q, 0, CZ + d, along_x(value, q))
        q, d = SEND_HIGH[i]
        value = jnp.where(below, jnp.where(even, following, pair), 0.0)
        store_column(s0, q, 0, -1 - d, along_x(value, q))
    weights = split(w[...])
    for z, channels, valid in ((CZ, Z_UP, above), (-1, Z_DOWN, below)):
        reads = stacked(
            [[load_column(s0, p, DIRS[p][1], z + DIRS[p][2])] for p in range(Q)] + [None]
        )
        out = mix(group(w, channels), reads)
        for i, q in enumerate(channels):
            value = jnp.where(valid, out[8 * i : 8 * i + 8, :], 0.0)
            store_column(s1, q, 0, z, along_x(value, q))
    for y in (0, CY - 1):
        store_line(s1, y, mix(weights, read_row(s0, y)))
    for y, channels, message in ((0, Y_UP, to_low), (CY - 1, Y_DOWN, to_high)):
        message[ENDS : ENDS + 16, :] = jnp.zeros((16, X), f32)
        for i, q in enumerate(channels):
            cz = DIRS[q][2]
            message[RAW + CZ * i : RAW + CZ * i + CZ, :] = s0[q, 1 + y, pl.ds(Z0 + cz, CZ), :]
            message[pl.ds(ENDS + 2 * i, 1), :] = s0[q, 1 + y, pl.ds(Z0 + cz - 1, 1), :]
            message[pl.ds(ENDS + 2 * i + 1, 1), :] = s0[q, 1 + y, pl.ds(Z0 + cz + CZ, 1), :]
            message[MIXED + CZ * i : MIXED + CZ * i + CZ, :] = s1[q, 1 + y, pl.ds(Z0 + cz, CZ), :]


def store_line(s1, y, out):
    for q in range(Q):
        for t in range(CZ // 8):
            s1[q, 1 + y, Z0 + 8 * t : Z0 + 8 * t + 8, :] = along_x(
                out[8 * q : 8 * q + 8, X * t : X * t + X], q
            )


def inner_rows_kernel(s0, w, s1_in, s1, beyond, out, kept, sem):
    del s1_in
    iz = lax.axis_index("gz")
    above = iz < lax.axis_size("gz") - 1
    below = iz > 0
    weights = split(w[...])

    @pl.loop(1, CY - 1)
    def _(y):
        store_line(s1, y, mix(weights, read_row(s0, y)))

    @pl.loop(2, CY - 2)
    def _(y):
        mixed = mix(weights, read_row(s1, y))
        for q in range(Q):
            for t in range(CZ // 8):
                kept[q, y - 2, 8 * t : 8 * t + 8, :] = mixed[8 * q : 8 * q + 8, X * t : X * t + X]

    copy = pltpu.make_async_copy(kept, out.at[:, pl.ds(2, CY - 4), :, :], sem)
    copy.start()
    for side, (y, channels, sources) in enumerate(((CY - 1, Y_UP, Y_DOWN), (0, Y_DOWN, Y_UP))):
        for shift in (0, 1, -1):
            wanted = [q for q in channels if DIRS[q][2] == shift]
            reads = stacked(
                [
                    line_tiles(s0[p, 1 + y, pl.ds(Z0 + DIRS[p][2] + shift, CZ), :])
                    if p in sources
                    else None
                    for p in range(Q)
                ]
                + [None]
            )
            mixed = mix(group(w, wanted), reads)
            cells = lax.broadcasted_iota(jnp.int32, (8, X), 0)
            for i, q in enumerate(wanted):
                at = CZ * (5 * side + channels.index(q))
                for t in range(CZ // 8):
                    value = mixed[8 * i : 8 * i + 8, X * t : X * t + X]
                    if shift == 1 and t == CZ // 8 - 1:
                        value = jnp.where(jnp.logical_or(above, cells < 7), value, 0.0)
                    if shift == -1 and t == 0:
                        value = jnp.where(jnp.logical_or(below, cells > 0), value, 0.0)
                    beyond[at + 8 * t : at + 8 * t + 8, :] = along_x(value, q)
    copy.wait()


def outer_rows_kernel(
    s1_in, w, beyond, from_high, from_low, panel, pick, out_in,
    s1, rows, out, kept, inner, scaled, ends, numbers, in_sem, out_sem,
):
    del s1_in
    iy = lax.axis_index("gy")
    iz = lax.axis_index("gz")
    fetch = pltpu.make_async_copy(out_in.at[:, pl.ds(2, CY - 4), :, :], inner, in_sem)
    fetch.start()
    weights = split(w[...])
    numbers[...] = jnp.zeros((128, X), f32)
    numbers[:, 0:CAP] = panel[...].astype(f32).T
    z_ok = (iz > 0, iz < lax.axis_size("gz") - 1)
    sides = (
        (0, CY - 1, CY, Y_UP, from_high, iy < lax.axis_size("gy") - 1),
        (1, 0, -1, Y_DOWN, from_low, iy > 0),
    )
    for side, y, halo, channels, arrived, valid in sides:
        ends[...] = jnp.zeros((5 * 8, X), f32)
        for i in range(5):
            ends[8 * i : 8 * i + 2, :] = arrived[ENDS + 2 * i : ENDS + 2 * i + 2, :]
        tiles = [None] * (Q + 1)
        for i, p in enumerate(channels):
            tiles[p] = line_tiles(arrived[RAW + CZ * i : RAW + CZ * i + CZ, :]) + [
                ends[8 * i : 8 * i + 8, :]
            ]
        mixed = mix(weights, jnp.where(valid, stacked(tiles), 0.0))
        for q in range(Q):
            for t in range(CZ // 8):
                at = pl.ds(Z0 + 8 * t, 8)
                s1[q, 1 + y, at, :] += along_x(mixed[8 * q : 8 * q + 8, X * t : X * t + X], q)
            cz = DIRS[q][2]
            if cz:
                row = 0 if cz < 0 else 1
                end = along_x(mixed[8 * q : 8 * q + 8, X * (CZ // 8) :], q)[row : row + 1, :]
                at = pl.ds(Z0 - 1 if cz < 0 else Z0 + CZ, 1)
                s1[q, 1 + y, at, :] += jnp.where(z_ok[row], end, 0.0)
        for i, q in enumerate(channels):
            line = beyond[CZ * (5 * side + i) : CZ * (5 * side + i) + CZ, :]
            line = line + arrived[MIXED + CZ * i : MIXED + CZ * i + CZ, :]
            s1[q, 1 + halo, pl.ds(Z0 + DIRS[q][2], CZ), :] = jnp.where(valid, line, 0.0)

    for k, y in enumerate((0, 1, CY - 2, CY - 1)):
        mixed = mix(weights, read_row(s1, y))
        for q in range(Q):
            for t in range(CZ // 8):
                value = mixed[8 * q : 8 * q + 8, X * t : X * t + X]
                kept[q, k, 8 * t : 8 * t + 8, :] = value
                at = q * (CY * CZ) + y * CZ + 8 * t
                scaled[at : at + 8, :] = value * LINK_WEIGHTS[q]
    copies = [
        pltpu.make_async_copy(
            kept.at[:, pl.ds(2 * h, 2), :, :], out.at[:, pl.ds(6 * h, 2), :, :], out_sem.at[h]
        )
        for h in range(2)
    ]
    for copy in copies:
        copy.start()
    fetch.wait()
    for q in range(Q):
        for y in range(2, CY - 2):
            at = q * (CY * CZ) + y * CZ
            scaled[at : at + CZ, :] = inner[q, y - 2, :, :] * LINK_WEIGHTS[q]

    @pl.loop(0, 128, unroll=4)
    def _(d):
        for k in range(CAP):
            rows[pl.ds(d * (CAP + 1) + k, 1), 0, :] = scaled[pl.ds(pick[k, d], 1), :]
        rows[pl.ds(d * (CAP + 1) + CAP, 1), 0, :] = numbers[pl.ds(d, 1), :]

    for copy in copies:
        copy.wait()


def sum_kernel(arrived, out):
    devices = arrived.shape[0] // (CAP + 1)
    numbers = arrived[pl.ds(CAP, devices, stride=CAP + 1), :].T
    panels = lax.broadcasted_iota(jnp.int32, (P_DEV, devices), 0).astype(f32)
    hot, rows = [], []
    for k in range(CAP):
        hot.append((numbers[k : k + 1, :] == panels).astype(f32).astype(bf16))
        rows.append(arrived[pl.ds(k, devices, stride=CAP + 1), :])
    hot = jnp.concatenate(hot, axis=1)
    high, low = split(jnp.concatenate(rows, axis=0))
    dot = functools.partial(jnp.dot, preferred_element_type=f32)
    out[...] = dot(hot, high) + dot(hot, low)


VMEM = pl.BlockSpec(memory_space=pltpu.VMEM)
SMEM = pl.BlockSpec(memory_space=pltpu.SMEM)
ANY = pl.BlockSpec(memory_space=pl.ANY)
LIMIT = 32 * 1024 * 1024


def call(kernel, name, ins, outs, shapes, scratch=(), aliases=None):
    return pl.pallas_call(
        kernel,
        out_shape=[jax.ShapeDtypeStruct(*s) for s in shapes],
        in_specs=ins,
        out_specs=outs,
        scratch_shapes=list(scratch),
        input_output_aliases=aliases or {},
        compiler_params=pltpu.CompilerParams(vmem_limit_bytes=LIMIT),
        name=name,
    )


def on_device(adjoint, collision, link_cell, link_dir, link_panel):
    gz = lax.axis_size("gz")
    gy = lax.axis_size("gy")
    devices = gy * gz
    flat = adjoint.reshape(Q, CY * CZ, X)
    pad = (Q, CY + 2, ROWS, X)
    to_pair, to_next = call(
        pack_z_kernel, "pack_z", [VMEM], [VMEM] * 2, [((Q * 8, X), f32)] * 2
    )(flat)
    pairs = [(i, i ^ 1) for i in range(gz)]
    nexts = [(i, (i - 1) % gz if i % 2 == 0 else (i + 1) % gz) for i in range(gz)]
    from_pair = lax.ppermute(to_pair, "gz", pairs)
    from_next = lax.ppermute(to_next, "gz", nexts)
    s0, w, pick = call(
        prepare_kernel, "prepare", [VMEM] * 4, [VMEM] * 3,
        [(pad, f32), ((QP * 8, QP * 8), f32), ((CAP, devices), jnp.int32)],
    )(flat, collision, link_cell[0].T, link_dir[0].T)
    s0, s1, to_low, to_high = call(
        edge_rows_kernel, "edge_rows", [VMEM] * 4, [VMEM] * 4,
        [(pad, f32), (pad, f32), ((Y_ROWS, X), f32), ((Y_ROWS, X), f32)],
        aliases={0: 0},
    )(s0, w, from_pair, from_next)
    from_high = lax.ppermute(to_low, "gy", [(i, (i - 1) % gy) for i in range(gy)])
    from_low = lax.ppermute(to_high, "gy", [(i, (i + 1) % gy) for i in range(gy)])
    s1, beyond, out = call(
        inner_rows_kernel, "inner_rows", [VMEM] * 3, [VMEM, VMEM, ANY],
        [(pad, f32), ((10 * CZ, X), f32), ((Q, CY, CZ, X), f32)],
        scratch=[pltpu.VMEM((Q, CY - 4, CZ, X), f32), pltpu.SemaphoreType.DMA],
        aliases={2: 0},
    )(s0, w, s1)
    _, rows, out = call(
        outer_rows_kernel, "outer_rows", [VMEM] * 6 + [SMEM, ANY], [VMEM, VMEM, ANY],
        [(pad, f32), ((devices * (CAP + 1), 1, X), f32), ((Q, CY, CZ, X), f32)],
        scratch=[
            pltpu.VMEM((Q, 4, CZ, X), f32),
            pltpu.VMEM((Q, 4, CZ, X), f32),
            pltpu.VMEM((Q * CY * CZ, X), f32),
            pltpu.VMEM((5 * 8, X), f32),
            pltpu.VMEM((devices, X), f32),
            pltpu.SemaphoreType.DMA,
            pltpu.SemaphoreType.DMA((2,)),
        ],
        aliases={0: 0, 7: 2},
    )(s1, w, beyond, from_high, from_low, link_panel[0].T, pick, out)
    arrived = lax.all_to_all(
        rows.reshape(devices, CAP + 1, 1, X), ("gy", "gz"), split_axis=0, concat_axis=0, tiled=True
    )
    (panel_sens,) = call(sum_kernel, "sum_rows", [VMEM], [VMEM], [((P_DEV, X), f32)])(
        arrived.reshape(devices * (CAP + 1), X)
    )
    return out, panel_sens


def solution(mesh):
    placed = (
        P(None, "gy", "gz", None),
        P(),
        P(("gy", "gz"), None, None),
        P(("gy", "gz"), None, None),
        P(("gy", "gz"), None, None),
    )
    return jax.shard_map(
        on_device,
        mesh=mesh,
        in_specs=placed,
        out_specs=(P(None, "gy", "gz", None), P(("gy", "gz"), None)),
        check_vma=False,
    )
```

```python
import functools

import jax
import jax.numpy as jnp
from jax import lax
from jax.experimental import pallas as pl
from jax.experimental.pallas import tpu as pltpu
from jax.sharding import PartitionSpec as P

Q = 19
QP = 20
P_DEV = 64
CAP = 8
CY = 8
CZ = 32
X = 128
ROWS = 48
Z0 = 8

DIRS = [
    (0, 0, 0),
    (1, 0, 0),
    (-1, 0, 0),
    (0, 1, 0),
    (0, -1, 0),
    (0, 0, 1),
    (0, 0, -1),
    (1, 1, 0),
    (-1, -1, 0),
    (1, -1, 0),
    (-1, 1, 0),
    (1, 0, 1),
    (-1, 0, -1),
    (1, 0, -1),
    (-1, 0, 1),
    (0, 1, 1),
    (0, -1, -1),
    (0, 1, -1),
    (0, -1, 1),
]
LINK_WEIGHTS = [2.0] + [1.0 / 3.0] * 6 + [1.0 / 6.0] * 12

Y_UP = [q for q in range(Q) if DIRS[q][1] == 1]
Y_DOWN = [q for q in range(Q) if DIRS[q][1] == -1]
Z_UP = [q for q in range(Q) if DIRS[q][2] == 1]
Z_DOWN = [q for q in range(Q) if DIRS[q][2] == -1]
Z_FLAT = [q for q in range(Q) if DIRS[q][2] == 0]
SEND_LOW = [(q, 0) for q in Z_FLAT] + [(q, 0) for q in Z_UP] + [(q, 1) for q in Z_UP]
SEND_HIGH = [(q, 0) for q in Z_FLAT] + [(q, 0) for q in Z_DOWN] + [(q, 1) for q in Z_DOWN]

RAW = 0
ENDS = 5 * CZ
MIXED = ENDS + 16
Y_ROWS = MIXED + 5 * CZ

f32 = jnp.float32
bf16 = jnp.bfloat16


def along_x(value, q):
    cx = DIRS[q][0]
    if cx == 0:
        return value
    return pltpu.roll(value, (-cx) % X, value.ndim - 1)


def split(value):
    high = value.astype(bf16)
    return high, (value - high.astype(f32)).astype(bf16)


def mix(weights, reads):
    wh, wl = weights
    rh, rl = split(reads)
    dot = functools.partial(jnp.dot, preferred_element_type=f32)
    return dot(wh, rh) + (dot(wl, rh) + dot(wh, rl))


def stacked(tiles):
    count = max(len(t) for t in tiles if t is not None)
    zero = jnp.zeros((8, X), f32)
    full = [t if t is not None else [zero] * count for t in tiles]
    return jnp.concatenate(
        [jnp.concatenate([t[c] for t in full], axis=0) for c in range(count)], axis=1
    )


def line_tiles(line):
    return [line[8 * t : 8 * t + 8, :] for t in range(CZ // 8)]


def read_line(ref, p, y, shift=0):
    cx, cy, cz = DIRS[p]
    return ref[p, y + 1 + cy, pl.ds(Z0 + cz + shift, CZ), :]


def read_row(ref, y):
    return stacked([line_tiles(read_line(ref, p, y)) for p in range(Q)] + [None])


def group(w_ref, channels):
    rows = [w_ref[8 * q : 8 * q + 8, :] for q in channels]
    rows += [jnp.zeros_like(rows[0])] * ((-len(rows)) % 2)
    return split(jnp.concatenate(rows, axis=0))


def load_column(ref, q, y, z):
    flat = ref.reshape(Q, (CY + 2) * ROWS, X)
    return flat[q, pl.ds((1 + y) * ROWS + Z0 + z, CY, stride=ROWS), :]


def store_column(ref, q, y, z, value):
    flat = ref.reshape(Q, (CY + 2) * ROWS, X)
    flat[q, pl.ds((1 + y) * ROWS + Z0 + z, CY, stride=ROWS), :] = value


def pack_z_kernel(field, to_pair, to_next):
    even = lax.rem(lax.axis_index("gz"), 2) == 0
    for i in range(Q):
        q, d = SEND_LOW[i]
        low = field[q, pl.ds(d, CY, stride=CZ), :]
        q, d = SEND_HIGH[i]
        high = field[q, pl.ds(CZ - 1 - d, CY, stride=CZ), :]
        to_pair[8 * i : 8 * i + 8, :] = jnp.where(even, high, low)
        to_next[8 * i : 8 * i + 8, :] = jnp.where(even, low, high)


def prepare_kernel(field, s0):
    for q in range(Q):
        for y in range(CY):
            s0[q, 1 + y, Z0 : Z0 + CZ, :] = along_x(field[q, CZ * y : CZ * y + CZ, :], q)
    zero = jnp.zeros((ROWS, X), f32)
    for q in Y_DOWN:
        s0[q, 0, :, :] = zero
    for q in Y_UP:
        s0[q, CY + 1, :, :] = zero


def spread_weights(collision):
    n = QP * 8
    spread = (
        lax.broadcasted_iota(jnp.int32, (n, Q), 0) // 8 == lax.broadcasted_iota(jnp.int32, (n, Q), 1)
    ).astype(f32).astype(bf16)
    same = (
        lax.broadcasted_iota(jnp.int32, (n, n), 0) % 8
        == lax.broadcasted_iota(jnp.int32, (n, n), 1) % 8
    )
    dims = (((1,), (1,)), ((), ()))
    total = 0.0
    for part in split(collision):
        turned = lax.dot_general(spread, part, dims, preferred_element_type=f32).astype(bf16)
        total += lax.dot_general(turned, spread, dims, preferred_element_type=f32)
    return jnp.where(same, total, 0.0)


def edge_rows_kernel(
    s0_in, collision, from_pair, from_next, s0, s1, to_low, to_high, w
):
    del s0_in
    w[...] = spread_weights(collision[...])
    iz = lax.axis_index("gz")
    even = lax.rem(iz, 2) == 0
    above = iz < lax.axis_size("gz") - 1
    below = iz > 0
    for i in range(Q):
        pair = from_pair[8 * i : 8 * i + 8, :]
        following = from_next[8 * i : 8 * i + 8, :]
        q, d = SEND_LOW[i]
        value = jnp.where(above, jnp.where(even, pair, following), 0.0)
        store_column(s0, q, 0, CZ + d, along_x(value, q))
        q, d = SEND_HIGH[i]
        value = jnp.where(below, jnp.where(even, following, pair), 0.0)
        store_column(s0, q, 0, -1 - d, along_x(value, q))
    weights = split(w[...])
    for z, channels, valid in ((CZ, Z_UP, above), (-1, Z_DOWN, below)):
        reads = stacked(
            [[load_column(s0, p, DIRS[p][1], z + DIRS[p][2])] for p in range(Q)] + [None]
        )
        out = mix(group(w, channels), reads)
        for i, q in enumerate(channels):
            value = jnp.where(valid, out[8 * i : 8 * i + 8, :], 0.0)
            store_column(s1, q, 0, z, along_x(value, q))
    for y in (0, CY - 1):
        store_line(s1, y, mix(weights, read_row(s0, y)))
    for y, channels, message in ((0, Y_UP, to_low), (CY - 1, Y_DOWN, to_high)):
        message[ENDS : ENDS + 16, :] = jnp.zeros((16, X), f32)
        for i, q in enumerate(channels):
            cz = DIRS[q][2]
            message[RAW + CZ * i : RAW + CZ * i + CZ, :] = s0[q, 1 + y, pl.ds(Z0 + cz, CZ), :]
            message[pl.ds(ENDS + 2 * i, 1), :] = s0[q, 1 + y, pl.ds(Z0 + cz - 1, 1), :]
            message[pl.ds(ENDS + 2 * i + 1, 1), :] = s0[q, 1 + y, pl.ds(Z0 + cz + CZ, 1), :]
            message[MIXED + CZ * i : MIXED + CZ * i + CZ, :] = s1[q, 1 + y, pl.ds(Z0 + cz, CZ), :]


def store_line(s1, y, out):
    for q in range(Q):
        for t in range(CZ // 8):
            s1[q, 1 + y, Z0 + 8 * t : Z0 + 8 * t + 8, :] = along_x(
                out[8 * q : 8 * q + 8, X * t : X * t + X], q
            )


def inner_rows_kernel(
    s0, w, s1_in, panel, cell, direction, s1, beyond, out, scaled, numbers, pick, kept, sem
):
    del s1_in
    iz = lax.axis_index("gz")
    above = iz < lax.axis_size("gz") - 1
    below = iz > 0
    weights = split(w[...])
    for y in range(1, CY - 1):
        store_line(s1, y, mix(weights, read_row(s0, y)))
    for y in range(2, CY - 2):
        mixed = mix(weights, read_row(s1, y))
        for q in range(Q):
            for t in range(CZ // 8):
                value = mixed[8 * q : 8 * q + 8, X * t : X * t + X]
                kept[q, y - 2, 8 * t : 8 * t + 8, :] = value
                at = q * (CY * CZ) + y * CZ + 8 * t
                scaled[at : at + 8, :] = value * LINK_WEIGHTS[q]
    copy = pltpu.make_async_copy(kept, out.at[:, pl.ds(2, CY - 4), :, :], sem)
    copy.start()
    numbers[...] = jnp.zeros((numbers.shape[0], X), f32)
    numbers[:, 0:CAP] = panel[...].astype(f32).T
    pick[...] = direction[...] * (CY * CZ) + cell[...]
    for side, (y, channels, sources) in enumerate(((CY - 1, Y_UP, Y_DOWN), (0, Y_DOWN, Y_UP))):
        for shift in (0, 1, -1):
            wanted = [q for q in channels if DIRS[q][2] == shift]
            reads = stacked(
                [
                    line_tiles(s0[p, 1 + y, pl.ds(Z0 + DIRS[p][2] + shift, CZ), :])
                    if p in sources
                    else None
                    for p in range(Q)
                ]
                + [None]
            )
            mixed = mix(group(w, wanted), reads)
            cells = lax.broadcasted_iota(jnp.int32, (8, X), 0)
            for i, q in enumerate(wanted):
                at = CZ * (5 * side + channels.index(q))
                for t in range(CZ // 8):
                    value = mixed[8 * i : 8 * i + 8, X * t : X * t + X]
                    if shift == 1 and t == CZ // 8 - 1:
                        value = jnp.where(jnp.logical_or(above, cells < 7), value, 0.0)
                    if shift == -1 and t == 0:
                        value = jnp.where(jnp.logical_or(below, cells > 0), value, 0.0)
                    beyond[at + 8 * t : at + 8 * t + 8, :] = along_x(value, q)
    copy.wait()


def outer_rows_kernel(
    s1_in, w, beyond, from_high, from_low, pick_in, numbers, scaled_in, out_in,
    s1, scaled, rows, out, kept, ends, pick, pick_sem, out_sem,
):
    del s1_in, scaled_in, out_in
    fetch = pltpu.make_async_copy(pick_in, pick, pick_sem)
    fetch.start()
    iy = lax.axis_index("gy")
    iz = lax.axis_index("gz")
    weights = split(w[...])
    z_ok = (iz > 0, iz < lax.axis_size("gz") - 1)
    sides = (
        (0, CY - 1, CY, Y_UP, from_high, iy < lax.axis_size("gy") - 1),
        (1, 0, -1, Y_DOWN, from_low, iy > 0),
    )
    for side, y, halo, channels, arrived, valid in sides:
        ends[side, :, :] = jnp.zeros((5 * 8, X), f32)
        for i in range(5):
            ends[side, 8 * i : 8 * i + 2, :] = arrived[ENDS + 2 * i : ENDS + 2 * i + 2, :]
        tiles = [None] * (Q + 1)
        for i, p in enumerate(channels):
            tiles[p] = line_tiles(arrived[RAW + CZ * i : RAW + CZ * i + CZ, :]) + [
                ends[side, 8 * i : 8 * i + 8, :]
            ]
        mixed = mix(weights, jnp.where(valid, stacked(tiles), 0.0))
        for q in range(Q):
            for t in range(CZ // 8):
                at = pl.ds(Z0 + 8 * t, 8)
                s1[q, 1 + y, at, :] += along_x(mixed[8 * q : 8 * q + 8, X * t : X * t + X], q)
            cz = DIRS[q][2]
            if cz:
                row = 0 if cz < 0 else 1
                end = along_x(mixed[8 * q : 8 * q + 8, X * (CZ // 8) :], q)[row : row + 1, :]
                at = pl.ds(Z0 - 1 if cz < 0 else Z0 + CZ, 1)
                s1[q, 1 + y, at, :] += jnp.where(z_ok[row], end, 0.0)
        for i, q in enumerate(channels):
            line = beyond[CZ * (5 * side + i) : CZ * (5 * side + i) + CZ, :]
            line = line + arrived[MIXED + CZ * i : MIXED + CZ * i + CZ, :]
            s1[q, 1 + halo, pl.ds(Z0 + DIRS[q][2], CZ), :] = jnp.where(valid, line, 0.0)

    copies = [
        pltpu.make_async_copy(
            kept.at[:, pl.ds(2 * h, 2), :, :], out.at[:, pl.ds(6 * h, 2), :, :], out_sem.at[h]
        )
        for h in range(2)
    ]
    for k, y in enumerate((0, 1, CY - 2, CY - 1)):
        mixed = mix(weights, read_row(s1, y))
        for q in range(Q):
            for t in range(CZ // 8):
                value = mixed[8 * q : 8 * q + 8, X * t : X * t + X]
                kept[q, k, 8 * t : 8 * t + 8, :] = value
                at = q * (CY * CZ) + y * CZ + 8 * t
                scaled[at : at + 8, :] = value * LINK_WEIGHTS[q]
        if k % 2:
            copies[k // 2].start()
    fetch.wait()

    @pl.loop(0, numbers.shape[0], unroll=4)
    def _(d):
        for k in range(CAP):
            rows[pl.ds(d * (CAP + 1) + k, 1), 0, :] = scaled[pl.ds(pick[k, d], 1), :]
        rows[pl.ds(d * (CAP + 1) + CAP, 1), 0, :] = numbers[pl.ds(d, 1), :]

    for copy in copies:
        copy.wait()


def sum_kernel(arrived, out):
    devices = arrived.shape[0] // (CAP + 1)
    numbers = arrived[pl.ds(CAP, devices, stride=CAP + 1), :].T
    panels = lax.broadcasted_iota(jnp.int32, (P_DEV, devices), 0).astype(f32)
    hot, rows = [], []
    for k in range(CAP):
        hot.append((numbers[k : k + 1, :] == panels).astype(f32).astype(bf16))
        rows.append(arrived[pl.ds(k, devices, stride=CAP + 1), :])
    hot = jnp.concatenate(hot, axis=1)
    high, low = split(jnp.concatenate(rows, axis=0))
    dot = functools.partial(jnp.dot, preferred_element_type=f32)
    out[...] = dot(hot, high) + dot(hot, low)


VMEM = pl.BlockSpec(memory_space=pltpu.VMEM)
HBM = pl.BlockSpec(memory_space=pltpu.HBM)
MIB = 1024 * 1024


def call(kernel, name, ins, outs, shapes, scratch=(), aliases=None):
    return pl.pallas_call(
        kernel,
        out_shape=[jax.ShapeDtypeStruct(*s) for s in shapes],
        in_specs=ins,
        out_specs=outs,
        scratch_shapes=list(scratch),
        input_output_aliases=aliases or {},
        compiler_params=pltpu.CompilerParams(vmem_limit_bytes=32 * MIB),
        name=name,
    )


def on_device(adjoint, collision, link_cell, link_dir, link_panel):
    gz = lax.axis_size("gz")
    gy = lax.axis_size("gy")
    devices = link_cell.shape[1]
    pad = (Q, CY + 2, ROWS, X)
    own = (Q, CY, CZ, X)
    flat = adjoint.reshape(Q, CY * CZ, X)
    dma = pltpu.SemaphoreType.DMA
    to_pair, to_next = call(
        pack_z_kernel, "pack_z", [VMEM], [VMEM] * 2, [((Q * 8, X), f32)] * 2
    )(flat)
    pairs = [(i, i ^ 1) for i in range(gz)]
    nexts = [(i, (i - 1) % gz if i % 2 == 0 else (i + 1) % gz) for i in range(gz)]
    from_pair = lax.ppermute(to_pair, "gz", pairs)
    from_next = lax.ppermute(to_next, "gz", nexts)
    (s0,) = call(prepare_kernel, "prepare", [VMEM], [VMEM], [(pad, f32)])(flat)
    s0, s1, to_low, to_high, w = call(
        edge_rows_kernel, "edge_rows", [VMEM] * 4, [VMEM] * 5,
        [(pad, f32), (pad, f32), ((Y_ROWS, X), f32), ((Y_ROWS, X), f32), ((QP * 8, QP * 8), f32)],
        aliases={0: 0},
    )(s0, collision, from_pair, from_next)
    from_high = lax.ppermute(to_low, "gy", [(i, (i - 1) % gy) for i in range(gy)])
    from_low = lax.ppermute(to_high, "gy", [(i, (i + 1) % gy) for i in range(gy)])
    s1, beyond, out, scaled, numbers, pick = call(
        inner_rows_kernel, "inner_rows", [VMEM] * 6, [VMEM, VMEM, HBM, VMEM, VMEM, VMEM],
        [
            (pad, f32),
            ((10 * CZ, X), f32),
            (own, f32),
            ((Q * CY * CZ, X), f32),
            ((devices, X), f32),
            ((CAP, devices), jnp.int32),
        ],
        scratch=[pltpu.VMEM((Q, CY - 4, CZ, X), f32), dma],
        aliases={2: 0},
    )(s0, w, s1, link_panel[0].T, link_cell[0].T, link_dir[0].T)
    _, _, rows, out = call(
        outer_rows_kernel, "outer_rows", [VMEM] * 8 + [HBM], [VMEM] * 3 + [HBM],
        [
            (pad, f32),
            ((Q * CY * CZ, X), f32),
            ((devices * (CAP + 1), 1, X), f32),
            (own, f32),
        ],
        scratch=[
            pltpu.VMEM((Q, 4, CZ, X), f32),
            pltpu.VMEM((2, 5 * 8, X), f32),
            pltpu.SMEM((CAP, devices), jnp.int32),
            dma,
            dma((2,)),
        ],
        aliases={0: 0, 7: 1, 8: 3},
    )(s1, w, beyond, from_high, from_low, pick, numbers, scaled, out)
    arrived = lax.all_to_all(
        rows.reshape(devices, CAP + 1, 1, X), ("gy", "gz"), split_axis=0, concat_axis=0, tiled=True
    )
    (panel_sens,) = call(sum_kernel, "sum_rows", [VMEM], [VMEM], [((P_DEV, X), f32)])(
        arrived.reshape(devices * (CAP + 1), X)
    )
    return out, panel_sens


def solution(mesh):
    placed = (
        P(None, "gy", "gz", None),
        P(),
        P(("gy", "gz"), None, None),
        P(("gy", "gz"), None, None),
        P(("gy", "gz"), None, None),
    )
    return jax.shard_map(
        on_device,
        mesh=mesh,
        in_specs=placed,
        out_specs=(P(None, "gy", "gz", None), P(("gy", "gz"), None)),
        check_vma=False,
    )
```

```python
import functools

import jax
import jax.numpy as jnp
from jax import lax
from jax.experimental import pallas as pl
from jax.experimental.pallas import tpu as pltpu
from jax.sharding import PartitionSpec as P

Q = 19
QP = 20
P_DEV = 64
CAP = 8
CY = 8
CZ = 32
X = 128
ROWS = 48
Z0 = 8

DIRS = [
    (0, 0, 0),
    (1, 0, 0),
    (-1, 0, 0),
    (0, 1, 0),
    (0, -1, 0),
    (0, 0, 1),
    (0, 0, -1),
    (1, 1, 0),
    (-1, -1, 0),
    (1, -1, 0),
    (-1, 1, 0),
    (1, 0, 1),
    (-1, 0, -1),
    (1, 0, -1),
    (-1, 0, 1),
    (0, 1, 1),
    (0, -1, -1),
    (0, 1, -1),
    (0, -1, 1),
]
LINK_WEIGHTS = [2.0] + [1.0 / 3.0] * 6 + [1.0 / 6.0] * 12

Y_UP = [q for q in range(Q) if DIRS[q][1] == 1]
Y_DOWN = [q for q in range(Q) if DIRS[q][1] == -1]
Z_UP = [q for q in range(Q) if DIRS[q][2] == 1]
Z_DOWN = [q for q in range(Q) if DIRS[q][2] == -1]
Z_FLAT = [q for q in range(Q) if DIRS[q][2] == 0]
SEND_LOW = [(q, 0) for q in Z_FLAT] + [(q, 0) for q in Z_UP] + [(q, 1) for q in Z_UP]
SEND_HIGH = [(q, 0) for q in Z_FLAT] + [(q, 0) for q in Z_DOWN] + [(q, 1) for q in Z_DOWN]

RAW = 0
MIXED = 5 * CZ
Y_ROWS = 10 * CZ
RAW_ENDS = 0
MIXED_ENDS = 10
CORNERS = 20
END_ROWS = 24
Z_ROWS = Y_ROWS
K1 = QP * 8
K2 = 6 * 8

f32 = jnp.float32
bf16 = jnp.bfloat16


def along_x(value, q):
    cx = DIRS[q][0]
    if cx == 0:
        return value
    return pltpu.roll(value, (-cx) % X, value.ndim - 1)


def split(value):
    high = value.astype(bf16)
    return high, (value - high.astype(f32)).astype(bf16)


def mix(weights, reads):
    high, low = split(reads)
    return jnp.dot(
        weights, jnp.concatenate([high, low, high], axis=0), preferred_element_type=f32
    )


def stacked(tiles):
    count = max(len(t) for t in tiles if t is not None)
    zero = jnp.zeros((8, X), f32)
    full = [t if t is not None else [zero] * count for t in tiles]
    return jnp.concatenate(
        [jnp.concatenate([t[c] for t in full], axis=0) for c in range(count)], axis=1
    )


def line_tiles(line):
    return [line[8 * t : 8 * t + 8, :] for t in range(CZ // 8)]


def read_line(ref, p, y, shift=0):
    cx, cy, cz = DIRS[p]
    return ref[p, y + 1 + cy, pl.ds(Z0 + cz + shift, CZ), :]


def read_row(ref, y):
    return stacked([line_tiles(read_line(ref, p, y)) for p in range(Q)] + [None])


def load_column(ref, q, y, z):
    flat = ref.reshape(Q, (CY + 2) * ROWS, X)
    return flat[q, pl.ds((1 + y) * ROWS + Z0 + z, CY, stride=ROWS), :]


def store_column(ref, q, y, z, value):
    flat = ref.reshape(Q, (CY + 2) * ROWS, X)
    flat[q, pl.ds((1 + y) * ROWS + Z0 + z, CY, stride=ROWS), :] = value


def pack_z_kernel(field, to_pair, to_next, empty):
    empty[...] = jnp.zeros((8, X), f32)
    to_pair[8 * Q :, :] = jnp.zeros((Z_ROWS - 8 * Q, X), f32)
    to_next[8 * Q :, :] = jnp.zeros((Z_ROWS - 8 * Q, X), f32)
    even = lax.rem(lax.axis_index("gz"), 2) == 0
    for i in range(Q):
        q, d = SEND_LOW[i]
        low = field[q, pl.ds(d, CY, stride=CZ), :]
        q, d = SEND_HIGH[i]
        high = field[q, pl.ds(CZ - 1 - d, CY, stride=CZ), :]
        to_pair[8 * i : 8 * i + 8, :] = jnp.where(even, high, low)
        to_next[8 * i : 8 * i + 8, :] = jnp.where(even, low, high)


def own_channel(shape, axis, channels):
    place = lax.broadcasted_iota(jnp.int32, shape, axis) // 8
    channel = lax.broadcasted_iota(jnp.int32, shape, 1 - axis)
    hit = jnp.zeros(shape, f32)
    for i, q in enumerate(channels):
        hit = jnp.where(jnp.logical_and(place == i, channel == q), 1.0, hit)
    return hit.astype(bf16)


def spread_weights(collision, channels, width):
    rows = (
        lax.broadcasted_iota(jnp.int32, (K1, Q), 0) // 8
        == lax.broadcasted_iota(jnp.int32, (K1, Q), 1)
    ).astype(f32).astype(bf16)
    columns = own_channel((width, Q), 0, channels)
    same = (
        lax.broadcasted_iota(jnp.int32, (K1, width), 0) % 8
        == lax.broadcasted_iota(jnp.int32, (K1, width), 1) % 8
    )
    dims = (((1,), (1,)), ((), ()))
    parts = []
    for part in split(collision):
        turned = lax.dot_general(rows, part, dims, preferred_element_type=f32).astype(bf16)
        wide = lax.dot_general(turned, columns, dims, preferred_element_type=f32)
        parts.append(jnp.where(same, wide, 0.0))
    return jnp.concatenate([parts[0], parts[0], parts[1]], axis=1)


def bulk_rows_kernel(field, collision, empty, s0, s1, to_pair, to_next, w):
    nothing = empty[...]
    for q in range(Q):
        for y in range(CY):
            s0[q, 1 + y, Z0 : Z0 + CZ, :] = along_x(field[q, CZ * y : CZ * y + CZ, :], q)
    for q in Y_DOWN + Y_UP:
        for t in range(ROWS // 8):
            s0[q, 0 if DIRS[q][1] < 0 else CY + 1, 8 * t : 8 * t + 8, :] = nothing
    for q in range(Q):
        if DIRS[q][2]:
            for y in range(CY):
                s0[q, 1 + y, 0:Z0, :] = nothing
                s0[q, 1 + y, Z0 + CZ : ROWS, :] = nothing
    weights = spread_weights(collision[...], range(Q), K1)
    w[...] = weights
    weights = weights.astype(bf16)
    for y in (0, CY - 1):
        store_line(s1, y, mix(weights, read_row(s0, y)))
    even = lax.rem(lax.axis_index("gy"), 2) == 0
    for ref, base in ((s0, RAW), (s1, MIXED)):
        for i in range(5):
            low = ref[Y_UP[i], 1, Z0 : Z0 + CZ, :]
            high = ref[Y_DOWN[i], CY, Z0 : Z0 + CZ, :]
            at = base + CZ * i
            to_pair[at : at + CZ, :] = jnp.where(even, high, low)
            to_next[at : at + CZ, :] = jnp.where(even, low, high)


def end_cells_kernel(
    s0_in, s1_in, w, from_pair, from_next, s0, s1, to_pair, to_next, both
):
    del s0_in, s1_in
    iz = lax.axis_index("gz")
    even = lax.rem(iz, 2) == 0
    above = iz < lax.axis_size("gz") - 1
    below = iz > 0
    for i in range(Q):
        pair = from_pair[8 * i : 8 * i + 8, :]
        following = from_next[8 * i : 8 * i + 8, :]
        q, d = SEND_LOW[i]
        value = jnp.where(above, jnp.where(even, pair, following), 0.0)
        store_column(s0, q, 0, CZ + d, along_x(value, q))
        q, d = SEND_HIGH[i]
        value = jnp.where(below, jnp.where(even, following, pair), 0.0)
        store_column(s0, q, 0, -1 - d, along_x(value, q))
    last = CZ // 8 - 1
    spots = [(y, t) for y in (0, CY - 1) for t in (0, last)]
    tiles = []
    for p in range(Q):
        cx, cy, cz = DIRS[p]
        tiles.append(
            [s0[p, y + 1 + cy, pl.ds(Z0 + 8 * t + cz, 8), :] for y, t in spots]
            + [load_column(s0, p, cy, z + cz) for z in (-1, CZ)]
        )
    mixed = mix(w[...].astype(bf16), stacked(tiles + [None]))
    for q in range(Q):
        for c, (y, t) in enumerate(spots):
            s1[q, 1 + y, Z0 + 8 * t : Z0 + 8 * t + 8, :] = along_x(
                mixed[8 * q : 8 * q + 8, X * c : X * c + X], q
            )
    for c, (z, channels, valid) in enumerate(((-1, Z_DOWN, below), (CZ, Z_UP, above))):
        for q in channels:
            value = mixed[8 * q : 8 * q + 8, X * (4 + c) : X * (4 + c) + X]
            store_column(s1, q, 0, z, along_x(jnp.where(valid, value, 0.0), q))
    for side, (y, channels) in enumerate(((0, Y_UP), (CY - 1, Y_DOWN))):
        message = both.at[side]
        message[16:END_ROWS, :] = jnp.zeros((8, X), f32)
        for i, q in enumerate(channels):
            cz = DIRS[q][2]
            for e, z in enumerate(RAW_CELLS[cz]):
                message[pl.ds(RAW_ENDS + 2 * i + e, 1), :] = s0[q, 1 + y, pl.ds(Z0 + z, 1), :]
            for e, z in enumerate((0, CZ - 1)):
                message[pl.ds(MIXED_ENDS + 2 * i + e, 1), :] = s1[q, 1 + y, pl.ds(Z0 + z, 1), :]
            if cz:
                z, e = (CZ, 0) if cz > 0 else (-1, 1)
                message[pl.ds(CORNERS + e, 1), :] = s1[q, 1 + y, pl.ds(Z0 + z, 1), :]
    even_y = lax.rem(lax.axis_index("gy"), 2) == 0
    to_pair[...] = jnp.where(even_y, both[1], both[0])
    to_next[...] = jnp.where(even_y, both[0], both[1])


RAW_CELLS = {0: (-1, CZ), 1: (CZ, CZ + 1), -1: (-2, -1)}


def store_line(s1, y, out):
    for q in range(Q):
        for t in range(CZ // 8):
            s1[q, 1 + y, Z0 + 8 * t : Z0 + 8 * t + 8, :] = along_x(
                out[8 * q : 8 * q + 8, X * t : X * t + X], q
            )


def five_lines(ref, spare, lead, channels):
    tiles = []
    for i, p in enumerate(channels):
        cz = DIRS[p][2]
        line = ref[lead(i, p) + (pl.ds(Z0 + cz, CZ), slice(None))]
        for e, z in enumerate((-1, CZ)):
            spare[pl.ds(8 * i + e, 1), :] = ref[lead(i, p) + (pl.ds(Z0 + z + cz, 1), slice(None))]
        tiles.append(line_tiles(line) + [spare[8 * i : 8 * i + 8, :]])
    return stacked(tiles + [None])


def inner_rows_kernel(
    s0, w, s1_in, collision, panel, cell, direction,
    s1, w_up, w_down, out, scaled, rows, pick, kept, spare, numbers, sem,
):
    del s1_in
    iy = lax.axis_index("gy")
    iz = lax.axis_index("gz")
    above = iz < lax.axis_size("gz") - 1
    below = iz > 0
    weights = w[...].astype(bf16)
    for y in range(1, CY - 1):
        store_line(s1, y, mix(weights, read_row(s0, y)))
    for y in range(2, CY - 2):
        mixed = mix(weights, read_row(s1, y))
        for q in range(Q):
            for t in range(CZ // 8):
                value = mixed[8 * q : 8 * q + 8, X * t : X * t + X]
                kept[q, y - 2, 8 * t : 8 * t + 8, :] = value
                at = q * (CY * CZ) + y * CZ + 8 * t
                scaled[at : at + 8, :] = value * LINK_WEIGHTS[q]
    copy = pltpu.make_async_copy(kept, out.at[:, pl.ds(2, CY - 4), :, :], sem)
    copy.start()
    numbers[...] = jnp.zeros((numbers.shape[0], X), f32)
    numbers[:, 0:CAP] = panel[...].astype(f32).T
    pick[...] = direction[...] * (CY * CZ) + cell[...]

    @pl.loop(0, numbers.shape[0], unroll=8)
    def _(d):
        rows[pl.ds(d * (CAP + 1) + CAP, 1), 0, :] = numbers[pl.ds(d, 1), :]

    w_up[...] = spread_weights(collision[...], Y_UP, K2)
    w_down[...] = spread_weights(collision[...], Y_DOWN, K2)
    spare[...] = jnp.zeros((2, K2, X), f32)
    sides = (
        (0, CY - 1, CY, Y_UP, Y_DOWN, w_down, iy < lax.axis_size("gy") - 1),
        (1, 0, -1, Y_DOWN, Y_UP, w_up, iy > 0),
    )
    for side, y, halo, channels, sources, part, valid in sides:
        rows = [part[8 * q : 8 * q + 8, :] for q in channels]
        rows = jnp.concatenate(rows + [jnp.zeros_like(rows[0])], axis=0).astype(bf16)
        reads = five_lines(s0, spare.at[side], lambda i, p: (p, 1 + y), sources)
        mixed = jnp.where(valid, mix(rows, reads), 0.0)
        for i, q in enumerate(channels):
            for t in range(CZ // 8):
                s1[q, 1 + halo, Z0 + 8 * t : Z0 + 8 * t + 8, :] = along_x(
                    mixed[8 * i : 8 * i + 8, X * t : X * t + X], q
                )
            cz = DIRS[q][2]
            if cz:
                z, row, ok = (-1, 0, below) if cz < 0 else (CZ, 1, above)
                end = along_x(mixed[8 * i : 8 * i + 8, X * (CZ // 8) :], q)[row : row + 1, :]
                s1[q, 1 + halo, pl.ds(Z0 + z, 1), :] = jnp.where(ok, end, 0.0)
    copy.wait()


def outer_rows_kernel(
    s1_in, w, w_up, w_down, from_pair, from_next, ends_pair, ends_next, pick_in, scaled_in,
    rows_in, out_in,
    s1, scaled, rows, out, kept, raw, spare, pick, pick_sem, out_sem,
):
    del s1_in, scaled_in, rows_in, out_in
    fetch = pltpu.make_async_copy(pick_in, pick, pick_sem)
    fetch.start()
    iy = lax.axis_index("gy")
    iz = lax.axis_index("gz")
    weights = w[...].astype(bf16)
    z_ok = (iz > 0, iz < lax.axis_size("gz") - 1)
    first = lax.broadcasted_iota(jnp.int32, (8, X), 0) == 0
    final = lax.broadcasted_iota(jnp.int32, (8, X), 0) == 7
    spare[...] = jnp.zeros((2, K2, X), f32)
    even = lax.rem(iy, 2) == 0
    sides = (
        (0, CY - 1, CY, Y_UP, w_up, iy < lax.axis_size("gy") - 1),
        (1, 0, -1, Y_DOWN, w_down, iy > 0),
    )
    for side, y, halo, channels, part, valid in sides:
        arrived, others = ((from_pair, from_next), (from_next, from_pair))[side]
        ends, other_ends = ((ends_pair, ends_next), (ends_next, ends_pair))[side]
        ends = jnp.where(even, ends[...], other_ends[...])
        for i, q in enumerate(channels):
            cz = DIRS[q][2]
            at = pl.ds(RAW + CZ * i, CZ)
            line = jnp.where(even, arrived[at, :], others[at, :])
            raw[side, i, Z0 : Z0 + CZ, :] = jnp.where(valid, line, 0.0)
            for e, z in enumerate(RAW_CELLS[cz]):
                at = RAW_ENDS + 2 * i + e
                raw[side, i, pl.ds(Z0 + z, 1), :] = jnp.where(valid, ends[at : at + 1, :], 0.0)
        reads = five_lines(raw.at[side], spare.at[side], lambda i, p: (i,), channels)
        mixed = mix(part[...].astype(bf16), reads)
        for q in range(Q):
            for t in range(CZ // 8):
                at = pl.ds(Z0 + 8 * t, 8)
                s1[q, 1 + y, at, :] += along_x(mixed[8 * q : 8 * q + 8, X * t : X * t + X], q)
            cz = DIRS[q][2]
            if cz:
                row = 0 if cz < 0 else 1
                end = along_x(mixed[8 * q : 8 * q + 8, X * (CZ // 8) :], q)[row : row + 1, :]
                at = pl.ds(Z0 - 1 if cz < 0 else Z0 + CZ, 1)
                s1[q, 1 + y, at, :] += jnp.where(z_ok[row], end, 0.0)
        for i, q in enumerate(channels):
            for t in range(CZ // 8):
                at = pl.ds(MIXED + CZ * i + 8 * t, 8)
                value = jnp.where(even, arrived[at, :], others[at, :])
                at = MIXED_ENDS + 2 * i
                if t == 0:
                    value = jnp.where(first, ends[at : at + 1, :], value)
                if t == CZ // 8 - 1:
                    value = jnp.where(final, ends[at + 1 : at + 2, :], value)
                s1[q, 1 + halo, Z0 + 8 * t : Z0 + 8 * t + 8, :] += jnp.where(valid, value, 0.0)
            cz = DIRS[q][2]
            if cz:
                z, e = (CZ, 0) if cz > 0 else (-1, 1)
                value = ends[CORNERS + e : CORNERS + e + 1, :]
                s1[q, 1 + halo, pl.ds(Z0 + z, 1), :] += jnp.where(valid, value, 0.0)

    copies = [
        pltpu.make_async_copy(
            kept.at[:, pl.ds(2 * h, 2), :, :], out.at[:, pl.ds(6 * h, 2), :, :], out_sem.at[h]
        )
        for h in range(2)
    ]
    for k, y in enumerate((0, 1, CY - 2, CY - 1)):
        mixed = mix(weights, read_row(s1, y))
        for q in range(Q):
            for t in range(CZ // 8):
                value = mixed[8 * q : 8 * q + 8, X * t : X * t + X]
                kept[q, k, 8 * t : 8 * t + 8, :] = value
                at = q * (CY * CZ) + y * CZ + 8 * t
                scaled[at : at + 8, :] = value * LINK_WEIGHTS[q]
        if k % 2:
            copies[k // 2].start()
    fetch.wait()

    @pl.loop(0, pick.shape[1], unroll=4)
    def _(d):
        for k in range(CAP):
            rows[pl.ds(d * (CAP + 1) + k, 1), 0, :] = scaled[pl.ds(pick[k, d], 1), :]

    for copy in copies:
        copy.wait()


def sum_kernel(arrived, out):
    devices = arrived.shape[0] // (CAP + 1)
    numbers = arrived[pl.ds(CAP, devices, stride=CAP + 1), :].T
    panels = lax.broadcasted_iota(jnp.int32, (P_DEV, devices), 0).astype(f32)
    hot, rows = [], []
    for k in range(CAP):
        hot.append((numbers[k : k + 1, :] == panels).astype(f32).astype(bf16))
        rows.append(arrived[pl.ds(k, devices, stride=CAP + 1), :])
    hot = jnp.concatenate(hot, axis=1)
    high, low = split(jnp.concatenate(rows, axis=0))
    dot = functools.partial(jnp.dot, preferred_element_type=f32)
    out[...] = dot(hot, high) + dot(hot, low)


VMEM = pl.BlockSpec(memory_space=pltpu.VMEM)
HBM = pl.BlockSpec(memory_space=pltpu.HBM)
MIB = 1024 * 1024


def call(kernel, name, ins, outs, shapes, scratch=(), aliases=None, cost=None):
    return pl.pallas_call(
        kernel,
        out_shape=[jax.ShapeDtypeStruct(*s) for s in shapes],
        in_specs=ins,
        out_specs=outs,
        scratch_shapes=list(scratch),
        input_output_aliases=aliases or {},
        compiler_params=pltpu.CompilerParams(vmem_limit_bytes=32 * MIB),
        cost_estimate=cost
        and pl.CostEstimate(flops=cost, bytes_accessed=cost // 1000, transcendentals=cost // 1000),
        name=name,
    )


def pairings(gy, gz):
    def exchange(partner):
        found = []
        for y in range(gy):
            for z in range(gz):
                py, pz = partner(y, z)
                found.append((y * gz + z, py * gz + pz))
        return found

    def step(i, n):
        j = i - 1 if i % 2 == 0 else i + 1
        return j if 0 <= j < n else None

    def z_next(y, z):
        return (y ^ 1, z) if step(z, gz) is None else (y, step(z, gz))

    def y_next(y, z):
        return (y, z ^ 1) if step(y, gy) is None else (step(y, gy), z)

    return (
        exchange(lambda y, z: (y, z ^ 1)),
        exchange(z_next),
        exchange(lambda y, z: (y ^ 1, z)),
        exchange(y_next),
    )


def on_device(adjoint, collision, link_cell, link_dir, link_panel):
    gz = lax.axis_size("gz")
    gy = lax.axis_size("gy")
    devices = link_cell.shape[1]
    pad = (Q, CY + 2, ROWS, X)
    own = (Q, CY, CZ, X)
    flat = adjoint.reshape(Q, CY * CZ, X)
    dma = pltpu.SemaphoreType.DMA
    to_pair, to_next, empty = call(
        pack_z_kernel, "pack_z", [VMEM], [VMEM] * 3, [((Z_ROWS, X), f32)] * 2 + [((8, X), f32)],
        cost=4_000_000_000,
    )(flat)
    both = ("gy", "gz")
    z_pairs, z_nexts, y_pairs, y_nexts = pairings(gy, gz)
    from_pair = lax.ppermute(to_pair, both, z_pairs)
    from_next = lax.ppermute(to_next, both, z_nexts)
    lines = ((Y_ROWS, X), f32)
    wide = ((K1, 3 * K1), f32)
    narrow = ((K1, 3 * K2), f32)
    s0, s1, to_y_pair, to_y_next, w = call(
        bulk_rows_kernel, "bulk_rows", [VMEM] * 3, [VMEM] * 5,
        [(pad, f32), (pad, f32), lines, lines, wide],
    )(flat, collision, empty)
    from_y_pair = lax.ppermute(to_y_pair, both, y_pairs)
    from_y_next = lax.ppermute(to_y_next, both, y_nexts)
    s0, s1, to_y_pair, to_y_next = call(
        end_cells_kernel, "end_cells", [VMEM] * 5, [VMEM] * 4,
        [(pad, f32), (pad, f32), ((END_ROWS, X), f32), ((END_ROWS, X), f32)],
        scratch=[pltpu.VMEM((2, END_ROWS, X), f32)],
        aliases={0: 0, 1: 1},
    )(s0, s1, w, from_pair, from_next)
    ends_pair = lax.ppermute(to_y_pair, both, y_pairs)
    ends_next = lax.ppermute(to_y_next, both, y_nexts)
    table = ((Q * CY * CZ, X), f32)
    message = ((devices * (CAP + 1), 1, X), f32)
    s1, w_up, w_down, out, scaled, rows, pick = call(
        inner_rows_kernel, "inner_rows", [VMEM] * 7, [VMEM] * 3 + [HBM] + [VMEM] * 3,
        [(pad, f32), narrow, narrow, (own, f32), table]
        + [message, ((CAP, devices), jnp.int32)],
        scratch=[
            pltpu.VMEM((Q, CY - 4, CZ, X), f32),
            pltpu.VMEM((2, K2, X), f32),
            pltpu.VMEM((devices, X), f32),
            dma,
        ],
        aliases={2: 0},
    )(s0, w, s1, collision, link_panel[0].T, link_cell[0].T, link_dir[0].T)
    _, _, rows, out = call(
        outer_rows_kernel, "outer_rows", [VMEM] * 11 + [HBM], [VMEM] * 3 + [HBM],
        [(pad, f32), table, message, (own, f32)],
        scratch=[
            pltpu.VMEM((Q, 4, CZ, X), f32),
            pltpu.VMEM((2, 5, ROWS, X), f32),
            pltpu.VMEM((2, K2, X), f32),
            pltpu.SMEM((CAP, devices), jnp.int32),
            dma,
            dma((2,)),
        ],
        aliases={0: 0, 9: 1, 10: 2, 11: 3},
    )(s1, w, w_up, w_down, from_y_pair, from_y_next, ends_pair, ends_next, pick, scaled, rows, out)
    arrived = lax.all_to_all(
        rows.reshape(devices, CAP + 1, 1, X), ("gy", "gz"), split_axis=0, concat_axis=0, tiled=True
    )
    (panel_sens,) = call(sum_kernel, "sum_rows", [VMEM], [VMEM], [((P_DEV, X), f32)])(
        arrived.reshape(devices * (CAP + 1), X)
    )
    return out, panel_sens


def solution(mesh):
    placed = (
        P(None, "gy", "gz", None),
        P(),
        P(("gy", "gz"), None, None),
        P(("gy", "gz"), None, None),
        P(("gy", "gz"), None, None),
    )
    return jax.shard_map(
        on_device,
        mesh=mesh,
        in_specs=placed,
        out_specs=(P(None, "gy", "gz", None), P(("gy", "gz"), None)),
        check_vma=False,
    )
```

```python
import functools

import jax
import jax.numpy as jnp
from jax import lax
from jax.experimental import pallas as pl
from jax.experimental.pallas import tpu as pltpu
from jax.sharding import PartitionSpec as P

Q = 19
QP = 20
P_DEV = 64
CAP = 8
CY = 8
CZ = 32
X = 128
ROWS = 48
Z0 = 8

DIRS = [
    (0, 0, 0),
    (1, 0, 0),
    (-1, 0, 0),
    (0, 1, 0),
    (0, -1, 0),
    (0, 0, 1),
    (0, 0, -1),
    (1, 1, 0),
    (-1, -1, 0),
    (1, -1, 0),
    (-1, 1, 0),
    (1, 0, 1),
    (-1, 0, -1),
    (1, 0, -1),
    (-1, 0, 1),
    (0, 1, 1),
    (0, -1, -1),
    (0, 1, -1),
    (0, -1, 1),
]
LINK_WEIGHTS = [2.0] + [1.0 / 3.0] * 6 + [1.0 / 6.0] * 12

Y_UP = [q for q in range(Q) if DIRS[q][1] == 1]
Y_DOWN = [q for q in range(Q) if DIRS[q][1] == -1]
Z_UP = [q for q in range(Q) if DIRS[q][2] == 1]
Z_DOWN = [q for q in range(Q) if DIRS[q][2] == -1]
Z_FLAT = [q for q in range(Q) if DIRS[q][2] == 0]
SEND_LOW = [(q, 0) for q in Z_FLAT] + [(q, 0) for q in Z_UP] + [(q, 1) for q in Z_UP]
SEND_HIGH = [(q, 0) for q in Z_FLAT] + [(q, 0) for q in Z_DOWN] + [(q, 1) for q in Z_DOWN]

RAW = 0
MIXED = 5 * CZ
Y_ROWS = 10 * CZ
RAW_ENDS = 0
MIXED_ENDS = 10
CORNERS = 20
END_ROWS = 24
Z_ROWS = 8 * Q
K1 = QP * 8
K2 = 6 * 8

f32 = jnp.float32
bf16 = jnp.bfloat16


def along_x(value, q):
    cx = DIRS[q][0]
    if cx == 0:
        return value
    return pltpu.roll(value, (-cx) % X, value.ndim - 1)


def split(value):
    high = value.astype(bf16)
    return high, (value - high.astype(f32)).astype(bf16)


def mix(weights, reads):
    high, low = split(reads)
    return jnp.dot(
        weights, jnp.concatenate([high, low, high], axis=0), preferred_element_type=f32
    )


def stacked(tiles):
    count = max(len(t) for t in tiles if t is not None)
    zero = jnp.zeros((8, X), f32)
    full = [t if t is not None else [zero] * count for t in tiles]
    return jnp.concatenate(
        [jnp.concatenate([t[c] for t in full], axis=0) for c in range(count)], axis=1
    )


def line_tiles(line):
    return [line[8 * t : 8 * t + 8, :] for t in range(CZ // 8)]


def read_line(ref, p, y, shift=0):
    cx, cy, cz = DIRS[p]
    return ref[p, y + 1 + cy, pl.ds(Z0 + cz + shift, CZ), :]


def read_row(ref, y):
    return stacked([line_tiles(read_line(ref, p, y)) for p in range(Q)] + [None])


def load_column(ref, q, y, z):
    flat = ref.reshape(Q, (CY + 2) * ROWS, X)
    return flat[q, pl.ds((1 + y) * ROWS + Z0 + z, CY, stride=ROWS), :]


def store_column(ref, q, y, z, value):
    flat = ref.reshape(Q, (CY + 2) * ROWS, X)
    flat[q, pl.ds((1 + y) * ROWS + Z0 + z, CY, stride=ROWS), :] = value


def pack_z_kernel(field, w, to_pair, to_next, empty):
    del w
    empty[...] = jnp.zeros((8, X), f32)
    even = lax.rem(lax.axis_index("gz"), 2) == 0
    for i in range(Q):
        q, d = SEND_LOW[i]
        low = field[q, pl.ds(d, CY, stride=CZ), :]
        q, d = SEND_HIGH[i]
        high = field[q, pl.ds(CZ - 1 - d, CY, stride=CZ), :]
        to_pair[8 * i : 8 * i + 8, :] = jnp.where(even, high, low)
        to_next[8 * i : 8 * i + 8, :] = jnp.where(even, low, high)


def own_channel(shape, axis, channels):
    place = lax.broadcasted_iota(jnp.int32, shape, axis) // 8
    channel = lax.broadcasted_iota(jnp.int32, shape, 1 - axis)
    hit = jnp.zeros(shape, f32)
    for i, q in enumerate(channels):
        hit = jnp.where(jnp.logical_and(place == i, channel == q), 1.0, hit)
    return hit.astype(bf16)


def spread_weights(collision, channels, width):
    rows = (
        lax.broadcasted_iota(jnp.int32, (K1, Q), 0) // 8
        == lax.broadcasted_iota(jnp.int32, (K1, Q), 1)
    ).astype(f32).astype(bf16)
    columns = own_channel((width, Q), 0, channels)
    same = (
        lax.broadcasted_iota(jnp.int32, (K1, width), 0) % 8
        == lax.broadcasted_iota(jnp.int32, (K1, width), 1) % 8
    )
    dims = (((1,), (1,)), ((), ()))
    parts = []
    for part in split(collision):
        turned = lax.dot_general(rows, part, dims, preferred_element_type=f32).astype(bf16)
        wide = lax.dot_general(turned, columns, dims, preferred_element_type=f32)
        parts.append(jnp.where(same, wide, 0.0))
    return jnp.concatenate([parts[0], parts[0], parts[1]], axis=1)


def weights_kernel(collision, w, w_up, w_down):
    w[...] = spread_weights(collision[...], range(Q), K1)
    w_up[...] = spread_weights(collision[...], Y_UP, K2)
    w_down[...] = spread_weights(collision[...], Y_DOWN, K2)


EDGE_ROWS = (0, 1, CY - 2, CY - 1)


def bulk_rows_kernel(field, w, empty, s0, s1, to_pair, to_next):
    nothing = empty[...]
    for q in range(Q):
        for y in EDGE_ROWS:
            s0[q, 1 + y, Z0 : Z0 + CZ, :] = along_x(field[q, CZ * y : CZ * y + CZ, :], q)
    for q in Y_DOWN + Y_UP:
        for t in range(ROWS // 8):
            s0[q, 0 if DIRS[q][1] < 0 else CY + 1, 8 * t : 8 * t + 8, :] = nothing
    for q in range(Q):
        if DIRS[q][2]:
            for y in EDGE_ROWS:
                s0[q, 1 + y, 0:Z0, :] = nothing
                s0[q, 1 + y, Z0 + CZ : ROWS, :] = nothing
    weights = w[...].astype(bf16)
    for y in (0, CY - 1):
        store_line(s1, y, mix(weights, read_row(s0, y)))
    even = lax.rem(lax.axis_index("gy"), 2) == 0
    for ref, base in ((s0, RAW), (s1, MIXED)):
        for i in range(5):
            low = ref[Y_UP[i], 1, Z0 : Z0 + CZ, :]
            high = ref[Y_DOWN[i], CY, Z0 : Z0 + CZ, :]
            at = base + CZ * i
            to_pair[at : at + CZ, :] = jnp.where(even, high, low)
            to_next[at : at + CZ, :] = jnp.where(even, low, high)


def end_cells_kernel(
    s0_in, s1_in, w, from_pair, from_next, s0, s1, to_pair, to_next, both, corner
):
    del s0_in, s1_in
    iz = lax.axis_index("gz")
    even = lax.rem(iz, 2) == 0
    above = iz < lax.axis_size("gz") - 1
    below = iz > 0
    for i in range(Q):
        pair = from_pair[8 * i : 8 * i + 8, :]
        following = from_next[8 * i : 8 * i + 8, :]
        q, d = SEND_LOW[i]
        value = jnp.where(above, jnp.where(even, pair, following), 0.0)
        store_column(s0, q, 0, CZ + d, along_x(value, q))
        q, d = SEND_HIGH[i]
        value = jnp.where(below, jnp.where(even, following, pair), 0.0)
        store_column(s0, q, 0, -1 - d, along_x(value, q))
    last = CZ // 8 - 1
    spots = [(y, t) for y in (0, CY - 1) for t in (0, last)]
    corners = [(y, z) for y in (0, CY - 1) for z in (-1, CZ)]
    corner[...] = jnp.zeros((Q, 8, X), f32)
    tiles = []
    for p in range(Q):
        cx, cy, cz = DIRS[p]
        for c, (y, z) in enumerate(corners):
            corner[p, pl.ds(c, 1), :] = s0[p, y + 1 + cy, pl.ds(Z0 + z + cz, 1), :]
        tiles.append(
            [s0[p, y + 1 + cy, pl.ds(Z0 + 8 * t + cz, 8), :] for y, t in spots] + [corner[p]]
        )
    mixed = mix(w[...].astype(bf16), stacked(tiles + [None]))
    for q in range(Q):
        for c, (y, t) in enumerate(spots):
            s1[q, 1 + y, Z0 + 8 * t : Z0 + 8 * t + 8, :] = along_x(
                mixed[8 * q : 8 * q + 8, X * c : X * c + X], q
            )
        if DIRS[q][2]:
            ends = along_x(mixed[8 * q : 8 * q + 8, X * 4 :], q)
            for c, (y, z) in enumerate(corners):
                if DIRS[q][2] == (1 if z > 0 else -1):
                    value = jnp.where(above if z > 0 else below, ends[c : c + 1, :], 0.0)
                    s1[q, 1 + y, pl.ds(Z0 + z, 1), :] = value
    for side, (y, channels) in enumerate(((0, Y_UP), (CY - 1, Y_DOWN))):
        message = both.at[side]
        message[16:END_ROWS, :] = jnp.zeros((8, X), f32)
        for i, q in enumerate(channels):
            cz = DIRS[q][2]
            for e, z in enumerate(RAW_CELLS[cz]):
                message[pl.ds(RAW_ENDS + 2 * i + e, 1), :] = s0[q, 1 + y, pl.ds(Z0 + z, 1), :]
            for e, z in enumerate((0, CZ - 1)):
                message[pl.ds(MIXED_ENDS + 2 * i + e, 1), :] = s1[q, 1 + y, pl.ds(Z0 + z, 1), :]
            if cz:
                z, e = (CZ, 0) if cz > 0 else (-1, 1)
                message[pl.ds(CORNERS + e, 1), :] = s1[q, 1 + y, pl.ds(Z0 + z, 1), :]
    even_y = lax.rem(lax.axis_index("gy"), 2) == 0
    to_pair[...] = jnp.where(even_y, both[1], both[0])
    to_next[...] = jnp.where(even_y, both[0], both[1])


RAW_CELLS = {0: (-1, CZ), 1: (CZ, CZ + 1), -1: (-2, -1)}


def store_line(s1, y, out):
    for q in range(Q):
        for t in range(CZ // 8):
            s1[q, 1 + y, Z0 + 8 * t : Z0 + 8 * t + 8, :] = along_x(
                out[8 * q : 8 * q + 8, X * t : X * t + X], q
            )


def five_lines(ref, spare, lead, channels):
    tiles = []
    for i, p in enumerate(channels):
        cz = DIRS[p][2]
        line = ref[lead(i, p) + (pl.ds(Z0 + cz, CZ), slice(None))]
        for e, z in enumerate((-1, CZ)):
            spare[pl.ds(8 * i + e, 1), :] = ref[lead(i, p) + (pl.ds(Z0 + z + cz, 1), slice(None))]
        tiles.append(line_tiles(line) + [spare[8 * i : 8 * i + 8, :]])
    return stacked(tiles + [None])


def inner_rows_kernel(
    s0_in, w, s1_in, w_up, w_down, field, panel, cell, direction,
    s0, s1, out, scaled, rows, pick, kept, spare, numbers, sem,
):
    del s0_in, s1_in
    iy = lax.axis_index("gy")
    iz = lax.axis_index("gz")
    above = iz < lax.axis_size("gz") - 1
    below = iz > 0
    weights = w[...].astype(bf16)
    for y in range(2, CY - 2):
        for q in range(Q):
            s0[q, 1 + y, Z0 : Z0 + CZ, :] = along_x(field[q, CZ * y : CZ * y + CZ, :], q)
    reads = stacked(
        [
            [load_column(s0, p, DIRS[p][1], z + DIRS[p][2]) for z in (-1, CZ)]
            for p in range(Q)
        ]
        + [None]
    )
    mixed = mix(weights, reads)
    for c, (z, channels, valid) in enumerate(((-1, Z_DOWN, below), (CZ, Z_UP, above))):
        for q in channels:
            value = along_x(mixed[8 * q : 8 * q + 8, X * c : X * c + X], q)
            store_column(s1, q, 0, z, jnp.where(valid, value, 0.0))
    for y in range(1, CY - 1):
        store_line(s1, y, mix(weights, read_row(s0, y)))
    for y in range(2, CY - 2):
        mixed = mix(weights, read_row(s1, y))
        for q in range(Q):
            for t in range(CZ // 8):
                value = mixed[8 * q : 8 * q + 8, X * t : X * t + X]
                kept[q, y - 2, 8 * t : 8 * t + 8, :] = value
                at = q * (CY * CZ) + y * CZ + 8 * t
                scaled[at : at + 8, :] = value * LINK_WEIGHTS[q]
    copy = pltpu.make_async_copy(kept, out.at[:, pl.ds(2, CY - 4), :, :], sem)
    copy.start()
    numbers[...] = jnp.zeros((numbers.shape[0], X), f32)
    numbers[:, 0:CAP] = panel[...].astype(f32).T
    pick[...] = direction[...] * (CY * CZ) + cell[...]

    @pl.loop(0, numbers.shape[0], unroll=8)
    def _(d):
        rows[pl.ds(d * (CAP + 1) + CAP, 1), 0, :] = numbers[pl.ds(d, 1), :]

    spare[...] = jnp.zeros((2, K2, X), f32)
    sides = (
        (0, CY - 1, CY, Y_UP, Y_DOWN, w_down, iy < lax.axis_size("gy") - 1),
        (1, 0, -1, Y_DOWN, Y_UP, w_up, iy > 0),
    )
    for side, y, halo, channels, sources, part, valid in sides:
        rows = [part[8 * q : 8 * q + 8, :] for q in channels]
        rows = jnp.concatenate(rows + [jnp.zeros_like(rows[0])], axis=0).astype(bf16)
        reads = five_lines(s0, spare.at[side], lambda i, p: (p, 1 + y), sources)
        mixed = jnp.where(valid, mix(rows, reads), 0.0)
        for i, q in enumerate(channels):
            for t in range(CZ // 8):
                s1[q, 1 + halo, Z0 + 8 * t : Z0 + 8 * t + 8, :] = along_x(
                    mixed[8 * i : 8 * i + 8, X * t : X * t + X], q
                )
            cz = DIRS[q][2]
            if cz:
                z, row, ok = (-1, 0, below) if cz < 0 else (CZ, 1, above)
                end = along_x(mixed[8 * i : 8 * i + 8, X * (CZ // 8) :], q)[row : row + 1, :]
                s1[q, 1 + halo, pl.ds(Z0 + z, 1), :] = jnp.where(ok, end, 0.0)
    copy.wait()


def outer_rows_kernel(
    s1_in, w, w_up, w_down, from_pair, from_next, ends_pair, ends_next, pick_in, scaled_in,
    rows_in, out_in,
    s1, scaled, rows, out, kept, raw, spare, pick, pick_sem, out_sem,
):
    del s1_in, scaled_in, rows_in, out_in
    fetch = pltpu.make_async_copy(pick_in, pick, pick_sem)
    fetch.start()
    iy = lax.axis_index("gy")
    iz = lax.axis_index("gz")
    weights = w[...].astype(bf16)
    z_ok = (iz > 0, iz < lax.axis_size("gz") - 1)
    first = lax.broadcasted_iota(jnp.int32, (8, X), 0) == 0
    final = lax.broadcasted_iota(jnp.int32, (8, X), 0) == 7
    spare[...] = jnp.zeros((2, K2, X), f32)
    sides = (
        (0, CY - 1, CY, Y_UP, w_up, iy < lax.axis_size("gy") - 1),
        (1, 0, -1, Y_DOWN, w_down, iy > 0),
    )

    def take(side, bulk, ends):
        _, _, halo, channels, _, _ = sides[side]
        for i, q in enumerate(channels):
            cz = DIRS[q][2]
            raw[side, i, Z0 : Z0 + CZ, :] = bulk[RAW + CZ * i : RAW + CZ * i + CZ, :]
            for e, z in enumerate(RAW_CELLS[cz]):
                raw[side, i, pl.ds(Z0 + z, 1), :] = ends[pl.ds(RAW_ENDS + 2 * i + e, 1), :]
            for t in range(CZ // 8):
                value = bulk[MIXED + CZ * i + 8 * t : MIXED + CZ * i + 8 * t + 8, :]
                at = MIXED_ENDS + 2 * i
                if t == 0:
                    value = jnp.where(first, ends[at : at + 1, :], value)
                if t == CZ // 8 - 1:
                    value = jnp.where(final, ends[at + 1 : at + 2, :], value)
                s1[q, 1 + halo, Z0 + 8 * t : Z0 + 8 * t + 8, :] += value
            if cz:
                z, e = (CZ, 0) if cz > 0 else (-1, 1)
                s1[q, 1 + halo, pl.ds(Z0 + z, 1), :] += ends[CORNERS + e : CORNERS + e + 1, :]

    odd = lax.rem(iy, 2)
    for side, (_, _, _, _, _, valid) in enumerate(sides):
        pl.when(jnp.logical_and(valid, odd == side))(
            functools.partial(take, side, from_pair, ends_pair)
        )
        pl.when(jnp.logical_and(valid, odd != side))(
            functools.partial(take, side, from_next, ends_next)
        )

        @pl.when(jnp.logical_not(valid))
        def _(side=side):
            raw[side] = jnp.zeros((5, ROWS, X), f32)

    for side, y, halo, channels, part, valid in sides:
        reads = five_lines(raw.at[side], spare.at[side], lambda i, p: (i,), channels)
        mixed = mix(part[...].astype(bf16), reads)
        for q in range(Q):
            for t in range(CZ // 8):
                at = pl.ds(Z0 + 8 * t, 8)
                s1[q, 1 + y, at, :] += along_x(mixed[8 * q : 8 * q + 8, X * t : X * t + X], q)
            cz = DIRS[q][2]
            if cz:
                row = 0 if cz < 0 else 1
                end = along_x(mixed[8 * q : 8 * q + 8, X * (CZ // 8) :], q)[row : row + 1, :]
                at = pl.ds(Z0 - 1 if cz < 0 else Z0 + CZ, 1)
                s1[q, 1 + y, at, :] += jnp.where(z_ok[row], end, 0.0)

    copies = [
        pltpu.make_async_copy(
            kept.at[:, pl.ds(2 * h, 2), :, :], out.at[:, pl.ds(6 * h, 2), :, :], out_sem.at[h]
        )
        for h in range(2)
    ]
    for k, y in enumerate((0, 1, CY - 2, CY - 1)):
        mixed = mix(weights, read_row(s1, y))
        for q in range(Q):
            for t in range(CZ // 8):
                value = mixed[8 * q : 8 * q + 8, X * t : X * t + X]
                kept[q, k, 8 * t : 8 * t + 8, :] = value
                at = q * (CY * CZ) + y * CZ + 8 * t
                scaled[at : at + 8, :] = value * LINK_WEIGHTS[q]
        if k % 2:
            copies[k // 2].start()
    fetch.wait()

    @pl.loop(0, pick.shape[1], unroll=8)
    def _(d):
        for k in range(CAP):
            rows[pl.ds(d * (CAP + 1) + k, 1), 0, :] = scaled[pl.ds(pick[k, d], 1), :]

    for copy in copies:
        copy.wait()


def sum_kernel(arrived, out):
    devices = arrived.shape[0] // (CAP + 1)
    numbers = arrived[pl.ds(CAP, devices, stride=CAP + 1), :].T
    panels = lax.broadcasted_iota(jnp.int32, (P_DEV, devices), 0).astype(f32)
    hot, rows = [], []
    for k in range(CAP):
        hot.append((numbers[k : k + 1, :] == panels).astype(f32).astype(bf16))
        rows.append(arrived[pl.ds(k, devices, stride=CAP + 1), :])
    hot = jnp.concatenate(hot, axis=1)
    high, low = split(jnp.concatenate(rows, axis=0))
    dot = functools.partial(jnp.dot, preferred_element_type=f32)
    out[...] = dot(hot, high) + dot(hot, low)


VMEM = pl.BlockSpec(memory_space=pltpu.VMEM)
HBM = pl.BlockSpec(memory_space=pltpu.HBM)
MIB = 1024 * 1024


def call(kernel, name, ins, outs, shapes, scratch=(), aliases=None, cost=None):
    return pl.pallas_call(
        kernel,
        out_shape=[jax.ShapeDtypeStruct(*s) for s in shapes],
        in_specs=ins,
        out_specs=outs,
        scratch_shapes=list(scratch),
        input_output_aliases=aliases or {},
        compiler_params=pltpu.CompilerParams(vmem_limit_bytes=32 * MIB),
        cost_estimate=cost
        and pl.CostEstimate(flops=cost, bytes_accessed=cost // 1000, transcendentals=cost // 1000),
        name=name,
    )


def pairings(gy, gz):
    def exchange(partner):
        found = []
        for y in range(gy):
            for z in range(gz):
                py, pz = partner(y, z)
                found.append((y * gz + z, py * gz + pz))
        return found

    def step(i, n):
        j = i - 1 if i % 2 == 0 else i + 1
        return j if 0 <= j < n else None

    def z_next(y, z):
        return (y ^ 1, z) if step(z, gz) is None else (y, step(z, gz))

    def y_next(y, z):
        return (y, z ^ 1) if step(y, gy) is None else (step(y, gy), z)

    return (
        exchange(lambda y, z: (y, z ^ 1)),
        exchange(z_next),
        exchange(lambda y, z: (y ^ 1, z)),
        exchange(y_next),
    )


def on_device(adjoint, collision, link_cell, link_dir, link_panel):
    gz = lax.axis_size("gz")
    gy = lax.axis_size("gy")
    devices = link_cell.shape[1]
    pad = (Q, CY + 2, ROWS, X)
    own = (Q, CY, CZ, X)
    flat = adjoint.reshape(Q, CY * CZ, X)
    dma = pltpu.SemaphoreType.DMA
    wide = ((K1, 3 * K1), f32)
    narrow = ((K1, 3 * K2), f32)
    w, w_up, w_down = call(
        weights_kernel, "weights", [VMEM], [VMEM] * 3, [wide, narrow, narrow], cost=4_000_000_000
    )(collision)
    to_pair, to_next, empty = call(
        pack_z_kernel, "pack_z", [VMEM] * 2, [VMEM] * 3, [((Z_ROWS, X), f32)] * 2 + [((8, X), f32)],
        cost=4_000_000_000,
    )(flat, w)
    both = ("gy", "gz")
    z_pairs, z_nexts, y_pairs, y_nexts = pairings(gy, gz)
    from_pair = lax.ppermute(to_pair, both, z_pairs)
    from_next = lax.ppermute(to_next, both, z_nexts)
    lines = ((Y_ROWS, X), f32)
    s0, s1, to_y_pair, to_y_next = call(
        bulk_rows_kernel, "bulk_rows", [VMEM] * 3, [VMEM] * 4,
        [(pad, f32), (pad, f32), lines, lines],
    )(flat, w, empty)
    from_y_pair = lax.ppermute(to_y_pair, both, y_pairs)
    from_y_next = lax.ppermute(to_y_next, both, y_nexts)
    s0, s1, to_y_pair, to_y_next = call(
        end_cells_kernel, "end_cells", [VMEM] * 5, [VMEM] * 4,
        [(pad, f32), (pad, f32), ((END_ROWS, X), f32), ((END_ROWS, X), f32)],
        scratch=[pltpu.VMEM((2, END_ROWS, X), f32), pltpu.VMEM((Q, 8, X), f32)],
        aliases={0: 0, 1: 1},
    )(s0, s1, w, from_pair, from_next)
    ends_pair = lax.ppermute(to_y_pair, both, y_pairs)
    ends_next = lax.ppermute(to_y_next, both, y_nexts)
    table = ((Q * CY * CZ, X), f32)
    message = ((devices * (CAP + 1), 1, X), f32)
    _, s1, out, scaled, rows, pick = call(
        inner_rows_kernel, "inner_rows", [VMEM] * 9, [VMEM] * 2 + [HBM] + [VMEM] * 3,
        [(pad, f32), (pad, f32), (own, f32), table]
        + [message, ((CAP, devices), jnp.int32)],
        scratch=[
            pltpu.VMEM((Q, CY - 4, CZ, X), f32),
            pltpu.VMEM((2, K2, X), f32),
            pltpu.VMEM((devices, X), f32),
            dma,
        ],
        cost=4_000_000_000,
        aliases={0: 0, 2: 1},
    )(s0, w, s1, w_up, w_down, flat, link_panel[0].T, link_cell[0].T, link_dir[0].T)
    _, _, rows, out = call(
        outer_rows_kernel, "outer_rows", [VMEM] * 11 + [HBM], [VMEM] * 3 + [HBM],
        [(pad, f32), table, message, (own, f32)],
        scratch=[
            pltpu.VMEM((Q, 4, CZ, X), f32),
            pltpu.VMEM((2, 5, ROWS, X), f32),
            pltpu.VMEM((2, K2, X), f32),
            pltpu.SMEM((CAP, devices), jnp.int32),
            dma,
            dma((2,)),
        ],
        aliases={0: 0, 9: 1, 10: 2, 11: 3},
    )(s1, w, w_up, w_down, from_y_pair, from_y_next, ends_pair, ends_next, pick, scaled, rows, out)
    arrived = lax.all_to_all(
        rows.reshape(devices, CAP + 1, 1, X), ("gy", "gz"), split_axis=0, concat_axis=0, tiled=True
    )
    (panel_sens,) = call(sum_kernel, "sum_rows", [VMEM], [VMEM], [((P_DEV, X), f32)])(
        arrived.reshape(devices * (CAP + 1), X)
    )
    return out, panel_sens


def solution(mesh):
    placed = (
        P(None, "gy", "gz", None),
        P(),
        P(("gy", "gz"), None, None),
        P(("gy", "gz"), None, None),
        P(("gy", "gz"), None, None),
    )
    return jax.shard_map(
        on_device,
        mesh=mesh,
        in_specs=placed,
        out_specs=(P(None, "gy", "gz", None), P(("gy", "gz"), None)),
        check_vma=False,
    )
```

```python
import functools

import jax
import jax.numpy as jnp
from jax import lax
from jax.experimental import pallas as pl
from jax.experimental.pallas import tpu as pltpu
from jax.sharding import PartitionSpec as P

Q = 19
QP = 20
P_DEV = 64
CAP = 8
CY = 8
CZ = 32
X = 128
ROWS = 48
Z0 = 8

DIRS = [
    (0, 0, 0),
    (1, 0, 0),
    (-1, 0, 0),
    (0, 1, 0),
    (0, -1, 0),
    (0, 0, 1),
    (0, 0, -1),
    (1, 1, 0),
    (-1, -1, 0),
    (1, -1, 0),
    (-1, 1, 0),
    (1, 0, 1),
    (-1, 0, -1),
    (1, 0, -1),
    (-1, 0, 1),
    (0, 1, 1),
    (0, -1, -1),
    (0, 1, -1),
    (0, -1, 1),
]
LINK_WEIGHTS = [2.0] + [1.0 / 3.0] * 6 + [1.0 / 6.0] * 12

Y_UP = [q for q in range(Q) if DIRS[q][1] == 1]
Y_DOWN = [q for q in range(Q) if DIRS[q][1] == -1]
Z_UP = [q for q in range(Q) if DIRS[q][2] == 1]
Z_DOWN = [q for q in range(Q) if DIRS[q][2] == -1]
Z_FLAT = [q for q in range(Q) if DIRS[q][2] == 0]
SEND_LOW = [(q, 0) for q in Z_FLAT] + [(q, 0) for q in Z_UP] + [(q, 1) for q in Z_UP]
SEND_HIGH = [(q, 0) for q in Z_FLAT] + [(q, 0) for q in Z_DOWN] + [(q, 1) for q in Z_DOWN]

RAW = 0
MIXED = 5 * CZ
Y_ROWS = 10 * CZ
RAW_ENDS = 0
MIXED_ENDS = 10
CORNERS = 20
END_ROWS = 24
Z_ROWS = 8 * Q
PAIR = 1 << 13
K1 = QP * 8
K2 = 6 * 8

f32 = jnp.float32
bf16 = jnp.bfloat16


def along_x(value, q):
    cx = DIRS[q][0]
    if cx == 0:
        return value
    return pltpu.roll(value, (-cx) % X, value.ndim - 1)


def split(value):
    high = value.astype(bf16)
    return high, (value - high.astype(f32)).astype(bf16)


def mix(weights, reads):
    high, low = split(reads)
    return jnp.dot(
        weights, jnp.concatenate([high, low, high], axis=0), preferred_element_type=f32
    )


def stacked(tiles):
    count = max(len(t) for t in tiles if t is not None)
    zero = jnp.zeros((8, X), f32)
    full = [t if t is not None else [zero] * count for t in tiles]
    return jnp.concatenate(
        [jnp.concatenate([t[c] for t in full], axis=0) for c in range(count)], axis=1
    )


def line_tiles(line):
    return [line[8 * t : 8 * t + 8, :] for t in range(CZ // 8)]


def read_line(ref, p, y, shift=0):
    cx, cy, cz = DIRS[p]
    return ref[p, y + 1 + cy, pl.ds(Z0 + cz + shift, CZ), :]


def read_row(ref, y):
    return stacked([line_tiles(read_line(ref, p, y)) for p in range(Q)] + [None])


def load_column(ref, q, y, z):
    flat = ref.reshape(Q, (CY + 2) * ROWS, X)
    return flat[q, pl.ds((1 + y) * ROWS + Z0 + z, CY, stride=ROWS), :]


def store_column(ref, q, y, z, value):
    flat = ref.reshape(Q, (CY + 2) * ROWS, X)
    flat[q, pl.ds((1 + y) * ROWS + Z0 + z, CY, stride=ROWS), :] = value


def pack_z_kernel(field, w, to_pair, to_next, empty):
    del w
    empty[...] = jnp.zeros((8, X), f32)
    even = lax.rem(lax.axis_index("gz"), 2) == 0
    for i in range(Q):
        q, d = SEND_LOW[i]
        low = field[q, pl.ds(d, CY, stride=CZ), :]
        q, d = SEND_HIGH[i]
        high = field[q, pl.ds(CZ - 1 - d, CY, stride=CZ), :]
        to_pair[8 * i : 8 * i + 8, :] = jnp.where(even, high, low)
        to_next[8 * i : 8 * i + 8, :] = jnp.where(even, low, high)


def own_channel(shape, axis, channels):
    place = lax.broadcasted_iota(jnp.int32, shape, axis) // 8
    channel = lax.broadcasted_iota(jnp.int32, shape, 1 - axis)
    hit = jnp.zeros(shape, f32)
    for i, q in enumerate(channels):
        hit = jnp.where(jnp.logical_and(place == i, channel == q), 1.0, hit)
    return hit.astype(bf16)


def spread_weights(collision, channels, width):
    rows = (
        lax.broadcasted_iota(jnp.int32, (K1, Q), 0) // 8
        == lax.broadcasted_iota(jnp.int32, (K1, Q), 1)
    ).astype(f32).astype(bf16)
    columns = own_channel((width, Q), 0, channels)
    same = (
        lax.broadcasted_iota(jnp.int32, (K1, width), 0) % 8
        == lax.broadcasted_iota(jnp.int32, (K1, width), 1) % 8
    )
    dims = (((1,), (1,)), ((), ()))
    parts = []
    for part in split(collision):
        turned = lax.dot_general(rows, part, dims, preferred_element_type=f32).astype(bf16)
        wide = lax.dot_general(turned, columns, dims, preferred_element_type=f32)
        parts.append(jnp.where(same, wide, 0.0))
    return jnp.concatenate([parts[0], parts[0], parts[1]], axis=1)


def weights_kernel(collision, w, w_up, w_down):
    w[...] = spread_weights(collision[...], range(Q), K1)
    w_up[...] = spread_weights(collision[...], Y_UP, K2)
    w_down[...] = spread_weights(collision[...], Y_DOWN, K2)


EDGE_ROWS = (0, 1, CY - 2, CY - 1)


def bulk_rows_kernel(field, w, empty, s0, s1, to_pair, to_next):
    nothing = empty[...]
    for q in range(Q):
        for y in EDGE_ROWS:
            s0[q, 1 + y, Z0 : Z0 + CZ, :] = along_x(field[q, CZ * y : CZ * y + CZ, :], q)
    for q in Y_DOWN + Y_UP:
        for t in range(ROWS // 8):
            s0[q, 0 if DIRS[q][1] < 0 else CY + 1, 8 * t : 8 * t + 8, :] = nothing
    for q in range(Q):
        if DIRS[q][2]:
            for y in EDGE_ROWS:
                s0[q, 1 + y, 0:Z0, :] = nothing
                s0[q, 1 + y, Z0 + CZ : ROWS, :] = nothing
    weights = w[...].astype(bf16)
    for y in (0, CY - 1):
        store_line(s1, y, mix(weights, read_row(s0, y)))
    even = lax.rem(lax.axis_index("gy"), 2) == 0
    for ref, base in ((s0, RAW), (s1, MIXED)):
        for i in range(5):
            low = ref[Y_UP[i], 1, Z0 : Z0 + CZ, :]
            high = ref[Y_DOWN[i], CY, Z0 : Z0 + CZ, :]
            at = base + CZ * i
            to_pair[at : at + CZ, :] = jnp.where(even, high, low)
            to_next[at : at + CZ, :] = jnp.where(even, low, high)


def end_cells_kernel(
    s0_in, s1_in, w, from_pair, from_next, s0, s1, to_pair, to_next, both, corner
):
    del s0_in, s1_in
    iz = lax.axis_index("gz")
    even = lax.rem(iz, 2) == 0
    above = iz < lax.axis_size("gz") - 1
    below = iz > 0
    for i in range(Q):
        pair = from_pair[8 * i : 8 * i + 8, :]
        following = from_next[8 * i : 8 * i + 8, :]
        q, d = SEND_LOW[i]
        value = jnp.where(above, jnp.where(even, pair, following), 0.0)
        store_column(s0, q, 0, CZ + d, along_x(value, q))
        q, d = SEND_HIGH[i]
        value = jnp.where(below, jnp.where(even, following, pair), 0.0)
        store_column(s0, q, 0, -1 - d, along_x(value, q))
    last = CZ // 8 - 1
    spots = [(y, t) for y in (0, CY - 1) for t in (0, last)]
    corners = [(y, z) for y in (0, CY - 1) for z in (-1, CZ)]
    corner[...] = jnp.zeros((Q, 8, X), f32)
    tiles = []
    for p in range(Q):
        cx, cy, cz = DIRS[p]
        for c, (y, z) in enumerate(corners):
            corner[p, pl.ds(c, 1), :] = s0[p, y + 1 + cy, pl.ds(Z0 + z + cz, 1), :]
        tiles.append(
            [s0[p, y + 1 + cy, pl.ds(Z0 + 8 * t + cz, 8), :] for y, t in spots] + [corner[p]]
        )
    mixed = mix(w[...].astype(bf16), stacked(tiles + [None]))
    for q in range(Q):
        for c, (y, t) in enumerate(spots):
            s1[q, 1 + y, Z0 + 8 * t : Z0 + 8 * t + 8, :] = along_x(
                mixed[8 * q : 8 * q + 8, X * c : X * c + X], q
            )
        if DIRS[q][2]:
            ends = along_x(mixed[8 * q : 8 * q + 8, X * 4 :], q)
            for c, (y, z) in enumerate(corners):
                if DIRS[q][2] == (1 if z > 0 else -1):
                    value = jnp.where(above if z > 0 else below, ends[c : c + 1, :], 0.0)
                    s1[q, 1 + y, pl.ds(Z0 + z, 1), :] = value
    for side, (y, channels) in enumerate(((0, Y_UP), (CY - 1, Y_DOWN))):
        message = both.at[side]
        message[16:END_ROWS, :] = jnp.zeros((8, X), f32)
        for i, q in enumerate(channels):
            cz = DIRS[q][2]
            for e, z in enumerate(RAW_CELLS[cz]):
                message[pl.ds(RAW_ENDS + 2 * i + e, 1), :] = s0[q, 1 + y, pl.ds(Z0 + z, 1), :]
            for e, z in enumerate((0, CZ - 1)):
                message[pl.ds(MIXED_ENDS + 2 * i + e, 1), :] = s1[q, 1 + y, pl.ds(Z0 + z, 1), :]
            if cz:
                z, e = (CZ, 0) if cz > 0 else (-1, 1)
                message[pl.ds(CORNERS + e, 1), :] = s1[q, 1 + y, pl.ds(Z0 + z, 1), :]
    even_y = lax.rem(lax.axis_index("gy"), 2) == 0
    to_pair[...] = jnp.where(even_y, both[1], both[0])
    to_next[...] = jnp.where(even_y, both[0], both[1])


RAW_CELLS = {0: (-1, CZ), 1: (CZ, CZ + 1), -1: (-2, -1)}


def store_line(s1, y, out):
    for q in range(Q):
        for t in range(CZ // 8):
            s1[q, 1 + y, Z0 + 8 * t : Z0 + 8 * t + 8, :] = along_x(
                out[8 * q : 8 * q + 8, X * t : X * t + X], q
            )


def five_lines(ref, spare, lead, channels):
    tiles = []
    for i, p in enumerate(channels):
        cz = DIRS[p][2]
        line = ref[lead(i, p) + (pl.ds(Z0 + cz, CZ), slice(None))]
        for e, z in enumerate((-1, CZ)):
            spare[pl.ds(8 * i + e, 1), :] = ref[lead(i, p) + (pl.ds(Z0 + z + cz, 1), slice(None))]
        tiles.append(line_tiles(line) + [spare[8 * i : 8 * i + 8, :]])
    return stacked(tiles + [None])


def inner_rows_kernel(
    s0_in, w, s1_in, w_up, w_down, field, panel, cell, direction,
    s0, s1, out, scaled, rows, pick, kept, spare, numbers, sem,
):
    del s0_in, s1_in
    iy = lax.axis_index("gy")
    iz = lax.axis_index("gz")
    above = iz < lax.axis_size("gz") - 1
    below = iz > 0
    weights = w[...].astype(bf16)
    for y in range(2, CY - 2):
        for q in range(Q):
            s0[q, 1 + y, Z0 : Z0 + CZ, :] = along_x(field[q, CZ * y : CZ * y + CZ, :], q)
    reads = stacked(
        [
            [load_column(s0, p, DIRS[p][1], z + DIRS[p][2]) for z in (-1, CZ)]
            for p in range(Q)
        ]
        + [None]
    )
    mixed = mix(weights, reads)
    for c, (z, channels, valid) in enumerate(((-1, Z_DOWN, below), (CZ, Z_UP, above))):
        for q in channels:
            value = along_x(mixed[8 * q : 8 * q + 8, X * c : X * c + X], q)
            store_column(s1, q, 0, z, jnp.where(valid, value, 0.0))
    for y in range(1, CY - 1):
        store_line(s1, y, mix(weights, read_row(s0, y)))
    for y in range(2, CY - 2):
        mixed = mix(weights, read_row(s1, y))
        for q in range(Q):
            for t in range(CZ // 8):
                value = mixed[8 * q : 8 * q + 8, X * t : X * t + X]
                kept[q, y - 2, 8 * t : 8 * t + 8, :] = value
                at = q * (CY * CZ) + y * CZ + 8 * t
                scaled[at : at + 8, :] = value * LINK_WEIGHTS[q]
    copy = pltpu.make_async_copy(kept, out.at[:, pl.ds(2, CY - 4), :, :], sem)
    copy.start()
    numbers[...] = jnp.zeros((numbers.shape[0], X), f32)
    numbers[:, 0:CAP] = panel[...].astype(f32).T
    place = direction[...] * (CY * CZ) + cell[...]
    pick[...] = place[: CAP // 2] + place[CAP // 2 :] * PAIR

    @pl.loop(0, numbers.shape[0], unroll=8)
    def _(d):
        rows[pl.ds(d * (CAP + 1) + CAP, 1), 0, :] = numbers[pl.ds(d, 1), :]

    spare[...] = jnp.zeros((2, K2, X), f32)
    sides = (
        (0, CY - 1, CY, Y_UP, Y_DOWN, w_down, iy < lax.axis_size("gy") - 1),
        (1, 0, -1, Y_DOWN, Y_UP, w_up, iy > 0),
    )
    for side, y, halo, channels, sources, part, valid in sides:
        rows = [part[8 * q : 8 * q + 8, :] for q in channels]
        rows = jnp.concatenate(rows + [jnp.zeros_like(rows[0])], axis=0).astype(bf16)
        reads = five_lines(s0, spare.at[side], lambda i, p: (p, 1 + y), sources)
        mixed = jnp.where(valid, mix(rows, reads), 0.0)
        for i, q in enumerate(channels):
            for t in range(CZ // 8):
                s1[q, 1 + halo, Z0 + 8 * t : Z0 + 8 * t + 8, :] = along_x(
                    mixed[8 * i : 8 * i + 8, X * t : X * t + X], q
                )
            cz = DIRS[q][2]
            if cz:
                z, row, ok = (-1, 0, below) if cz < 0 else (CZ, 1, above)
                end = along_x(mixed[8 * i : 8 * i + 8, X * (CZ // 8) :], q)[row : row + 1, :]
                s1[q, 1 + halo, pl.ds(Z0 + z, 1), :] = jnp.where(ok, end, 0.0)
    copy.wait()


def sides_of(iy, w_up, w_down):
    return (
        (CY - 1, CY, Y_UP, w_up, iy < lax.axis_size("gy") - 1),
        (0, -1, Y_DOWN, w_down, iy > 0),
    )


def take_arrivals(iy, sides, take, from_pair, from_next):
    odd = lax.rem(iy, 2)
    for side in range(2):
        valid = sides[side][-1]
        pl.when(jnp.logical_and(valid, odd == side))(functools.partial(take, side, from_pair))
        pl.when(jnp.logical_and(valid, odd != side))(functools.partial(take, side, from_next))


def store_mixed(mixed, q, y, k, tiles, kept, scaled):
    for c, t in enumerate(tiles):
        value = mixed[8 * q : 8 * q + 8, X * c : X * c + X]
        kept[q, k, 8 * t : 8 * t + 8, :] = value
        at = q * (CY * CZ) + y * CZ + 8 * t
        scaled[at : at + 8, :] = value * LINK_WEIGHTS[q]


def read_tiles(ref, y, tiles):
    return stacked(
        [
            [ref[p, y + 1 + DIRS[p][1], pl.ds(Z0 + 8 * t + DIRS[p][2], 8), :] for t in tiles]
            for p in range(Q)
        ]
        + [None]
    )


MIDDLE = tuple(range(1, CZ // 8 - 1))
OUTER = (0, CZ // 8 - 1)


def middle_tiles_kernel(
    s1_in, w, w_up, w_down, from_pair, from_next, scaled_in, s1, scaled, raw, kept
):
    del s1_in, scaled_in
    iy = lax.axis_index("gy")
    weights = w[...].astype(bf16)
    cells = lax.broadcasted_iota(jnp.int32, (8, X), 0)
    sides = sides_of(iy, w_up, w_down)
    raw[...] = jnp.zeros((2, 5, ROWS, X), f32)

    def take(side, bulk):
        _, halo, channels, _, _ = sides[side]
        for i, q in enumerate(channels):
            raw[side, i, Z0 : Z0 + CZ, :] = bulk[RAW + CZ * i : RAW + CZ * i + CZ, :]
            for t in range(CZ // 8):
                value = bulk[MIXED + CZ * i + 8 * t : MIXED + CZ * i + 8 * t + 8, :]
                if t == 0:
                    value = jnp.where(cells > 0, value, 0.0)
                if t == CZ // 8 - 1:
                    value = jnp.where(cells < 7, value, 0.0)
                s1[q, 1 + halo, Z0 + 8 * t : Z0 + 8 * t + 8, :] += value

    take_arrivals(iy, sides, take, from_pair, from_next)
    for side, (y, _, channels, part, _) in enumerate(sides):
        tiles = [
            line_tiles(raw[side, i, pl.ds(Z0 + DIRS[p][2], CZ), :])
            for i, p in enumerate(channels)
        ]
        mixed = mix(part[...].astype(bf16), stacked(tiles + [None]))
        for q in range(Q):
            for t in range(CZ // 8):
                s1[q, 1 + y, Z0 + 8 * t : Z0 + 8 * t + 8, :] += along_x(
                    mixed[8 * q : 8 * q + 8, X * t : X * t + X], q
                )
    for k, y in enumerate(EDGE_ROWS):
        mixed = mix(weights, read_tiles(s1, y, MIDDLE))
        for q in range(Q):
            store_mixed(mixed, q, y, k, MIDDLE, kept, scaled)


def outer_tiles_kernel(
    s1_in, w, w_up, w_down, ends_pair, ends_next, pick_in, scaled_in, raw_in, kept_in,
    rows_in, out_in,
    s1, scaled, raw, kept, rows, out, spare, pick, pick_sem, out_sem,
):
    del s1_in, scaled_in, raw_in, kept_in, rows_in, out_in
    fetch = pltpu.make_async_copy(pick_in, pick, pick_sem)
    fetch.start()
    iy = lax.axis_index("gy")
    iz = lax.axis_index("gz")
    weights = w[...].astype(bf16)
    z_ok = (iz > 0, iz < lax.axis_size("gz") - 1)
    sides = sides_of(iy, w_up, w_down)
    spare[...] = jnp.zeros((2, K2, X), f32)

    def take(side, ends):
        _, halo, channels, _, _ = sides[side]
        for i, q in enumerate(channels):
            cz = DIRS[q][2]
            for e, z in enumerate(RAW_CELLS[cz]):
                raw[side, i, pl.ds(Z0 + z, 1), :] = ends[pl.ds(RAW_ENDS + 2 * i + e, 1), :]
            for e, z in enumerate((0, CZ - 1)):
                at = pl.ds(MIXED_ENDS + 2 * i + e, 1)
                s1[q, 1 + halo, pl.ds(Z0 + z, 1), :] += ends[at, :]
            if cz:
                z, e = (CZ, 0) if cz > 0 else (-1, 1)
                s1[q, 1 + halo, pl.ds(Z0 + z, 1), :] += ends[CORNERS + e : CORNERS + e + 1, :]

    take_arrivals(iy, sides, take, ends_pair, ends_next)
    for side, (y, _, channels, part, _) in enumerate(sides):
        for i, p in enumerate(channels):
            cz = DIRS[p][2]
            wanted = [(2, cz - 1), (3, CZ + cz)]
            if cz < 0:
                wanted.append((0, -1))
            if cz > 0:
                wanted.append((1, CZ))
            for j, z in wanted:
                spare[side, pl.ds(8 * i + j, 1), :] = raw[side, i, pl.ds(Z0 + z, 1), :]
        mixed = mix(part[...].astype(bf16), spare[side])
        for q in range(Q):
            cz = DIRS[q][2]
            value = along_x(mixed[8 * q : 8 * q + 8, :], q)
            for j, z in ((0, 0), (1, CZ - 1)):
                s1[q, 1 + y, pl.ds(Z0 + z, 1), :] += value[j : j + 1, :]
            if cz:
                j, z = (2, -1) if cz < 0 else (3, CZ)
                value = jnp.where(z_ok[j - 2], value[j : j + 1, :], 0.0)
                s1[q, 1 + y, pl.ds(Z0 + z, 1), :] += value

    copies = [
        pltpu.make_async_copy(
            kept.at[:, pl.ds(2 * h, 2), :, :], out.at[:, pl.ds(6 * h, 2), :, :], out_sem.at[h]
        )
        for h in range(2)
    ]
    for k, y in enumerate(EDGE_ROWS):
        mixed = mix(weights, read_tiles(s1, y, OUTER))
        for q in range(Q):
            store_mixed(mixed, q, y, k, OUTER, kept, scaled)
        if k % 2:
            copies[k // 2].start()
    fetch.wait()

    @pl.loop(0, pick.shape[1], unroll=8)
    def _(d):
        for k in range(CAP // 2):
            places = pick[k, d]
            for j, at in ((k, places & (PAIR - 1)), (k + CAP // 2, places >> 13)):
                rows[pl.ds(d * (CAP + 1) + j, 1), 0, :] = scaled[pl.ds(at, 1), :]

    for copy in copies:
        copy.wait()


def sum_kernel(arrived, out):
    devices = arrived.shape[0] // (CAP + 1)
    numbers = arrived[pl.ds(CAP, devices, stride=CAP + 1), :].T
    panels = lax.broadcasted_iota(jnp.int32, (P_DEV, devices), 0).astype(f32)
    hot, rows = [], []
    for k in range(CAP):
        hot.append((numbers[k : k + 1, :] == panels).astype(f32).astype(bf16))
        rows.append(arrived[pl.ds(k, devices, stride=CAP + 1), :])
    hot = jnp.concatenate(hot, axis=1)
    high, low = split(jnp.concatenate(rows, axis=0))
    dot = functools.partial(jnp.dot, preferred_element_type=f32)
    out[...] = dot(hot, high) + dot(hot, low)


VMEM = pl.BlockSpec(memory_space=pltpu.VMEM)
HBM = pl.BlockSpec(memory_space=pltpu.HBM)
MIB = 1024 * 1024


def call(kernel, name, ins, outs, shapes, scratch=(), aliases=None, cost=None):
    return pl.pallas_call(
        kernel,
        out_shape=[jax.ShapeDtypeStruct(*s) for s in shapes],
        in_specs=ins,
        out_specs=outs,
        scratch_shapes=list(scratch),
        input_output_aliases=aliases or {},
        compiler_params=pltpu.CompilerParams(vmem_limit_bytes=32 * MIB),
        cost_estimate=cost
        and pl.CostEstimate(flops=cost, bytes_accessed=cost // 1000, transcendentals=cost // 1000),
        name=name,
    )


def pairings(gy, gz):
    def exchange(partner):
        found = []
        for y in range(gy):
            for z in range(gz):
                py, pz = partner(y, z)
                found.append((y * gz + z, py * gz + pz))
        return found

    def step(i, n):
        j = i - 1 if i % 2 == 0 else i + 1
        return j if 0 <= j < n else None

    def z_next(y, z):
        return (y ^ 1, z) if step(z, gz) is None else (y, step(z, gz))

    def y_next(y, z):
        return (y, z ^ 1) if step(y, gy) is None else (step(y, gy), z)

    return (
        exchange(lambda y, z: (y, z ^ 1)),
        exchange(z_next),
        exchange(lambda y, z: (y ^ 1, z)),
        exchange(y_next),
    )


def on_device(adjoint, collision, link_cell, link_dir, link_panel):
    gz = lax.axis_size("gz")
    gy = lax.axis_size("gy")
    devices = link_cell.shape[1]
    pad = (Q, CY + 2, ROWS, X)
    own = (Q, CY, CZ, X)
    flat = adjoint.reshape(Q, CY * CZ, X)
    dma = pltpu.SemaphoreType.DMA
    wide = ((K1, 3 * K1), f32)
    narrow = ((K1, 3 * K2), f32)
    w, w_up, w_down = call(
        weights_kernel, "weights", [VMEM], [VMEM] * 3, [wide, narrow, narrow], cost=4_000_000_000
    )(collision)
    to_pair, to_next, empty = call(
        pack_z_kernel, "pack_z", [VMEM] * 2, [VMEM] * 3, [((Z_ROWS, X), f32)] * 2 + [((8, X), f32)],
        cost=4_000_000_000,
    )(flat, w)
    both = ("gy", "gz")
    z_pairs, z_nexts, y_pairs, y_nexts = pairings(gy, gz)
    from_pair = lax.ppermute(to_pair, both, z_pairs)
    from_next = lax.ppermute(to_next, both, z_nexts)
    lines = ((Y_ROWS, X), f32)
    s0, s1, to_y_pair, to_y_next = call(
        bulk_rows_kernel, "bulk_rows", [VMEM] * 3, [VMEM] * 4,
        [(pad, f32), (pad, f32), lines, lines],
    )(flat, w, empty)
    from_y_pair = lax.ppermute(to_y_pair, both, y_pairs)
    from_y_next = lax.ppermute(to_y_next, both, y_nexts)
    s0, s1, to_y_pair, to_y_next = call(
        end_cells_kernel, "end_cells", [VMEM] * 5, [VMEM] * 4,
        [(pad, f32), (pad, f32), ((END_ROWS, X), f32), ((END_ROWS, X), f32)],
        scratch=[pltpu.VMEM((2, END_ROWS, X), f32), pltpu.VMEM((Q, 8, X), f32)],
        aliases={0: 0, 1: 1},
    )(s0, s1, w, from_pair, from_next)
    ends_pair = lax.ppermute(to_y_pair, both, y_pairs)
    ends_next = lax.ppermute(to_y_next, both, y_nexts)
    table = ((Q * CY * CZ, X), f32)
    message = ((devices * (CAP + 1), 1, X), f32)
    _, s1, out, scaled, rows, pick = call(
        inner_rows_kernel, "inner_rows", [VMEM] * 9, [VMEM] * 2 + [HBM] + [VMEM] * 3,
        [(pad, f32), (pad, f32), (own, f32), table]
        + [message, ((CAP // 2, devices), jnp.int32)],
        scratch=[
            pltpu.VMEM((Q, CY - 4, CZ, X), f32),
            pltpu.VMEM((2, K2, X), f32),
            pltpu.VMEM((devices, X), f32),
            dma,
        ],
        cost=4_000_000_000,
        aliases={0: 0, 2: 1},
    )(s0, w, s1, w_up, w_down, flat, link_panel[0].T, link_cell[0].T, link_dir[0].T)
    edge = ((Q, 4, CZ, X), f32)
    lines = ((2, 5, ROWS, X), f32)
    s1, scaled, raw, kept = call(
        middle_tiles_kernel, "middle_tiles", [VMEM] * 7, [VMEM] * 4,
        [(pad, f32), table, lines, edge],
        aliases={0: 0, 6: 1},
        cost=1_000_000_000,
    )(s1, w, w_up, w_down, from_y_pair, from_y_next, scaled)
    _, _, _, _, rows, out = call(
        outer_tiles_kernel, "outer_tiles", [VMEM] * 11 + [HBM], [VMEM] * 5 + [HBM],
        [(pad, f32), table, lines, edge, message, (own, f32)],
        scratch=[
            pltpu.VMEM((2, K2, X), f32),
            pltpu.SMEM((CAP // 2, devices), jnp.int32),
            dma,
            dma((2,)),
        ],
        aliases={0: 0, 7: 1, 8: 2, 9: 3, 10: 4, 11: 5},
    )(s1, w, w_up, w_down, ends_pair, ends_next, pick, scaled, raw, kept, rows, out)
    arrived = lax.all_to_all(
        rows.reshape(devices, CAP + 1, 1, X), ("gy", "gz"), split_axis=0, concat_axis=0, tiled=True
    )
    (panel_sens,) = call(sum_kernel, "sum_rows", [VMEM], [VMEM], [((P_DEV, X), f32)])(
        arrived.reshape(devices * (CAP + 1), X)
    )
    return out, panel_sens


def solution(mesh):
    placed = (
        P(None, "gy", "gz", None),
        P(),
        P(("gy", "gz"), None, None),
        P(("gy", "gz"), None, None),
        P(("gy", "gz"), None, None),
    )
    return jax.shard_map(
        on_device,
        mesh=mesh,
        in_specs=placed,
        out_specs=(P(None, "gy", "gz", None), P(("gy", "gz"), None)),
        check_vma=False,
    )
```

```python
import functools

import jax
import jax.numpy as jnp
from jax import lax
from jax.experimental import pallas as pl
from jax.experimental.pallas import tpu as pltpu
from jax.sharding import PartitionSpec as P

Q = 19
QP = 20
P_DEV = 64
CAP = 8
CY = 8
CZ = 32
X = 128
ROWS = 48
Z0 = 8

DIRS = [
    (0, 0, 0),
    (1, 0, 0),
    (-1, 0, 0),
    (0, 1, 0),
    (0, -1, 0),
    (0, 0, 1),
    (0, 0, -1),
    (1, 1, 0),
    (-1, -1, 0),
    (1, -1, 0),
    (-1, 1, 0),
    (1, 0, 1),
    (-1, 0, -1),
    (1, 0, -1),
    (-1, 0, 1),
    (0, 1, 1),
    (0, -1, -1),
    (0, 1, -1),
    (0, -1, 1),
]
LINK_WEIGHTS = [2.0] + [1.0 / 3.0] * 6 + [1.0 / 6.0] * 12

Y_UP = [q for q in range(Q) if DIRS[q][1] == 1]
Y_DOWN = [q for q in range(Q) if DIRS[q][1] == -1]
Z_UP = [q for q in range(Q) if DIRS[q][2] == 1]
Z_DOWN = [q for q in range(Q) if DIRS[q][2] == -1]
Z_FLAT = [q for q in range(Q) if DIRS[q][2] == 0]
SEND_LOW = [(q, 0) for q in Z_FLAT] + [(q, 0) for q in Z_UP] + [(q, 1) for q in Z_UP]
SEND_HIGH = [(q, 0) for q in Z_FLAT] + [(q, 0) for q in Z_DOWN] + [(q, 1) for q in Z_DOWN]

RAW = 0
MIXED = 5 * CZ
Y_ROWS = 10 * CZ
RAW_ENDS = 0
MIXED_ENDS = 10
CORNERS = 20
END_ROWS = 24
Z_ROWS = 8 * Q
PAIR = 1 << 13
K1 = QP * 8
K2 = 6 * 8

f32 = jnp.float32
bf16 = jnp.bfloat16


def along_x(value, q):
    cx = DIRS[q][0]
    if cx == 0:
        return value
    return pltpu.roll(value, (-cx) % X, value.ndim - 1)


def split(value):
    high = value.astype(bf16)
    return high, (value - high.astype(f32)).astype(bf16)


def mix(weights, reads):
    high, low = split(reads)
    return jnp.dot(
        weights, jnp.concatenate([high, low, high], axis=0), preferred_element_type=f32
    )


def stacked(tiles):
    count = max(len(t) for t in tiles if t is not None)
    zero = jnp.zeros((8, X), f32)
    full = [t if t is not None else [zero] * count for t in tiles]
    return jnp.concatenate(
        [jnp.concatenate([t[c] for t in full], axis=0) for c in range(count)], axis=1
    )


def line_tiles(line):
    return [line[8 * t : 8 * t + 8, :] for t in range(CZ // 8)]


def read_line(ref, p, y, shift=0):
    cx, cy, cz = DIRS[p]
    return ref[p, y + 1 + cy, pl.ds(Z0 + cz + shift, CZ), :]


def read_row(ref, y):
    return stacked([line_tiles(read_line(ref, p, y)) for p in range(Q)] + [None])


def load_column(ref, q, y, z):
    flat = ref.reshape(Q, (CY + 2) * ROWS, X)
    return flat[q, pl.ds((1 + y) * ROWS + Z0 + z, CY, stride=ROWS), :]


def store_column(ref, q, y, z, value):
    flat = ref.reshape(Q, (CY + 2) * ROWS, X)
    flat[q, pl.ds((1 + y) * ROWS + Z0 + z, CY, stride=ROWS), :] = value


def pack_z_kernel(field, w, to_pair, to_next, empty):
    del w
    empty[...] = jnp.zeros((8, X), f32)
    even = lax.rem(lax.axis_index("gz"), 2) == 0
    for i in range(Q):
        q, d = SEND_LOW[i]
        low = field[q, pl.ds(d, CY, stride=CZ), :]
        q, d = SEND_HIGH[i]
        high = field[q, pl.ds(CZ - 1 - d, CY, stride=CZ), :]
        to_pair[8 * i : 8 * i + 8, :] = jnp.where(even, high, low)
        to_next[8 * i : 8 * i + 8, :] = jnp.where(even, low, high)


def own_channel(shape, axis, channels):
    place = lax.broadcasted_iota(jnp.int32, shape, axis) // 8
    channel = lax.broadcasted_iota(jnp.int32, shape, 1 - axis)
    hit = jnp.zeros(shape, f32)
    for i, q in enumerate(channels):
        hit = jnp.where(jnp.logical_and(place == i, channel == q), 1.0, hit)
    return hit.astype(bf16)


def spread_weights(collision, channels, width):
    rows = (
        lax.broadcasted_iota(jnp.int32, (K1, Q), 0) // 8
        == lax.broadcasted_iota(jnp.int32, (K1, Q), 1)
    ).astype(f32).astype(bf16)
    columns = own_channel((width, Q), 0, channels)
    same = (
        lax.broadcasted_iota(jnp.int32, (K1, width), 0) % 8
        == lax.broadcasted_iota(jnp.int32, (K1, width), 1) % 8
    )
    dims = (((1,), (1,)), ((), ()))
    parts = []
    for part in split(collision):
        turned = lax.dot_general(rows, part, dims, preferred_element_type=f32).astype(bf16)
        wide = lax.dot_general(turned, columns, dims, preferred_element_type=f32)
        parts.append(jnp.where(same, wide, 0.0))
    return jnp.concatenate([parts[0], parts[0], parts[1]], axis=1)


def weights_kernel(collision, w, w_up, w_down):
    w[...] = spread_weights(collision[...], range(Q), K1)
    w_up[...] = spread_weights(collision[...], Y_UP, K2)
    w_down[...] = spread_weights(collision[...], Y_DOWN, K2)


EDGE_ROWS = (0, 1, CY - 2, CY - 1)


def bulk_rows_kernel(field, w, empty, s0, s1, to_pair, to_next):
    nothing = empty[...]
    for q in range(Q):
        for y in EDGE_ROWS:
            s0[q, 1 + y, Z0 : Z0 + CZ, :] = along_x(field[q, CZ * y : CZ * y + CZ, :], q)
    for q in Y_DOWN + Y_UP:
        for t in range(ROWS // 8):
            s0[q, 0 if DIRS[q][1] < 0 else CY + 1, 8 * t : 8 * t + 8, :] = nothing
    for q in range(Q):
        if DIRS[q][2]:
            for y in EDGE_ROWS:
                s0[q, 1 + y, 0:Z0, :] = nothing
                s0[q, 1 + y, Z0 + CZ : ROWS, :] = nothing
    weights = w[...].astype(bf16)
    for y in (0, CY - 1):
        store_line(s1, y, mix(weights, read_row(s0, y)))
    even = lax.rem(lax.axis_index("gy"), 2) == 0
    for ref, base in ((s0, RAW), (s1, MIXED)):
        for i in range(5):
            low = ref[Y_UP[i], 1, Z0 : Z0 + CZ, :]
            high = ref[Y_DOWN[i], CY, Z0 : Z0 + CZ, :]
            at = base + CZ * i
            to_pair[at : at + CZ, :] = jnp.where(even, high, low)
            to_next[at : at + CZ, :] = jnp.where(even, low, high)


def end_cells_kernel(
    s0_in, s1_in, w, from_pair, from_next, s0, s1, to_pair, to_next, both, corner
):
    del s0_in, s1_in
    iz = lax.axis_index("gz")
    even = lax.rem(iz, 2) == 0
    above = iz < lax.axis_size("gz") - 1
    below = iz > 0
    for i in range(Q):
        pair = from_pair[8 * i : 8 * i + 8, :]
        following = from_next[8 * i : 8 * i + 8, :]
        q, d = SEND_LOW[i]
        value = jnp.where(above, jnp.where(even, pair, following), 0.0)
        store_column(s0, q, 0, CZ + d, along_x(value, q))
        q, d = SEND_HIGH[i]
        value = jnp.where(below, jnp.where(even, following, pair), 0.0)
        store_column(s0, q, 0, -1 - d, along_x(value, q))
    last = CZ // 8 - 1
    spots = [(y, t) for y in (0, CY - 1) for t in (0, last)]
    corners = [(y, z) for y in (0, CY - 1) for z in (-1, CZ)]
    corner[...] = jnp.zeros((Q, 8, X), f32)
    tiles = []
    for p in range(Q):
        cx, cy, cz = DIRS[p]
        for c, (y, z) in enumerate(corners):
            corner[p, pl.ds(c, 1), :] = s0[p, y + 1 + cy, pl.ds(Z0 + z + cz, 1), :]
        tiles.append(
            [s0[p, y + 1 + cy, pl.ds(Z0 + 8 * t + cz, 8), :] for y, t in spots] + [corner[p]]
        )
    mixed = mix(w[...].astype(bf16), stacked(tiles + [None]))
    for q in range(Q):
        for c, (y, t) in enumerate(spots):
            s1[q, 1 + y, Z0 + 8 * t : Z0 + 8 * t + 8, :] = along_x(
                mixed[8 * q : 8 * q + 8, X * c : X * c + X], q
            )
        if DIRS[q][2]:
            ends = along_x(mixed[8 * q : 8 * q + 8, X * 4 :], q)
            for c, (y, z) in enumerate(corners):
                if DIRS[q][2] == (1 if z > 0 else -1):
                    value = jnp.where(above if z > 0 else below, ends[c : c + 1, :], 0.0)
                    s1[q, 1 + y, pl.ds(Z0 + z, 1), :] = value
    for side, (y, channels) in enumerate(((0, Y_UP), (CY - 1, Y_DOWN))):
        message = both.at[side]
        message[16:END_ROWS, :] = jnp.zeros((8, X), f32)
        for i, q in enumerate(channels):
            cz = DIRS[q][2]
            for e, z in enumerate(RAW_CELLS[cz]):
                message[pl.ds(RAW_ENDS + 2 * i + e, 1), :] = s0[q, 1 + y, pl.ds(Z0 + z, 1), :]
            for e, z in enumerate((0, CZ - 1)):
                message[pl.ds(MIXED_ENDS + 2 * i + e, 1), :] = s1[q, 1 + y, pl.ds(Z0 + z, 1), :]
            if cz:
                z, e = (CZ, 0) if cz > 0 else (-1, 1)
                message[pl.ds(CORNERS + e, 1), :] = s1[q, 1 + y, pl.ds(Z0 + z, 1), :]
    even_y = lax.rem(lax.axis_index("gy"), 2) == 0
    to_pair[...] = jnp.where(even_y, both[1], both[0])
    to_next[...] = jnp.where(even_y, both[0], both[1])


RAW_CELLS = {0: (-1, CZ), 1: (CZ, CZ + 1), -1: (-2, -1)}


def store_line(s1, y, out):
    for q in range(Q):
        for t in range(CZ // 8):
            s1[q, 1 + y, Z0 + 8 * t : Z0 + 8 * t + 8, :] = along_x(
                out[8 * q : 8 * q + 8, X * t : X * t + X], q
            )


def five_lines(ref, spare, lead, channels):
    tiles = []
    for i, p in enumerate(channels):
        cz = DIRS[p][2]
        line = ref[lead(i, p) + (pl.ds(Z0 + cz, CZ), slice(None))]
        for e, z in enumerate((-1, CZ)):
            spare[pl.ds(8 * i + e, 1), :] = ref[lead(i, p) + (pl.ds(Z0 + z + cz, 1), slice(None))]
        tiles.append(line_tiles(line) + [spare[8 * i : 8 * i + 8, :]])
    return stacked(tiles + [None])


def inner_rows_kernel(
    s0_in, w, s1_in, w_up, w_down, field, panel, cell, direction,
    s0, s1, out, scaled, rows, pick, kept, spare, numbers, sem,
):
    del s0_in, s1_in
    iy = lax.axis_index("gy")
    iz = lax.axis_index("gz")
    above = iz < lax.axis_size("gz") - 1
    below = iz > 0
    weights = w[...].astype(bf16)
    for y in range(2, CY - 2):
        for q in range(Q):
            s0[q, 1 + y, Z0 : Z0 + CZ, :] = along_x(field[q, CZ * y : CZ * y + CZ, :], q)
    reads = stacked(
        [
            [load_column(s0, p, DIRS[p][1], z + DIRS[p][2]) for z in (-1, CZ)]
            for p in range(Q)
        ]
        + [None]
    )
    mixed = mix(weights, reads)
    for c, (z, channels, valid) in enumerate(((-1, Z_DOWN, below), (CZ, Z_UP, above))):
        for q in channels:
            value = along_x(mixed[8 * q : 8 * q + 8, X * c : X * c + X], q)
            store_column(s1, q, 0, z, jnp.where(valid, value, 0.0))
    for y in range(1, CY - 1):
        store_line(s1, y, mix(weights, read_row(s0, y)))
    for y in range(2, CY - 2):
        mixed = mix(weights, read_row(s1, y))
        for q in range(Q):
            for t in range(CZ // 8):
                value = mixed[8 * q : 8 * q + 8, X * t : X * t + X]
                kept[q, y - 2, 8 * t : 8 * t + 8, :] = value
                at = q * (CY * CZ) + y * CZ + 8 * t
                scaled[at : at + 8, :] = value * LINK_WEIGHTS[q]
    copy = pltpu.make_async_copy(kept, out.at[:, pl.ds(2, CY - 4), :, :], sem)
    copy.start()
    numbers[...] = jnp.zeros((numbers.shape[0], X), f32)
    numbers[:, 0:CAP] = panel[...].astype(f32).T
    place = direction[...] * (CY * CZ) + cell[...]
    pick[...] = place[: CAP // 2] + place[CAP // 2 :] * PAIR

    @pl.loop(0, numbers.shape[0], unroll=8)
    def _(d):
        rows[pl.ds(d * (CAP + 1) + CAP, 1), 0, :] = numbers[pl.ds(d, 1), :]

    spare[...] = jnp.zeros((2, K2, X), f32)
    sides = (
        (0, CY - 1, CY, Y_UP, Y_DOWN, w_down, iy < lax.axis_size("gy") - 1),
        (1, 0, -1, Y_DOWN, Y_UP, w_up, iy > 0),
    )
    for side, y, halo, channels, sources, part, valid in sides:
        rows = [part[8 * q : 8 * q + 8, :] for q in channels]
        rows = jnp.concatenate(rows + [jnp.zeros_like(rows[0])], axis=0).astype(bf16)
        reads = five_lines(s0, spare.at[side], lambda i, p: (p, 1 + y), sources)
        mixed = jnp.where(valid, mix(rows, reads), 0.0)
        for i, q in enumerate(channels):
            for t in range(CZ // 8):
                s1[q, 1 + halo, Z0 + 8 * t : Z0 + 8 * t + 8, :] = along_x(
                    mixed[8 * i : 8 * i + 8, X * t : X * t + X], q
                )
            cz = DIRS[q][2]
            if cz:
                z, row, ok = (-1, 0, below) if cz < 0 else (CZ, 1, above)
                end = along_x(mixed[8 * i : 8 * i + 8, X * (CZ // 8) :], q)[row : row + 1, :]
                s1[q, 1 + halo, pl.ds(Z0 + z, 1), :] = jnp.where(ok, end, 0.0)
    copy.wait()


def outer_rows_kernel(
    s1_in, w, w_up, w_down, from_next, from_pair, ends_next, ends_pair, pick_in, scaled_in,
    rows_in, out_in,
    s1, scaled, rows, out, kept, raw, spare, pick, pick_sem, out_sem,
):
    del s1_in, scaled_in, rows_in, out_in
    fetch = pltpu.make_async_copy(pick_in, pick, pick_sem)
    fetch.start()
    iy = lax.axis_index("gy")
    iz = lax.axis_index("gz")
    weights = w[...].astype(bf16)
    z_ok = (iz > 0, iz < lax.axis_size("gz") - 1)
    first = lax.broadcasted_iota(jnp.int32, (8, X), 0) == 0
    final = lax.broadcasted_iota(jnp.int32, (8, X), 0) == 7
    spare[...] = jnp.zeros((2, K2, X), f32)
    sides = (
        (0, CY - 1, CY, Y_UP, w_up, iy < lax.axis_size("gy") - 1),
        (1, 0, -1, Y_DOWN, w_down, iy > 0),
    )

    def take(side, bulk, ends):
        _, _, halo, channels, _, _ = sides[side]
        for i, q in enumerate(channels):
            cz = DIRS[q][2]
            raw[side, i, Z0 : Z0 + CZ, :] = bulk[RAW + CZ * i : RAW + CZ * i + CZ, :]
            for e, z in enumerate(RAW_CELLS[cz]):
                raw[side, i, pl.ds(Z0 + z, 1), :] = ends[pl.ds(RAW_ENDS + 2 * i + e, 1), :]
            for t in range(CZ // 8):
                value = bulk[MIXED + CZ * i + 8 * t : MIXED + CZ * i + 8 * t + 8, :]
                at = MIXED_ENDS + 2 * i
                if t == 0:
                    value = jnp.where(first, ends[at : at + 1, :], value)
                if t == CZ // 8 - 1:
                    value = jnp.where(final, ends[at + 1 : at + 2, :], value)
                s1[q, 1 + halo, Z0 + 8 * t : Z0 + 8 * t + 8, :] += value
            if cz:
                z, e = (CZ, 0) if cz > 0 else (-1, 1)
                s1[q, 1 + halo, pl.ds(Z0 + z, 1), :] += ends[CORNERS + e : CORNERS + e + 1, :]

    odd = lax.rem(iy, 2)
    for side, (_, _, _, _, _, valid) in enumerate(sides):
        pl.when(jnp.logical_and(valid, odd == side))(
            functools.partial(take, side, from_pair, ends_pair)
        )
        pl.when(jnp.logical_and(valid, odd != side))(
            functools.partial(take, side, from_next, ends_next)
        )

        @pl.when(jnp.logical_not(valid))
        def _(side=side):
            raw[side] = jnp.zeros((5, ROWS, X), f32)

    for side, y, halo, channels, part, valid in sides:
        reads = five_lines(raw.at[side], spare.at[side], lambda i, p: (i,), channels)
        mixed = mix(part[...].astype(bf16), reads)
        for q in range(Q):
            for t in range(CZ // 8):
                at = pl.ds(Z0 + 8 * t, 8)
                s1[q, 1 + y, at, :] += along_x(mixed[8 * q : 8 * q + 8, X * t : X * t + X], q)
            cz = DIRS[q][2]
            if cz:
                row = 0 if cz < 0 else 1
                end = along_x(mixed[8 * q : 8 * q + 8, X * (CZ // 8) :], q)[row : row + 1, :]
                at = pl.ds(Z0 - 1 if cz < 0 else Z0 + CZ, 1)
                s1[q, 1 + y, at, :] += jnp.where(z_ok[row], end, 0.0)

    copies = [
        pltpu.make_async_copy(
            kept.at[:, pl.ds(2 * h, 2), :, :], out.at[:, pl.ds(6 * h, 2), :, :], out_sem.at[h]
        )
        for h in range(2)
    ]
    for k, y in enumerate((0, 1, CY - 2, CY - 1)):
        mixed = mix(weights, read_row(s1, y))
        for q in range(Q):
            for t in range(CZ // 8):
                value = mixed[8 * q : 8 * q + 8, X * t : X * t + X]
                kept[q, k, 8 * t : 8 * t + 8, :] = value
                at = q * (CY * CZ) + y * CZ + 8 * t
                scaled[at : at + 8, :] = value * LINK_WEIGHTS[q]
        if k % 2:
            copies[k // 2].start()
    fetch.wait()

    @pl.loop(0, pick.shape[1], unroll=8)
    def _(d):
        for k in range(CAP // 2):
            places = pick[k, d]
            for j, at in ((k, places & (PAIR - 1)), (k + CAP // 2, places >> 13)):
                rows[pl.ds(d * (CAP + 1) + j, 1), 0, :] = scaled[pl.ds(at, 1), :]

    for copy in copies:
        copy.wait()


def sum_kernel(arrived, out):
    devices = arrived.shape[0] // (CAP + 1)
    numbers = arrived[pl.ds(CAP, devices, stride=CAP + 1), :].T
    panels = lax.broadcasted_iota(jnp.int32, (P_DEV, devices), 0).astype(f32)
    hot, rows = [], []
    for k in range(CAP):
        hot.append((numbers[k : k + 1, :] == panels).astype(f32).astype(bf16))
        rows.append(arrived[pl.ds(k, devices, stride=CAP + 1), :])
    hot = jnp.concatenate(hot, axis=1)
    high, low = split(jnp.concatenate(rows, axis=0))
    dot = functools.partial(jnp.dot, preferred_element_type=f32)
    out[...] = dot(hot, high) + dot(hot, low)


VMEM = pl.BlockSpec(memory_space=pltpu.VMEM)
HBM = pl.BlockSpec(memory_space=pltpu.HBM)
MIB = 1024 * 1024


def call(kernel, name, ins, outs, shapes, scratch=(), aliases=None, cost=None):
    return pl.pallas_call(
        kernel,
        out_shape=[jax.ShapeDtypeStruct(*s) for s in shapes],
        in_specs=ins,
        out_specs=outs,
        scratch_shapes=list(scratch),
        input_output_aliases=aliases or {},
        compiler_params=pltpu.CompilerParams(vmem_limit_bytes=32 * MIB),
        cost_estimate=cost
        and pl.CostEstimate(flops=cost, bytes_accessed=cost // 1000, transcendentals=cost // 1000),
        name=name,
    )


def pairings(gy, gz):
    def exchange(partner):
        found = []
        for y in range(gy):
            for z in range(gz):
                py, pz = partner(y, z)
                found.append((y * gz + z, py * gz + pz))
        return found

    def step(i, n):
        j = i - 1 if i % 2 == 0 else i + 1
        return j if 0 <= j < n else None

    def z_next(y, z):
        return (y ^ 1, z) if step(z, gz) is None else (y, step(z, gz))

    def y_next(y, z):
        return (y, z ^ 1) if step(y, gy) is None else (step(y, gy), z)

    return (
        exchange(lambda y, z: (y, z ^ 1)),
        exchange(z_next),
        exchange(lambda y, z: (y ^ 1, z)),
        exchange(y_next),
    )


def on_device(adjoint, collision, link_cell, link_dir, link_panel):
    gz = lax.axis_size("gz")
    gy = lax.axis_size("gy")
    devices = link_cell.shape[1]
    pad = (Q, CY + 2, ROWS, X)
    own = (Q, CY, CZ, X)
    flat = adjoint.reshape(Q, CY * CZ, X)
    dma = pltpu.SemaphoreType.DMA
    wide = ((K1, 3 * K1), f32)
    narrow = ((K1, 3 * K2), f32)
    w, w_up, w_down = call(
        weights_kernel, "weights", [VMEM], [VMEM] * 3, [wide, narrow, narrow], cost=4_000_000_000
    )(collision)
    to_pair, to_next, empty = call(
        pack_z_kernel, "pack_z", [VMEM] * 2, [VMEM] * 3, [((Z_ROWS, X), f32)] * 2 + [((8, X), f32)],
        cost=4_000_000_000,
    )(flat, w)
    both = ("gy", "gz")
    z_pairs, z_nexts, y_pairs, y_nexts = pairings(gy, gz)
    from_pair = lax.ppermute(to_pair, both, z_pairs)
    from_next = lax.ppermute(to_next, both, z_nexts)
    lines = ((Y_ROWS, X), f32)
    s0, s1, to_y_pair, to_y_next = call(
        bulk_rows_kernel, "bulk_rows", [VMEM] * 3, [VMEM] * 4,
        [(pad, f32), (pad, f32), lines, lines],
    )(flat, w, empty)
    from_y_pair = lax.ppermute(to_y_pair, both, y_pairs)
    from_y_next = lax.ppermute(to_y_next, both, y_nexts)
    s0, s1, to_y_pair, to_y_next = call(
        end_cells_kernel, "end_cells", [VMEM] * 5, [VMEM] * 4,
        [(pad, f32), (pad, f32), ((END_ROWS, X), f32), ((END_ROWS, X), f32)],
        scratch=[pltpu.VMEM((2, END_ROWS, X), f32), pltpu.VMEM((Q, 8, X), f32)],
        aliases={0: 0, 1: 1},
    )(s0, s1, w, from_pair, from_next)
    ends_pair = lax.ppermute(to_y_pair, both, y_pairs)
    ends_next = lax.ppermute(to_y_next, both, y_nexts)
    table = ((Q * CY * CZ, X), f32)
    message = ((devices * (CAP + 1), 1, X), f32)
    _, s1, out, scaled, rows, pick = call(
        inner_rows_kernel, "inner_rows", [VMEM] * 9, [VMEM] * 2 + [HBM] + [VMEM] * 3,
        [(pad, f32), (pad, f32), (own, f32), table]
        + [message, ((CAP // 2, devices), jnp.int32)],
        scratch=[
            pltpu.VMEM((Q, CY - 4, CZ, X), f32),
            pltpu.VMEM((2, K2, X), f32),
            pltpu.VMEM((devices, X), f32),
            dma,
        ],
        cost=4_000_000_000,
        aliases={0: 0, 2: 1},
    )(s0, w, s1, w_up, w_down, flat, link_panel[0].T, link_cell[0].T, link_dir[0].T)
    _, _, rows, out = call(
        outer_rows_kernel, "outer_rows", [VMEM] * 11 + [HBM], [VMEM] * 3 + [HBM],
        [(pad, f32), table, message, (own, f32)],
        scratch=[
            pltpu.VMEM((Q, 4, CZ, X), f32),
            pltpu.VMEM((2, 5, ROWS, X), f32),
            pltpu.VMEM((2, K2, X), f32),
            pltpu.SMEM((CAP // 2, devices), jnp.int32),
            dma,
            dma((2,)),
        ],
        aliases={0: 0, 9: 1, 10: 2, 11: 3},
    )(s1, w, w_up, w_down, from_y_next, from_y_pair, ends_next, ends_pair, pick, scaled, rows, out)
    arrived = lax.all_to_all(
        rows.reshape(devices, CAP + 1, 1, X), ("gy", "gz"), split_axis=0, concat_axis=0, tiled=True
    )
    (panel_sens,) = call(sum_kernel, "sum_rows", [VMEM], [VMEM], [((P_DEV, X), f32)])(
        arrived.reshape(devices * (CAP + 1), X)
    )
    return out, panel_sens


def solution(mesh):
    placed = (
        P(None, "gy", "gz", None),
        P(),
        P(("gy", "gz"), None, None),
        P(("gy", "gz"), None, None),
        P(("gy", "gz"), None, None),
    )
    return jax.shard_map(
        on_device,
        mesh=mesh,
        in_specs=placed,
        out_specs=(P(None, "gy", "gz", None), P(("gy", "gz"), None)),
        check_vma=False,
    )
```

```python
import functools

import jax
import jax.numpy as jnp
from jax import lax
from jax.experimental import pallas as pl
from jax.experimental.pallas import tpu as pltpu
from jax.sharding import PartitionSpec as P

Q = 19
QP = 20
P_DEV = 64
CAP = 8
CY = 8
CZ = 32
X = 128
ROWS = 48
Z0 = 8

DIRS = [
    (0, 0, 0),
    (1, 0, 0),
    (-1, 0, 0),
    (0, 1, 0),
    (0, -1, 0),
    (0, 0, 1),
    (0, 0, -1),
    (1, 1, 0),
    (-1, -1, 0),
    (1, -1, 0),
    (-1, 1, 0),
    (1, 0, 1),
    (-1, 0, -1),
    (1, 0, -1),
    (-1, 0, 1),
    (0, 1, 1),
    (0, -1, -1),
    (0, 1, -1),
    (0, -1, 1),
]
LINK_WEIGHTS = [2.0] + [1.0 / 3.0] * 6 + [1.0 / 6.0] * 12

Y_UP = [q for q in range(Q) if DIRS[q][1] == 1]
Y_DOWN = [q for q in range(Q) if DIRS[q][1] == -1]
Z_UP = [q for q in range(Q) if DIRS[q][2] == 1]
Z_DOWN = [q for q in range(Q) if DIRS[q][2] == -1]
Z_FLAT = [q for q in range(Q) if DIRS[q][2] == 0]
SEND_LOW = [(q, 0) for q in Z_FLAT] + [(q, 0) for q in Z_UP] + [(q, 1) for q in Z_UP]
SEND_HIGH = [(q, 0) for q in Z_FLAT] + [(q, 0) for q in Z_DOWN] + [(q, 1) for q in Z_DOWN]

RAW = 0
MIXED = 5 * CZ
Y_ROWS = 10 * CZ
RAW_ENDS = 0
MIXED_ENDS = 10
CORNERS = 20
END_ROWS = 24
Z_ROWS = 8 * Q
PAIR = 1 << 13
K1 = QP * 8
K2 = 6 * 8

f32 = jnp.float32
bf16 = jnp.bfloat16


def along_x(value, q):
    cx = DIRS[q][0]
    if cx == 0:
        return value
    return pltpu.roll(value, (-cx) % X, value.ndim - 1)


def split(value):
    high = value.astype(bf16)
    return high, (value - high.astype(f32)).astype(bf16)


def mix(weights, reads):
    high, low = split(reads)
    return jnp.dot(
        weights, jnp.concatenate([high, low, high], axis=0), preferred_element_type=f32
    )


def stacked(tiles):
    count = max(len(t) for t in tiles if t is not None)
    zero = jnp.zeros((8, X), f32)
    full = [t if t is not None else [zero] * count for t in tiles]
    return jnp.concatenate(
        [jnp.concatenate([t[c] for t in full], axis=0) for c in range(count)], axis=1
    )


def line_tiles(line):
    return [line[8 * t : 8 * t + 8, :] for t in range(CZ // 8)]


def read_line(ref, p, y, shift=0):
    cx, cy, cz = DIRS[p]
    return ref[p, y + 1 + cy, pl.ds(Z0 + cz + shift, CZ), :]


def read_row(ref, y):
    return stacked([line_tiles(read_line(ref, p, y)) for p in range(Q)] + [None])


def load_column(ref, q, y, z):
    flat = ref.reshape(Q, (CY + 2) * ROWS, X)
    return flat[q, pl.ds((1 + y) * ROWS + Z0 + z, CY, stride=ROWS), :]


def store_column(ref, q, y, z, value):
    flat = ref.reshape(Q, (CY + 2) * ROWS, X)
    flat[q, pl.ds((1 + y) * ROWS + Z0 + z, CY, stride=ROWS), :] = value


def pack_z_kernel(field, w, to_pair, to_next, empty):
    del w
    empty[...] = jnp.zeros((8, X), f32)
    even = lax.rem(lax.axis_index("gz"), 2) == 0
    for i in range(Q):
        q, d = SEND_LOW[i]
        low = field[q, pl.ds(d, CY, stride=CZ), :]
        q, d = SEND_HIGH[i]
        high = field[q, pl.ds(CZ - 1 - d, CY, stride=CZ), :]
        to_pair[8 * i : 8 * i + 8, :] = jnp.where(even, high, low)
        to_next[8 * i : 8 * i + 8, :] = jnp.where(even, low, high)


def own_channel(shape, axis, channels):
    place = lax.broadcasted_iota(jnp.int32, shape, axis) // 8
    channel = lax.broadcasted_iota(jnp.int32, shape, 1 - axis)
    hit = jnp.zeros(shape, f32)
    for i, q in enumerate(channels):
        hit = jnp.where(jnp.logical_and(place == i, channel == q), 1.0, hit)
    return hit.astype(bf16)


def spread_weights(collision, channels, width):
    rows = (
        lax.broadcasted_iota(jnp.int32, (K1, Q), 0) // 8
        == lax.broadcasted_iota(jnp.int32, (K1, Q), 1)
    ).astype(f32).astype(bf16)
    columns = own_channel((width, Q), 0, channels)
    same = (
        lax.broadcasted_iota(jnp.int32, (K1, width), 0) % 8
        == lax.broadcasted_iota(jnp.int32, (K1, width), 1) % 8
    )
    dims = (((1,), (1,)), ((), ()))
    parts = []
    for part in split(collision):
        turned = lax.dot_general(rows, part, dims, preferred_element_type=f32).astype(bf16)
        wide = lax.dot_general(turned, columns, dims, preferred_element_type=f32)
        parts.append(jnp.where(same, wide, 0.0))
    return jnp.concatenate([parts[0], parts[0], parts[1]], axis=1)


def weights_kernel(collision, w, w_up, w_down):
    w[...] = spread_weights(collision[...], range(Q), K1)
    w_up[...] = spread_weights(collision[...], Y_UP, K2)
    w_down[...] = spread_weights(collision[...], Y_DOWN, K2)


EDGE_ROWS = (0, 1, CY - 2, CY - 1)


def bulk_rows_kernel(field, w, empty, s0, s1, to_pair, to_next):
    nothing = empty[...]
    for q in range(Q):
        for y in EDGE_ROWS:
            s0[q, 1 + y, Z0 : Z0 + CZ, :] = along_x(field[q, CZ * y : CZ * y + CZ, :], q)
    for q in Y_DOWN + Y_UP:
        for t in range(ROWS // 8):
            s0[q, 0 if DIRS[q][1] < 0 else CY + 1, 8 * t : 8 * t + 8, :] = nothing
    for q in range(Q):
        if DIRS[q][2]:
            for y in EDGE_ROWS:
                s0[q, 1 + y, 0:Z0, :] = nothing
                s0[q, 1 + y, Z0 + CZ : ROWS, :] = nothing
    weights = w[...].astype(bf16)
    for y in (0, CY - 1):
        store_line(s1, y, mix(weights, read_row(s0, y)))
    even = lax.rem(lax.axis_index("gy"), 2) == 0
    for ref, base in ((s0, RAW), (s1, MIXED)):
        for i in range(5):
            low = ref[Y_UP[i], 1, Z0 : Z0 + CZ, :]
            high = ref[Y_DOWN[i], CY, Z0 : Z0 + CZ, :]
            at = base + CZ * i
            to_pair[at : at + CZ, :] = jnp.where(even, high, low)
            to_next[at : at + CZ, :] = jnp.where(even, low, high)


def end_cells_kernel(
    s0_in, s1_in, w, from_pair, from_next, s0, s1, to_pair, to_next, both, corner
):
    del s0_in, s1_in
    iz = lax.axis_index("gz")
    even = lax.rem(iz, 2) == 0
    above = iz < lax.axis_size("gz") - 1
    below = iz > 0
    for i in range(Q):
        pair = from_pair[8 * i : 8 * i + 8, :]
        following = from_next[8 * i : 8 * i + 8, :]
        q, d = SEND_LOW[i]
        value = jnp.where(above, jnp.where(even, pair, following), 0.0)
        store_column(s0, q, 0, CZ + d, along_x(value, q))
        q, d = SEND_HIGH[i]
        value = jnp.where(below, jnp.where(even, following, pair), 0.0)
        store_column(s0, q, 0, -1 - d, along_x(value, q))
    last = CZ // 8 - 1
    spots = [(y, t) for y in (0, CY - 1) for t in (0, last)]
    corners = [(y, z) for y in (0, CY - 1) for z in (-1, CZ)]
    corner[...] = jnp.zeros((Q, 8, X), f32)
    tiles = []
    for p in range(Q):
        cx, cy, cz = DIRS[p]
        for c, (y, z) in enumerate(corners):
            corner[p, pl.ds(c, 1), :] = s0[p, y + 1 + cy, pl.ds(Z0 + z + cz, 1), :]
        tiles.append(
            [s0[p, y + 1 + cy, pl.ds(Z0 + 8 * t + cz, 8), :] for y, t in spots] + [corner[p]]
        )
    mixed = mix(w[...].astype(bf16), stacked(tiles + [None]))
    for q in range(Q):
        for c, (y, t) in enumerate(spots):
            s1[q, 1 + y, Z0 + 8 * t : Z0 + 8 * t + 8, :] = along_x(
                mixed[8 * q : 8 * q + 8, X * c : X * c + X], q
            )
        if DIRS[q][2]:
            ends = along_x(mixed[8 * q : 8 * q + 8, X * 4 :], q)
            for c, (y, z) in enumerate(corners):
                if DIRS[q][2] == (1 if z > 0 else -1):
                    value = jnp.where(above if z > 0 else below, ends[c : c + 1, :], 0.0)
                    s1[q, 1 + y, pl.ds(Z0 + z, 1), :] = value
    for side, (y, channels) in enumerate(((0, Y_UP), (CY - 1, Y_DOWN))):
        message = both.at[side]
        message[16:END_ROWS, :] = jnp.zeros((8, X), f32)
        for i, q in enumerate(channels):
            cz = DIRS[q][2]
            for e, z in enumerate(RAW_CELLS[cz]):
                message[pl.ds(RAW_ENDS + 2 * i + e, 1), :] = s0[q, 1 + y, pl.ds(Z0 + z, 1), :]
            for e, z in enumerate((0, CZ - 1)):
                message[pl.ds(MIXED_ENDS + 2 * i + e, 1), :] = s1[q, 1 + y, pl.ds(Z0 + z, 1), :]
            if cz:
                z, e = (CZ, 0) if cz > 0 else (-1, 1)
                message[pl.ds(CORNERS + e, 1), :] = s1[q, 1 + y, pl.ds(Z0 + z, 1), :]
    even_y = lax.rem(lax.axis_index("gy"), 2) == 0
    to_pair[...] = jnp.where(even_y, both[1], both[0])
    to_next[...] = jnp.where(even_y, both[0], both[1])


RAW_CELLS = {0: (-1, CZ), 1: (CZ, CZ + 1), -1: (-2, -1)}


def store_line(s1, y, out):
    for q in range(Q):
        for t in range(CZ // 8):
            s1[q, 1 + y, Z0 + 8 * t : Z0 + 8 * t + 8, :] = along_x(
                out[8 * q : 8 * q + 8, X * t : X * t + X], q
            )


def five_lines(ref, spare, lead, channels):
    tiles = []
    for i, p in enumerate(channels):
        cz = DIRS[p][2]
        line = ref[lead(i, p) + (pl.ds(Z0 + cz, CZ), slice(None))]
        for e, z in enumerate((-1, CZ)):
            spare[pl.ds(8 * i + e, 1), :] = ref[lead(i, p) + (pl.ds(Z0 + z + cz, 1), slice(None))]
        tiles.append(line_tiles(line) + [spare[8 * i : 8 * i + 8, :]])
    return stacked(tiles + [None])


def inner_rows_kernel(
    s0_in, w, s1_in, w_up, w_down, field, panel, cell, direction,
    s0, s1, out, scaled, rows, pick, kept, spare, numbers, sem,
):
    del s0_in, s1_in
    iy = lax.axis_index("gy")
    iz = lax.axis_index("gz")
    above = iz < lax.axis_size("gz") - 1
    below = iz > 0
    weights = w[...].astype(bf16)
    for y in range(2, CY - 2):
        for q in range(Q):
            s0[q, 1 + y, Z0 : Z0 + CZ, :] = along_x(field[q, CZ * y : CZ * y + CZ, :], q)
    reads = stacked(
        [
            [load_column(s0, p, DIRS[p][1], z + DIRS[p][2]) for z in (-1, CZ)]
            for p in range(Q)
        ]
        + [None]
    )
    mixed = mix(weights, reads)
    for c, (z, channels, valid) in enumerate(((-1, Z_DOWN, below), (CZ, Z_UP, above))):
        for q in channels:
            value = along_x(mixed[8 * q : 8 * q + 8, X * c : X * c + X], q)
            store_column(s1, q, 0, z, jnp.where(valid, value, 0.0))
    for y in range(1, CY - 1):
        store_line(s1, y, mix(weights, read_row(s0, y)))
    for y in range(2, CY - 2):
        mixed = mix(weights, read_row(s1, y))
        for q in range(Q):
            for t in range(CZ // 8):
                value = mixed[8 * q : 8 * q + 8, X * t : X * t + X]
                kept[q, y - 2, 8 * t : 8 * t + 8, :] = value
                at = q * (CY * CZ) + y * CZ + 8 * t
                scaled[at : at + 8, :] = value * LINK_WEIGHTS[q]
    copy = pltpu.make_async_copy(kept, out.at[:, pl.ds(2, CY - 4), :, :], sem)
    copy.start()
    numbers[...] = jnp.zeros((numbers.shape[0], X), f32)
    numbers[:, 0:CAP] = panel[...].astype(f32).T
    place = direction[...] * (CY * CZ) + cell[...]
    pick[...] = place[: CAP // 2] + place[CAP // 2 :] * PAIR

    @pl.loop(0, numbers.shape[0], unroll=8)
    def _(d):
        rows[pl.ds(d * (CAP + 1) + CAP, 1), 0, :] = numbers[pl.ds(d, 1), :]

    spare[...] = jnp.zeros((2, K2, X), f32)
    sides = (
        (0, CY - 1, CY, Y_UP, Y_DOWN, w_down, iy < lax.axis_size("gy") - 1),
        (1, 0, -1, Y_DOWN, Y_UP, w_up, iy > 0),
    )
    for side, y, halo, channels, sources, part, valid in sides:
        rows = [part[8 * q : 8 * q + 8, :] for q in channels]
        rows = jnp.concatenate(rows + [jnp.zeros_like(rows[0])], axis=0).astype(bf16)
        reads = five_lines(s0, spare.at[side], lambda i, p: (p, 1 + y), sources)
        mixed = jnp.where(valid, mix(rows, reads), 0.0)
        for i, q in enumerate(channels):
            for t in range(CZ // 8):
                s1[q, 1 + halo, Z0 + 8 * t : Z0 + 8 * t + 8, :] = along_x(
                    mixed[8 * i : 8 * i + 8, X * t : X * t + X], q
                )
            cz = DIRS[q][2]
            if cz:
                z, row, ok = (-1, 0, below) if cz < 0 else (CZ, 1, above)
                end = along_x(mixed[8 * i : 8 * i + 8, X * (CZ // 8) :], q)[row : row + 1, :]
                s1[q, 1 + halo, pl.ds(Z0 + z, 1), :] = jnp.where(ok, end, 0.0)
    copy.wait()


def sides_of(iy, w_up, w_down):
    return (
        (CY - 1, CY, Y_UP, w_up, iy < lax.axis_size("gy") - 1),
        (0, -1, Y_DOWN, w_down, iy > 0),
    )


def take_arrivals(iy, sides, take, from_pair, from_next):
    odd = lax.rem(iy, 2)
    for side in range(2):
        valid = sides[side][-1]
        pl.when(jnp.logical_and(valid, odd == side))(functools.partial(take, side, from_pair))
        pl.when(jnp.logical_and(valid, odd != side))(functools.partial(take, side, from_next))


def store_mixed(mixed, q, y, k, tiles, kept, scaled):
    for c, t in enumerate(tiles):
        value = mixed[8 * q : 8 * q + 8, X * c : X * c + X]
        kept[q, k, 8 * t : 8 * t + 8, :] = value
        at = q * (CY * CZ) + y * CZ + 8 * t
        scaled[at : at + 8, :] = value * LINK_WEIGHTS[q]


def read_tiles(ref, y, tiles):
    return stacked(
        [
            [ref[p, y + 1 + DIRS[p][1], pl.ds(Z0 + 8 * t + DIRS[p][2], 8), :] for t in tiles]
            for p in range(Q)
        ]
        + [None]
    )


MIDDLE = tuple(range(1, CZ // 8 - 1))
OUTER = (0, CZ // 8 - 1)


def middle_tiles_kernel(
    s1_in, w, w_up, w_down, from_next, from_pair, scaled_in, s1, scaled, raw, kept
):
    del s1_in, scaled_in
    iy = lax.axis_index("gy")
    weights = w[...].astype(bf16)
    cells = lax.broadcasted_iota(jnp.int32, (8, X), 0)
    sides = sides_of(iy, w_up, w_down)
    raw[...] = jnp.zeros((2, 5, ROWS, X), f32)

    def take(side, bulk):
        _, halo, channels, _, _ = sides[side]
        for i, q in enumerate(channels):
            raw[side, i, Z0 : Z0 + CZ, :] = bulk[RAW + CZ * i : RAW + CZ * i + CZ, :]
            for t in range(CZ // 8):
                value = bulk[MIXED + CZ * i + 8 * t : MIXED + CZ * i + 8 * t + 8, :]
                if t == 0:
                    value = jnp.where(cells > 0, value, 0.0)
                if t == CZ // 8 - 1:
                    value = jnp.where(cells < 7, value, 0.0)
                s1[q, 1 + halo, Z0 + 8 * t : Z0 + 8 * t + 8, :] += value

    take_arrivals(iy, sides, take, from_pair, from_next)
    for side, (y, _, channels, part, _) in enumerate(sides):
        tiles = [
            line_tiles(raw[side, i, pl.ds(Z0 + DIRS[p][2], CZ), :])
            for i, p in enumerate(channels)
        ]
        mixed = mix(part[...].astype(bf16), stacked(tiles + [None]))
        for q in range(Q):
            for t in range(CZ // 8):
                s1[q, 1 + y, Z0 + 8 * t : Z0 + 8 * t + 8, :] += along_x(
                    mixed[8 * q : 8 * q + 8, X * t : X * t + X], q
                )
    for k, y in enumerate(EDGE_ROWS):
        mixed = mix(weights, read_tiles(s1, y, MIDDLE))
        for q in range(Q):
            store_mixed(mixed, q, y, k, MIDDLE, kept, scaled)


def outer_tiles_kernel(
    s1_in, w, w_up, w_down, ends_next, ends_pair, pick_in, scaled_in, raw_in, kept_in,
    rows_in, out_in,
    s1, scaled, raw, kept, rows, out, spare, pick, pick_sem, out_sem,
):
    del s1_in, scaled_in, raw_in, kept_in, rows_in, out_in
    fetch = pltpu.make_async_copy(pick_in, pick, pick_sem)
    fetch.start()
    iy = lax.axis_index("gy")
    iz = lax.axis_index("gz")
    weights = w[...].astype(bf16)
    z_ok = (iz > 0, iz < lax.axis_size("gz") - 1)
    sides = sides_of(iy, w_up, w_down)
    spare[...] = jnp.zeros((2, K2, X), f32)

    def take(side, ends):
        _, halo, channels, _, _ = sides[side]
        for i, q in enumerate(channels):
            cz = DIRS[q][2]
            for e, z in enumerate(RAW_CELLS[cz]):
                raw[side, i, pl.ds(Z0 + z, 1), :] = ends[pl.ds(RAW_ENDS + 2 * i + e, 1), :]
            for e, z in enumerate((0, CZ - 1)):
                at = pl.ds(MIXED_ENDS + 2 * i + e, 1)
                s1[q, 1 + halo, pl.ds(Z0 + z, 1), :] += ends[at, :]
            if cz:
                z, e = (CZ, 0) if cz > 0 else (-1, 1)
                s1[q, 1 + halo, pl.ds(Z0 + z, 1), :] += ends[CORNERS + e : CORNERS + e + 1, :]

    take_arrivals(iy, sides, take, ends_pair, ends_next)
    for side, (y, _, channels, part, _) in enumerate(sides):
        for i, p in enumerate(channels):
            cz = DIRS[p][2]
            wanted = [(2, cz - 1), (3, CZ + cz)]
            if cz < 0:
                wanted.append((0, -1))
            if cz > 0:
                wanted.append((1, CZ))
            for j, z in wanted:
                spare[side, pl.ds(8 * i + j, 1), :] = raw[side, i, pl.ds(Z0 + z, 1), :]
        mixed = mix(part[...].astype(bf16), spare[side])
        for q in range(Q):
            cz = DIRS[q][2]
            value = along_x(mixed[8 * q : 8 * q + 8, :], q)
            for j, z in ((0, 0), (1, CZ - 1)):
                s1[q, 1 + y, pl.ds(Z0 + z, 1), :] += value[j : j + 1, :]
            if cz:
                j, z = (2, -1) if cz < 0 else (3, CZ)
                value = jnp.where(z_ok[j - 2], value[j : j + 1, :], 0.0)
                s1[q, 1 + y, pl.ds(Z0 + z, 1), :] += value

    copies = [
        pltpu.make_async_copy(
            kept.at[:, pl.ds(2 * h, 2), :, :], out.at[:, pl.ds(6 * h, 2), :, :], out_sem.at[h]
        )
        for h in range(2)
    ]
    for k, y in enumerate(EDGE_ROWS):
        mixed = mix(weights, read_tiles(s1, y, OUTER))
        for q in range(Q):
            store_mixed(mixed, q, y, k, OUTER, kept, scaled)
        if k % 2:
            copies[k // 2].start()
    fetch.wait()

    @pl.loop(0, pick.shape[1], unroll=8)
    def _(d):
        for k in range(CAP // 2):
            places = pick[k, d]
            for j, at in ((k, places & (PAIR - 1)), (k + CAP // 2, places >> 13)):
                rows[pl.ds(d * (CAP + 1) + j, 1), 0, :] = scaled[pl.ds(at, 1), :]

    for copy in copies:
        copy.wait()


def sum_kernel(arrived, out):
    devices = arrived.shape[0] // (CAP + 1)
    numbers = arrived[pl.ds(CAP, devices, stride=CAP + 1), :].T
    panels = lax.broadcasted_iota(jnp.int32, (P_DEV, devices), 0).astype(f32)
    hot, rows = [], []
    for k in range(CAP):
        hot.append((numbers[k : k + 1, :] == panels).astype(f32).astype(bf16))
        rows.append(arrived[pl.ds(k, devices, stride=CAP + 1), :])
    hot = jnp.concatenate(hot, axis=1)
    high, low = split(jnp.concatenate(rows, axis=0))
    dot = functools.partial(jnp.dot, preferred_element_type=f32)
    out[...] = dot(hot, high) + dot(hot, low)


VMEM = pl.BlockSpec(memory_space=pltpu.VMEM)
HBM = pl.BlockSpec(memory_space=pltpu.HBM)
MIB = 1024 * 1024


def call(kernel, name, ins, outs, shapes, scratch=(), aliases=None, cost=None):
    return pl.pallas_call(
        kernel,
        out_shape=[jax.ShapeDtypeStruct(*s) for s in shapes],
        in_specs=ins,
        out_specs=outs,
        scratch_shapes=list(scratch),
        input_output_aliases=aliases or {},
        compiler_params=pltpu.CompilerParams(vmem_limit_bytes=32 * MIB),
        cost_estimate=cost
        and pl.CostEstimate(flops=cost, bytes_accessed=cost // 1000, transcendentals=cost // 1000),
        name=name,
    )


def pairings(gy, gz):
    def exchange(partner):
        found = []
        for y in range(gy):
            for z in range(gz):
                py, pz = partner(y, z)
                found.append((y * gz + z, py * gz + pz))
        return found

    def step(i, n):
        j = i - 1 if i % 2 == 0 else i + 1
        return j if 0 <= j < n else None

    def z_next(y, z):
        return (y ^ 1, z) if step(z, gz) is None else (y, step(z, gz))

    def y_next(y, z):
        return (y, z ^ 1) if step(y, gy) is None else (step(y, gy), z)

    return (
        exchange(lambda y, z: (y, z ^ 1)),
        exchange(z_next),
        exchange(lambda y, z: (y ^ 1, z)),
        exchange(y_next),
    )


def on_device(adjoint, collision, link_cell, link_dir, link_panel):
    gz = lax.axis_size("gz")
    gy = lax.axis_size("gy")
    devices = link_cell.shape[1]
    pad = (Q, CY + 2, ROWS, X)
    own = (Q, CY, CZ, X)
    flat = adjoint.reshape(Q, CY * CZ, X)
    dma = pltpu.SemaphoreType.DMA
    wide = ((K1, 3 * K1), f32)
    narrow = ((K1, 3 * K2), f32)
    w, w_up, w_down = call(
        weights_kernel, "weights", [VMEM], [VMEM] * 3, [wide, narrow, narrow], cost=4_000_000_000
    )(collision)
    to_pair, to_next, empty = call(
        pack_z_kernel, "pack_z", [VMEM] * 2, [VMEM] * 3, [((Z_ROWS, X), f32)] * 2 + [((8, X), f32)],
        cost=4_000_000_000,
    )(flat, w)
    both = ("gy", "gz")
    z_pairs, z_nexts, y_pairs, y_nexts = pairings(gy, gz)
    from_pair = lax.ppermute(to_pair, both, z_pairs)
    from_next = lax.ppermute(to_next, both, z_nexts)
    lines = ((Y_ROWS, X), f32)
    s0, s1, to_y_pair, to_y_next = call(
        bulk_rows_kernel, "bulk_rows", [VMEM] * 3, [VMEM] * 4,
        [(pad, f32), (pad, f32), lines, lines],
    )(flat, w, empty)
    from_y_pair = lax.ppermute(to_y_pair, both, y_pairs)
    from_y_next = lax.ppermute(to_y_next, both, y_nexts)
    s0, s1, to_y_pair, to_y_next = call(
        end_cells_kernel, "end_cells", [VMEM] * 5, [VMEM] * 4,
        [(pad, f32), (pad, f32), ((END_ROWS, X), f32), ((END_ROWS, X), f32)],
        scratch=[pltpu.VMEM((2, END_ROWS, X), f32), pltpu.VMEM((Q, 8, X), f32)],
        aliases={0: 0, 1: 1},
    )(s0, s1, w, from_pair, from_next)
    ends_pair = lax.ppermute(to_y_pair, both, y_pairs)
    ends_next = lax.ppermute(to_y_next, both, y_nexts)
    table = ((Q * CY * CZ, X), f32)
    message = ((devices * (CAP + 1), 1, X), f32)
    _, s1, out, scaled, rows, pick = call(
        inner_rows_kernel, "inner_rows", [VMEM] * 9, [VMEM] * 2 + [HBM] + [VMEM] * 3,
        [(pad, f32), (pad, f32), (own, f32), table]
        + [message, ((CAP // 2, devices), jnp.int32)],
        scratch=[
            pltpu.VMEM((Q, CY - 4, CZ, X), f32),
            pltpu.VMEM((2, K2, X), f32),
            pltpu.VMEM((devices, X), f32),
            dma,
        ],
        cost=4_000_000_000,
        aliases={0: 0, 2: 1},
    )(s0, w, s1, w_up, w_down, flat, link_panel[0].T, link_cell[0].T, link_dir[0].T)
    edge = ((Q, 4, CZ, X), f32)
    lines = ((2, 5, ROWS, X), f32)
    s1, scaled, raw, kept = call(
        middle_tiles_kernel, "middle_tiles", [VMEM] * 7, [VMEM] * 4,
        [(pad, f32), table, lines, edge],
        aliases={0: 0, 6: 1},
        cost=1_000_000_000,
    )(s1, w, w_up, w_down, from_y_next, from_y_pair, scaled)
    _, _, _, _, rows, out = call(
        outer_tiles_kernel, "outer_tiles", [VMEM] * 11 + [HBM], [VMEM] * 5 + [HBM],
        [(pad, f32), table, lines, edge, message, (own, f32)],
        scratch=[
            pltpu.VMEM((2, K2, X), f32),
            pltpu.SMEM((CAP // 2, devices), jnp.int32),
            dma,
            dma((2,)),
        ],
        aliases={0: 0, 7: 1, 8: 2, 9: 3, 10: 4, 11: 5},
    )(s1, w, w_up, w_down, ends_next, ends_pair, pick, scaled, raw, kept, rows, out)
    arrived = lax.all_to_all(
        rows.reshape(devices, CAP + 1, 1, X), ("gy", "gz"), split_axis=0, concat_axis=0, tiled=True
    )
    (panel_sens,) = call(sum_kernel, "sum_rows", [VMEM], [VMEM], [((P_DEV, X), f32)])(
        arrived.reshape(devices * (CAP + 1), X)
    )
    return out, panel_sens


def solution(mesh):
    placed = (
        P(None, "gy", "gz", None),
        P(),
        P(("gy", "gz"), None, None),
        P(("gy", "gz"), None, None),
        P(("gy", "gz"), None, None),
    )
    return jax.shard_map(
        on_device,
        mesh=mesh,
        in_specs=placed,
        out_specs=(P(None, "gy", "gz", None), P(("gy", "gz"), None)),
        check_vma=False,
    )
```

```python
import functools

import jax
import jax.numpy as jnp
from jax import lax
from jax.experimental import pallas as pl
from jax.experimental.pallas import tpu as pltpu
from jax.sharding import PartitionSpec as P

Q = 19
QP = 20
P_DEV = 64
CAP = 8
CY = 8
CZ = 32
X = 128
ROWS = 48
Z0 = 8

DIRS = [
    (0, 0, 0),
    (1, 0, 0),
    (-1, 0, 0),
    (0, 1, 0),
    (0, -1, 0),
    (0, 0, 1),
    (0, 0, -1),
    (1, 1, 0),
    (-1, -1, 0),
    (1, -1, 0),
    (-1, 1, 0),
    (1, 0, 1),
    (-1, 0, -1),
    (1, 0, -1),
    (-1, 0, 1),
    (0, 1, 1),
    (0, -1, -1),
    (0, 1, -1),
    (0, -1, 1),
]
LINK_WEIGHTS = [2.0] + [1.0 / 3.0] * 6 + [1.0 / 6.0] * 12

Y_UP = [q for q in range(Q) if DIRS[q][1] == 1]
Y_DOWN = [q for q in range(Q) if DIRS[q][1] == -1]
Z_UP = [q for q in range(Q) if DIRS[q][2] == 1]
Z_DOWN = [q for q in range(Q) if DIRS[q][2] == -1]
Z_FLAT = [q for q in range(Q) if DIRS[q][2] == 0]
SEND_LOW = [(q, 0) for q in Z_FLAT] + [(q, 0) for q in Z_UP] + [(q, 1) for q in Z_UP]
SEND_HIGH = [(q, 0) for q in Z_FLAT] + [(q, 0) for q in Z_DOWN] + [(q, 1) for q in Z_DOWN]

RAW = 0
MIXED = 5 * CZ
Y_ROWS = 10 * CZ
RAW_ENDS = 0
MIXED_ENDS = 10
CORNERS = 20
END_ROWS = 24
Z_ROWS = 8 * Q
PAIR = 1 << 13
K1 = QP * 8
K2 = 6 * 8

f32 = jnp.float32
bf16 = jnp.bfloat16


def along_x(value, q):
    cx = DIRS[q][0]
    if cx == 0:
        return value
    return pltpu.roll(value, (-cx) % X, value.ndim - 1)


def split(value):
    high = value.astype(bf16)
    return high, (value - high.astype(f32)).astype(bf16)


def mix(weights, reads):
    high, low = split(reads)
    return jnp.dot(
        weights, jnp.concatenate([high, low, high], axis=0), preferred_element_type=f32
    )


def stacked(tiles):
    count = max(len(t) for t in tiles if t is not None)
    zero = jnp.zeros((8, X), f32)
    full = [t if t is not None else [zero] * count for t in tiles]
    return jnp.concatenate(
        [jnp.concatenate([t[c] for t in full], axis=0) for c in range(count)], axis=1
    )


def line_tiles(line):
    return [line[8 * t : 8 * t + 8, :] for t in range(CZ // 8)]


def read_line(ref, p, y, shift=0):
    cx, cy, cz = DIRS[p]
    return ref[p, y + 1 + cy, pl.ds(Z0 + cz + shift, CZ), :]


def read_row(ref, y):
    return stacked([line_tiles(read_line(ref, p, y)) for p in range(Q)] + [None])


def load_column(ref, q, y, z):
    flat = ref.reshape(Q, (CY + 2) * ROWS, X)
    return flat[q, pl.ds((1 + y) * ROWS + Z0 + z, CY, stride=ROWS), :]


def store_column(ref, q, y, z, value):
    flat = ref.reshape(Q, (CY + 2) * ROWS, X)
    flat[q, pl.ds((1 + y) * ROWS + Z0 + z, CY, stride=ROWS), :] = value


def pack_z_kernel(field, w, to_pair, to_next, empty):
    del w
    empty[...] = jnp.zeros((8, X), f32)
    even = lax.rem(lax.axis_index("gz"), 2) == 0
    for i in range(Q):
        q, d = SEND_LOW[i]
        low = field[q, pl.ds(d, CY, stride=CZ), :]
        q, d = SEND_HIGH[i]
        high = field[q, pl.ds(CZ - 1 - d, CY, stride=CZ), :]
        to_pair[8 * i : 8 * i + 8, :] = jnp.where(even, high, low)
        to_next[8 * i : 8 * i + 8, :] = jnp.where(even, low, high)


def own_channel(shape, axis, channels):
    place = lax.broadcasted_iota(jnp.int32, shape, axis) // 8
    channel = lax.broadcasted_iota(jnp.int32, shape, 1 - axis)
    hit = jnp.zeros(shape, f32)
    for i, q in enumerate(channels):
        hit = jnp.where(jnp.logical_and(place == i, channel == q), 1.0, hit)
    return hit.astype(bf16)


def spread_weights(collision, channels, width):
    rows = (
        lax.broadcasted_iota(jnp.int32, (K1, Q), 0) // 8
        == lax.broadcasted_iota(jnp.int32, (K1, Q), 1)
    ).astype(f32).astype(bf16)
    columns = own_channel((width, Q), 0, channels)
    same = (
        lax.broadcasted_iota(jnp.int32, (K1, width), 0) % 8
        == lax.broadcasted_iota(jnp.int32, (K1, width), 1) % 8
    )
    dims = (((1,), (1,)), ((), ()))
    parts = []
    for part in split(collision):
        turned = lax.dot_general(rows, part, dims, preferred_element_type=f32).astype(bf16)
        wide = lax.dot_general(turned, columns, dims, preferred_element_type=f32)
        parts.append(jnp.where(same, wide, 0.0))
    return jnp.concatenate([parts[0], parts[0], parts[1]], axis=1)


def weights_kernel(collision, w, w_up, w_down):
    w[...] = spread_weights(collision[...], range(Q), K1)
    w_up[...] = spread_weights(collision[...], Y_UP, K2)
    w_down[...] = spread_weights(collision[...], Y_DOWN, K2)


EDGE_ROWS = (0, 1, CY - 2, CY - 1)


def bulk_rows_kernel(field, w, empty, s0, s1, to_pair, to_next):
    nothing = empty[...]
    for q in range(Q):
        for y in EDGE_ROWS:
            s0[q, 1 + y, Z0 : Z0 + CZ, :] = along_x(field[q, CZ * y : CZ * y + CZ, :], q)
    for q in Y_DOWN + Y_UP:
        for t in range(ROWS // 8):
            s0[q, 0 if DIRS[q][1] < 0 else CY + 1, 8 * t : 8 * t + 8, :] = nothing
    for q in range(Q):
        if DIRS[q][2]:
            for y in EDGE_ROWS:
                s0[q, 1 + y, 0:Z0, :] = nothing
                s0[q, 1 + y, Z0 + CZ : ROWS, :] = nothing
    weights = w[...].astype(bf16)
    for y in (0, CY - 1):
        store_line(s1, y, mix(weights, read_row(s0, y)))
    even = lax.rem(lax.axis_index("gy"), 2) == 0
    for ref, base in ((s0, RAW), (s1, MIXED)):
        for i in range(5):
            low = ref[Y_UP[i], 1, Z0 : Z0 + CZ, :]
            high = ref[Y_DOWN[i], CY, Z0 : Z0 + CZ, :]
            at = base + CZ * i
            to_pair[at : at + CZ, :] = jnp.where(even, high, low)
            to_next[at : at + CZ, :] = jnp.where(even, low, high)


def end_cells_kernel(
    s0_in, s1_in, w, from_pair, from_next, s0, s1, to_pair, to_next, both, corner
):
    del s0_in, s1_in
    iz = lax.axis_index("gz")
    even = lax.rem(iz, 2) == 0
    above = iz < lax.axis_size("gz") - 1
    below = iz > 0

    def insert(sends, place, arrived):
        for i, (q, d) in enumerate(sends):
            value = 0.0 if arrived is None else along_x(arrived[8 * i : 8 * i + 8, :], q)
            store_column(s0, q, 0, place(d), jnp.broadcast_to(value, (CY, X)))

    for sends, place, valid, when_even, when_odd in (
        (SEND_LOW, lambda d: CZ + d, above, from_pair, from_next),
        (SEND_HIGH, lambda d: -1 - d, below, from_next, from_pair),
    ):
        put = functools.partial(insert, sends, place)
        pl.when(jnp.logical_and(valid, even))(functools.partial(put, when_even))
        pl.when(jnp.logical_and(valid, jnp.logical_not(even)))(functools.partial(put, when_odd))
        pl.when(jnp.logical_not(valid))(functools.partial(put, None))
    last = CZ // 8 - 1
    spots = [(y, t) for y in (0, CY - 1) for t in (0, last)]
    corners = [(y, z) for y in (0, CY - 1) for z in (-1, CZ)]
    corner[...] = jnp.zeros((Q, 8, X), f32)
    tiles = []
    for p in range(Q):
        cx, cy, cz = DIRS[p]
        for c, (y, z) in enumerate(corners):
            corner[p, pl.ds(c, 1), :] = s0[p, y + 1 + cy, pl.ds(Z0 + z + cz, 1), :]
        tiles.append(
            [s0[p, y + 1 + cy, pl.ds(Z0 + 8 * t + cz, 8), :] for y, t in spots] + [corner[p]]
        )
    mixed = mix(w[...].astype(bf16), stacked(tiles + [None]))
    for q in range(Q):
        for c, (y, t) in enumerate(spots):
            s1[q, 1 + y, Z0 + 8 * t : Z0 + 8 * t + 8, :] = along_x(
                mixed[8 * q : 8 * q + 8, X * c : X * c + X], q
            )
        if DIRS[q][2]:
            ends = along_x(mixed[8 * q : 8 * q + 8, X * 4 :], q)
            for c, (y, z) in enumerate(corners):
                if DIRS[q][2] == (1 if z > 0 else -1):
                    value = jnp.where(above if z > 0 else below, ends[c : c + 1, :], 0.0)
                    s1[q, 1 + y, pl.ds(Z0 + z, 1), :] = value
    for side, (y, channels) in enumerate(((0, Y_UP), (CY - 1, Y_DOWN))):
        message = both.at[side]
        message[16:END_ROWS, :] = jnp.zeros((8, X), f32)
        for i, q in enumerate(channels):
            cz = DIRS[q][2]
            for e, z in enumerate(RAW_CELLS[cz]):
                message[pl.ds(RAW_ENDS + 2 * i + e, 1), :] = s0[q, 1 + y, pl.ds(Z0 + z, 1), :]
            for e, z in enumerate((0, CZ - 1)):
                message[pl.ds(MIXED_ENDS + 2 * i + e, 1), :] = s1[q, 1 + y, pl.ds(Z0 + z, 1), :]
            if cz:
                z, e = (CZ, 0) if cz > 0 else (-1, 1)
                message[pl.ds(CORNERS + e, 1), :] = s1[q, 1 + y, pl.ds(Z0 + z, 1), :]
    even_y = lax.rem(lax.axis_index("gy"), 2) == 0
    to_pair[...] = jnp.where(even_y, both[1], both[0])
    to_next[...] = jnp.where(even_y, both[0], both[1])


RAW_CELLS = {0: (-1, CZ), 1: (CZ, CZ + 1), -1: (-2, -1)}


def store_line(s1, y, out):
    for q in range(Q):
        for t in range(CZ // 8):
            s1[q, 1 + y, Z0 + 8 * t : Z0 + 8 * t + 8, :] = along_x(
                out[8 * q : 8 * q + 8, X * t : X * t + X], q
            )


def five_lines(ref, spare, lead, channels):
    tiles = []
    for i, p in enumerate(channels):
        cz = DIRS[p][2]
        line = ref[lead(i, p) + (pl.ds(Z0 + cz, CZ), slice(None))]
        for e, z in enumerate((-1, CZ)):
            spare[pl.ds(8 * i + e, 1), :] = ref[lead(i, p) + (pl.ds(Z0 + z + cz, 1), slice(None))]
        tiles.append(line_tiles(line) + [spare[8 * i : 8 * i + 8, :]])
    return stacked(tiles + [None])


def inner_rows_kernel(
    s0_in, w, s1_in, w_up, w_down, field, panel, cell, direction,
    s0, s1, out, scaled, rows, pick, kept, spare, numbers, sem,
):
    del s0_in, s1_in
    iy = lax.axis_index("gy")
    iz = lax.axis_index("gz")
    above = iz < lax.axis_size("gz") - 1
    below = iz > 0
    weights = w[...].astype(bf16)
    for y in range(2, CY - 2):
        for q in range(Q):
            s0[q, 1 + y, Z0 : Z0 + CZ, :] = along_x(field[q, CZ * y : CZ * y + CZ, :], q)
    reads = stacked(
        [
            [load_column(s0, p, DIRS[p][1], z + DIRS[p][2]) for z in (-1, CZ)]
            for p in range(Q)
        ]
        + [None]
    )
    mixed = mix(weights, reads)
    for c, (z, channels, valid) in enumerate(((-1, Z_DOWN, below), (CZ, Z_UP, above))):
        for q in channels:
            value = along_x(mixed[8 * q : 8 * q + 8, X * c : X * c + X], q)
            store_column(s1, q, 0, z, jnp.where(valid, value, 0.0))
    for y in range(1, CY - 1):
        store_line(s1, y, mix(weights, read_row(s0, y)))
    for y in range(2, CY - 2):
        mixed = mix(weights, read_row(s1, y))
        for q in range(Q):
            for t in range(CZ // 8):
                value = mixed[8 * q : 8 * q + 8, X * t : X * t + X]
                kept[q, y - 2, 8 * t : 8 * t + 8, :] = value
                at = q * (CY * CZ) + y * CZ + 8 * t
                scaled[at : at + 8, :] = value * LINK_WEIGHTS[q]
    copy = pltpu.make_async_copy(kept, out.at[:, pl.ds(2, CY - 4), :, :], sem)
    copy.start()
    numbers[...] = jnp.zeros((numbers.shape[0], X), f32)
    numbers[:, 0:CAP] = panel[...].astype(f32).T
    place = direction[...] * (CY * CZ) + cell[...]
    pick[...] = place[: CAP // 2] + place[CAP // 2 :] * PAIR

    @pl.loop(0, numbers.shape[0], unroll=8)
    def _(d):
        rows[pl.ds(d * (CAP + 1) + CAP, 1), 0, :] = numbers[pl.ds(d, 1), :]

    spare[...] = jnp.zeros((2, K2, X), f32)
    sides = (
        (0, CY - 1, CY, Y_UP, Y_DOWN, w_down, iy < lax.axis_size("gy") - 1),
        (1, 0, -1, Y_DOWN, Y_UP, w_up, iy > 0),
    )
    for side, y, halo, channels, sources, part, valid in sides:
        rows = [part[8 * q : 8 * q + 8, :] for q in channels]
        rows = jnp.concatenate(rows + [jnp.zeros_like(rows[0])], axis=0).astype(bf16)
        reads = five_lines(s0, spare.at[side], lambda i, p: (p, 1 + y), sources)
        mixed = jnp.where(valid, mix(rows, reads), 0.0)
        for i, q in enumerate(channels):
            for t in range(CZ // 8):
                s1[q, 1 + halo, Z0 + 8 * t : Z0 + 8 * t + 8, :] = along_x(
                    mixed[8 * i : 8 * i + 8, X * t : X * t + X], q
                )
            cz = DIRS[q][2]
            if cz:
                z, row, ok = (-1, 0, below) if cz < 0 else (CZ, 1, above)
                end = along_x(mixed[8 * i : 8 * i + 8, X * (CZ // 8) :], q)[row : row + 1, :]
                s1[q, 1 + halo, pl.ds(Z0 + z, 1), :] = jnp.where(ok, end, 0.0)
    copy.wait()


def outer_rows_kernel(
    s1_in, w, w_up, w_down, from_next, from_pair, ends_next, ends_pair, pick_in, scaled_in,
    rows_in, out_in,
    s1, scaled, rows, out, kept, raw, spare, pick, pick_sem, out_sem,
):
    del s1_in, scaled_in, rows_in, out_in
    fetch = pltpu.make_async_copy(pick_in, pick, pick_sem)
    fetch.start()
    iy = lax.axis_index("gy")
    iz = lax.axis_index("gz")
    weights = w[...].astype(bf16)
    z_ok = (iz > 0, iz < lax.axis_size("gz") - 1)
    first = lax.broadcasted_iota(jnp.int32, (8, X), 0) == 0
    final = lax.broadcasted_iota(jnp.int32, (8, X), 0) == 7
    spare[...] = jnp.zeros((2, K2, X), f32)
    sides = (
        (0, CY - 1, CY, Y_UP, w_up, iy < lax.axis_size("gy") - 1),
        (1, 0, -1, Y_DOWN, w_down, iy > 0),
    )

    def take(side, bulk, ends):
        _, _, halo, channels, _, _ = sides[side]
        for i, q in enumerate(channels):
            cz = DIRS[q][2]
            raw[side, i, Z0 : Z0 + CZ, :] = bulk[RAW + CZ * i : RAW + CZ * i + CZ, :]
            for e, z in enumerate(RAW_CELLS[cz]):
                raw[side, i, pl.ds(Z0 + z, 1), :] = ends[pl.ds(RAW_ENDS + 2 * i + e, 1), :]
            for t in range(CZ // 8):
                value = bulk[MIXED + CZ * i + 8 * t : MIXED + CZ * i + 8 * t + 8, :]
                at = MIXED_ENDS + 2 * i
                if t == 0:
                    value = jnp.where(first, ends[at : at + 1, :], value)
                if t == CZ // 8 - 1:
                    value = jnp.where(final, ends[at + 1 : at + 2, :], value)
                s1[q, 1 + halo, Z0 + 8 * t : Z0 + 8 * t + 8, :] += value
            if cz:
                z, e = (CZ, 0) if cz > 0 else (-1, 1)
                s1[q, 1 + halo, pl.ds(Z0 + z, 1), :] += ends[CORNERS + e : CORNERS + e + 1, :]

    odd = lax.rem(iy, 2)
    for side, (_, _, _, _, _, valid) in enumerate(sides):
        pl.when(jnp.logical_and(valid, odd == side))(
            functools.partial(take, side, from_pair, ends_pair)
        )
        pl.when(jnp.logical_and(valid, odd != side))(
            functools.partial(take, side, from_next, ends_next)
        )

        @pl.when(jnp.logical_not(valid))
        def _(side=side):
            raw[side] = jnp.zeros((5, ROWS, X), f32)

    for side, y, halo, channels, part, valid in sides:
        reads = five_lines(raw.at[side], spare.at[side], lambda i, p: (i,), channels)
        mixed = mix(part[...].astype(bf16), reads)
        for q in range(Q):
            for t in range(CZ // 8):
                at = pl.ds(Z0 + 8 * t, 8)
                s1[q, 1 + y, at, :] += along_x(mixed[8 * q : 8 * q + 8, X * t : X * t + X], q)
            cz = DIRS[q][2]
            if cz:
                row = 0 if cz < 0 else 1
                end = along_x(mixed[8 * q : 8 * q + 8, X * (CZ // 8) :], q)[row : row + 1, :]
                at = pl.ds(Z0 - 1 if cz < 0 else Z0 + CZ, 1)
                s1[q, 1 + y, at, :] += jnp.where(z_ok[row], end, 0.0)

    copies = [
        pltpu.make_async_copy(
            kept.at[:, pl.ds(2 * h, 2), :, :], out.at[:, pl.ds(6 * h, 2), :, :], out_sem.at[h]
        )
        for h in range(2)
    ]
    for k, y in enumerate((0, 1, CY - 2, CY - 1)):
        mixed = mix(weights, read_row(s1, y))
        for q in range(Q):
            for t in range(CZ // 8):
                value = mixed[8 * q : 8 * q + 8, X * t : X * t + X]
                kept[q, k, 8 * t : 8 * t + 8, :] = value
                at = q * (CY * CZ) + y * CZ + 8 * t
                scaled[at : at + 8, :] = value * LINK_WEIGHTS[q]
        if k % 2:
            copies[k // 2].start()
    fetch.wait()

    @pl.loop(0, pick.shape[1], unroll=8)
    def _(d):
        for k in range(CAP // 2):
            places = pick[k, d]
            for j, at in ((k, places & (PAIR - 1)), (k + CAP // 2, places >> 13)):
                rows[pl.ds(d * (CAP + 1) + j, 1), 0, :] = scaled[pl.ds(at, 1), :]

    for copy in copies:
        copy.wait()


def sum_kernel(arrived, out):
    devices = arrived.shape[0] // (CAP + 1)
    numbers = arrived[pl.ds(CAP, devices, stride=CAP + 1), :].T
    panels = lax.broadcasted_iota(jnp.int32, (P_DEV, devices), 0).astype(f32)
    hot, rows = [], []
    for k in range(CAP):
        hot.append((numbers[k : k + 1, :] == panels).astype(f32).astype(bf16))
        rows.append(arrived[pl.ds(k, devices, stride=CAP + 1), :])
    hot = jnp.concatenate(hot, axis=1)
    high, low = split(jnp.concatenate(rows, axis=0))
    dot = functools.partial(jnp.dot, preferred_element_type=f32)
    out[...] = dot(hot, high) + dot(hot, low)


VMEM = pl.BlockSpec(memory_space=pltpu.VMEM)
HBM = pl.BlockSpec(memory_space=pltpu.HBM)
MIB = 1024 * 1024


def call(kernel, name, ins, outs, shapes, scratch=(), aliases=None, cost=None):
    return pl.pallas_call(
        kernel,
        out_shape=[jax.ShapeDtypeStruct(*s) for s in shapes],
        in_specs=ins,
        out_specs=outs,
        scratch_shapes=list(scratch),
        input_output_aliases=aliases or {},
        compiler_params=pltpu.CompilerParams(vmem_limit_bytes=32 * MIB),
        cost_estimate=cost
        and pl.CostEstimate(flops=cost, bytes_accessed=cost // 1000, transcendentals=cost // 1000),
        name=name,
    )


def pairings(gy, gz):
    def exchange(partner):
        found = []
        for y in range(gy):
            for z in range(gz):
                py, pz = partner(y, z)
                found.append((y * gz + z, py * gz + pz))
        return found

    def step(i, n):
        j = i - 1 if i % 2 == 0 else i + 1
        return j if 0 <= j < n else None

    def z_next(y, z):
        return (y ^ 1, z) if step(z, gz) is None else (y, step(z, gz))

    def y_next(y, z):
        return (y, z ^ 1) if step(y, gy) is None else (step(y, gy), z)

    return (
        exchange(lambda y, z: (y, z ^ 1)),
        exchange(z_next),
        exchange(lambda y, z: (y ^ 1, z)),
        exchange(y_next),
    )


def on_device(adjoint, collision, link_cell, link_dir, link_panel):
    gz = lax.axis_size("gz")
    gy = lax.axis_size("gy")
    devices = link_cell.shape[1]
    pad = (Q, CY + 2, ROWS, X)
    own = (Q, CY, CZ, X)
    flat = adjoint.reshape(Q, CY * CZ, X)
    dma = pltpu.SemaphoreType.DMA
    wide = ((K1, 3 * K1), f32)
    narrow = ((K1, 3 * K2), f32)
    w, w_up, w_down = call(
        weights_kernel, "weights", [VMEM], [VMEM] * 3, [wide, narrow, narrow], cost=4_000_000_000
    )(collision)
    to_pair, to_next, empty = call(
        pack_z_kernel, "pack_z", [VMEM] * 2, [VMEM] * 3, [((Z_ROWS, X), f32)] * 2 + [((8, X), f32)],
        cost=4_000_000_000,
    )(flat, w)
    both = ("gy", "gz")
    z_pairs, z_nexts, y_pairs, y_nexts = pairings(gy, gz)
    from_pair = lax.ppermute(to_pair, both, z_pairs)
    from_next = lax.ppermute(to_next, both, z_nexts)
    lines = ((Y_ROWS, X), f32)
    s0, s1, to_y_pair, to_y_next = call(
        bulk_rows_kernel, "bulk_rows", [VMEM] * 3, [VMEM] * 4,
        [(pad, f32), (pad, f32), lines, lines],
    )(flat, w, empty)
    from_y_pair = lax.ppermute(to_y_pair, both, y_pairs)
    from_y_next = lax.ppermute(to_y_next, both, y_nexts)
    s0, s1, to_y_pair, to_y_next = call(
        end_cells_kernel, "end_cells", [VMEM] * 5, [VMEM] * 4,
        [(pad, f32), (pad, f32), ((END_ROWS, X), f32), ((END_ROWS, X), f32)],
        scratch=[pltpu.VMEM((2, END_ROWS, X), f32), pltpu.VMEM((Q, 8, X), f32)],
        aliases={0: 0, 1: 1},
    )(s0, s1, w, from_pair, from_next)
    ends_pair = lax.ppermute(to_y_pair, both, y_pairs)
    ends_next = lax.ppermute(to_y_next, both, y_nexts)
    table = ((Q * CY * CZ, X), f32)
    message = ((devices * (CAP + 1), 1, X), f32)
    _, s1, out, scaled, rows, pick = call(
        inner_rows_kernel, "inner_rows", [VMEM] * 9, [VMEM] * 2 + [HBM] + [VMEM] * 3,
        [(pad, f32), (pad, f32), (own, f32), table]
        + [message, ((CAP // 2, devices), jnp.int32)],
        scratch=[
            pltpu.VMEM((Q, CY - 4, CZ, X), f32),
            pltpu.VMEM((2, K2, X), f32),
            pltpu.VMEM((devices, X), f32),
            dma,
        ],
        cost=4_000_000_000,
        aliases={0: 0, 2: 1},
    )(s0, w, s1, w_up, w_down, flat, link_panel[0].T, link_cell[0].T, link_dir[0].T)
    _, _, rows, out = call(
        outer_rows_kernel, "outer_rows", [VMEM] * 11 + [HBM], [VMEM] * 3 + [HBM],
        [(pad, f32), table, message, (own, f32)],
        scratch=[
            pltpu.VMEM((Q, 4, CZ, X), f32),
            pltpu.VMEM((2, 5, ROWS, X), f32),
            pltpu.VMEM((2, K2, X), f32),
            pltpu.SMEM((CAP // 2, devices), jnp.int32),
            dma,
            dma((2,)),
        ],
        aliases={0: 0, 9: 1, 10: 2, 11: 3},
    )(s1, w, w_up, w_down, from_y_next, from_y_pair, ends_next, ends_pair, pick, scaled, rows, out)
    arrived = lax.all_to_all(
        rows.reshape(devices, CAP + 1, 1, X), ("gy", "gz"), split_axis=0, concat_axis=0, tiled=True
    )
    (panel_sens,) = call(sum_kernel, "sum_rows", [VMEM], [VMEM], [((P_DEV, X), f32)])(
        arrived.reshape(devices * (CAP + 1), X)
    )
    return out, panel_sens


def solution(mesh):
    placed = (
        P(None, "gy", "gz", None),
        P(),
        P(("gy", "gz"), None, None),
        P(("gy", "gz"), None, None),
        P(("gy", "gz"), None, None),
    )
    return jax.shard_map(
        on_device,
        mesh=mesh,
        in_specs=placed,
        out_specs=(P(None, "gy", "gz", None), P(("gy", "gz"), None)),
        check_vma=False,
    )
```
